32 devices in a mesh: dp: 8 (over z, x), seq: 4 (over y, core).
Axes of the slice: x: 2, y: 2, z: 4, core: 2. Of those that a mesh axis runs over, the one named last changes fastest.
Arguments:
- inputs: bfloat16 [2, 4096, 2048], P(None, ('dp', 'seq')), may hold values from -6 to 6
- segments: int32 [2, 4096], P(None, 'dp'), may hold values from 0 to 31, never falling along the last dimension, each value on 1 to 512 neighbouring positions
- cotangent: bfloat16 [2, 4096, 2048], P(None, ('dp', 'seq')), may hold values from -6 to 6
- attn_gain: bfloat16 [2048], P(('dp', 'seq')), may hold values from 0.5 to 1.5
- w_query: bfloat16 [2048, 2048], P('dp', 'seq'), may hold values from -0.125 to 0.125
- w_key: bfloat16 [2048, 256], P('dp', 'seq'), may hold values from -0.125 to 0.125
- w_value: bfloat16 [2048, 256], P('dp', 'seq'), may hold values from -0.125 to 0.125
- w_out: bfloat16 [2048, 2048], P('dp', 'seq'), may hold values from -0.5 to 0.5
- mlp_gain: bfloat16 [2048], P(('dp', 'seq')), may hold values from 0.5 to 1.5
- w_gate: bfloat16 [2048, 5632], P('dp', 'seq'), may hold values from -0.125 to 0.125
- w_up: bfloat16 [2048, 5632], P('dp', 'seq'), may hold values from -0.125 to 0.125
- w_down: bfloat16 [2048, 5632], P('dp', 'seq'), may hold values from -0.078125 to 0.078125
Outputs:
- outputs: bfloat16 [2, 4096, 2048], P(None, ('dp', 'seq'))
- input_grad: float32 [2, 4096, 2048], P(None, ('dp', 'seq'))
- attn_gain_grad: float32 [2048], P(('dp', 'seq'))
- query_grad: float32 [2048, 2048], P('dp', 'seq')
- key_grad: float32 [2048, 256], P('dp', 'seq')
- value_grad: float32 [2048, 256], P('dp', 'seq')
- out_grad: float32 [2048, 2048], P('dp', 'seq')
- mlp_gain_grad: float32 [2048], P(('dp', 'seq'))
- gate_grad: float32 [2048, 5632], P('dp', 'seq')
- up_grad: float32 [2048, 5632], P('dp', 'seq')
- down_grad: float32 [2048, 5632], P('dp', 'seq')
The draws below stay inside these ranges and needn't reach their ends.
Inputs may be any that keep to these rules, and one draw needn't show every extreme that they name: `segments`: segment numbers never fall along a micro-batch's tokens; a document holds 1 to 512 tokens, and one holds exactly 512.
All inputs are finite; a program needn't handle non-finite values.
Results may differ from the reference program's by a relative error of at most 0.02.
Values may be sent and summed in bfloat16 or wider, within the bound.
A program may use at most 768 MiB of HBM per device.

```python
import math
import jax
import jax.numpy as jnp
import numpy as np
from jax import lax

D = 2048
H = 32
KVH = 4
HD = 64
FF = 5632
MICRO = 2
LEN = 512
TOKENS = 4096
N_DP = 8


def draw_attn_gain(key, part):
    key = jax.random.fold_in(key, 7)
    gain_vec = jax.random.uniform(key, (D,), jnp.float32, 0.5, 1.5)
    return gain_vec.astype(jnp.bfloat16)


def levels(stream_key, extent, pieces, smallest, largest):
    level = 1.0
    for dim, blocks in pieces:
        heights = jax.random.uniform(jax.random.fold_in(jax.random.fold_in(stream_key, 6), dim), (blocks,), jnp.float32, smallest / len(pieces), largest / len(pieces))
        level = level * jnp.repeat(jnp.exp(heights), extent[dim] // blocks).reshape((-1,) + (1,) * (len(extent) - 1 - dim))
    return level


def length_profile(number_of, total, limit, slope):
    weights = [(1 << 20) // math.isqrt(rank ** slope) + 1 for rank in range(2, number_of + 1)]
    surplus, counts = total - limit - (number_of - 1), [1] * (number_of - 1)
    while surplus > 0:
        movable = [i for i in range(number_of - 1) if counts[i] < limit]
        pool, remaining = sum([weights[i] for i in movable]), surplus
        for i in movable:
            extra = min(limit - counts[i], max(1, remaining * weights[i] // pool), surplus)
            counts[i] = counts[i] + extra
            surplus = surplus - extra
    return np.array([limit] + counts)


def ragged(rng, amount, total, most, slope):
    if amount == 2:
        one = jax.random.randint(rng, (), max(1, total - most), min(most, total - 1) + 1)
        return jnp.stack([one, total - one])
    lengths = jnp.asarray(length_profile(amount, total, most, slope), jnp.int32)
    pairs = (amount - 1) // 2
    giver, receiver = lengths[1:1 + 2 * pairs:2], lengths[2:2 + 2 * pairs:2]
    margin = jnp.minimum(giver - 1, most - receiver)
    shifted = jax.random.randint(jax.random.fold_in(rng, 1), (pairs,), 0, 1 << 20) % (margin + 1)
    lengths = lengths.at[1:1 + 2 * pairs:2].set(giver - shifted).at[2:2 + 2 * pairs:2].set(receiver + shifted)
    return lengths[jax.random.permutation(jax.random.fold_in(rng, 2), amount)]


def scatter_about(key, shape, width, reach, pieces=(), dtype=jnp.bfloat16):
    loudness = levels(key, shape, pieces, -0.22, 0.18) if pieces else 1.0
    result = jax.random.normal(key, shape, jnp.float32) * width * loudness
    return jnp.minimum(jnp.maximum(result, -reach), reach).astype(dtype)


def setup_inputs(seed: int = 0) -> dict:
    key_of = jax.random.split(jax.random.key(seed), 13)
    inputs = scatter_about(key_of[0], (MICRO, TOKENS, D), 1.0, 6.0, ((1, 32),))
    segments = jax.vmap(lambda own: jnp.searchsorted(jnp.cumsum(ragged(own, 4 * N_DP, TOKENS, LEN, 2)), jnp.arange(TOKENS), side="right"))(jax.random.split(key_of[1], MICRO)).reshape((MICRO, TOKENS)).astype(jnp.int32)
    cotangent = scatter_about(key_of[2], (MICRO, TOKENS, D), 1.0, 6.0, ((1, 32),))
    attn_gain = draw_attn_gain(jax.random.fold_in(key_of[12], 71), 0)
    w_query = scatter_about(key_of[4], (D, H * HD), D ** -0.5, 0.125, ((0, 8), (1, 4)))
    w_key = scatter_about(key_of[5], (D, KVH * HD), D ** -0.5, 0.125, ((0, 8), (1, 4)))
    w_value = scatter_about(key_of[6], (D, KVH * HD), D ** -0.5, 0.125, ((0, 8), (1, 4)))
    w_out = scatter_about(key_of[7], (D, H * HD), (D // 16) ** -0.5, 0.5, ((0, 8), (1, 4)))
    mlp_gain = jnp.clip(1.0 + 0.1 * jax.random.normal(key_of[8], (D,), jnp.float32), 0.5, 1.5).astype(jnp.bfloat16)
    w_gate = scatter_about(key_of[9], (D, FF), D ** -0.5, 0.125, ((0, 8), (1, 4)))
    w_up = scatter_about(key_of[10], (D, FF), D ** -0.5, 0.125, ((0, 8), (1, 4)))
    w_down = scatter_about(key_of[11], (D, FF), FF ** -0.5, 0.078125, ((0, 8), (1, 4)))
    return dict(inputs=inputs, segments=segments, cotangent=cotangent, attn_gain=attn_gain, w_query=w_query, w_key=w_key, w_value=w_value, w_out=w_out, mlp_gain=mlp_gain, w_gate=w_gate, w_up=w_up, w_down=w_down)


EPS = 1e-05
THETA = 10000.0
NEGATIVE = -1e+30

def rope_tables(positions):
    half_dim = HD // 2
    frequency = THETA ** (-(jnp.arange(half_dim).astype(jnp.float32) * (2.0 / HD)))
    angles = positions.astype(jnp.float32)[:, None] * frequency[None, :]
    return (jnp.cos(angles), jnp.sin(angles))

def rotate(values, cosine, sine_table):
    half_dim = values.shape[-1] // 2
    c = cosine[:, None, :]
    s = sine_table[:, None, :]
    first_half = values[..., :half_dim]
    second = values[..., half_dim:]
    return jnp.concatenate([first_half * c - second * s, second * c + first_half * s], axis=-1)

def unrotate(gradient, cosine, sine_table):
    half_dim = gradient.shape[-1] // 2
    c = cosine[:, None, :]
    s = sine_table[:, None, :]
    first_half = gradient[..., :half_dim]
    second = gradient[..., half_dim:]
    return jnp.concatenate([first_half * c + second * s, second * c - first_half * s], axis=-1)

def normalize(hidden, gain_vec):
    inverse = lax.rsqrt(lax.optimization_barrier(jnp.mean(hidden * hidden, axis=-1, keepdims=True)) + EPS)
    return (hidden * inverse * gain_vec, inverse)

def normalize_back(hidden, inverse, gain_vec, gradient):
    unit_rows = hidden * inverse
    gain_grad = lax.optimization_barrier(jnp.sum(gradient * unit_rows, axis=tuple(range(hidden.ndim - 1))))
    weighted = gradient * gain_vec
    return (inverse * (weighted - unit_rows * lax.optimization_barrier(jnp.mean(weighted * unit_rows, axis=-1, keepdims=True))), gain_grad)

def rounded(values):
    return lax.optimization_barrier(values.astype(jnp.bfloat16)).astype(jnp.float32)

def matmul(left_side, right_side):
    return jnp.dot(left_side, right_side, preferred_element_type=jnp.float32)

def one_sequence(tokens, segment, upstream, attn_gain, w_query, w_key, w_value, w_out, mlp_gain, w_gate, w_up, w_down):
    length = tokens.shape[0]
    groups = H // KVH
    factor = HD ** (-0.5)
    position = jnp.arange(length).astype(jnp.int32)
    cosine, sine_table = rope_tables(position)
    gain_a = attn_gain.astype(jnp.float32)
    gain_m = mlp_gain.astype(jnp.float32)
    hidden = tokens.astype(jnp.float32)
    normed, inverse_a = normalize(hidden, gain_a)
    normed_a = normed.astype(jnp.bfloat16)
    queries = rotate(matmul(normed_a, w_query).reshape(length, H, HD), cosine, sine_table).astype(jnp.bfloat16)
    keys_rot = rotate(matmul(normed_a, w_key).reshape(length, KVH, HD), cosine, sine_table).astype(jnp.bfloat16)
    values = matmul(normed_a, w_value).astype(jnp.bfloat16)
    allowed = (segment[:, None] == segment[None, :]) & (position[None, :] <= position[:, None])
    query_f = queries.astype(jnp.float32).reshape(length, KVH, groups, HD)
    keys_f = keys_rot.astype(jnp.float32)
    values_f = values.astype(jnp.float32).reshape(length, KVH, HD)
    scores = jnp.where(allowed, jnp.einsum('qkgd,pkd->kgqp', query_f, keys_f) * factor, NEGATIVE)
    maximum = lax.optimization_barrier(jnp.max(scores, axis=-1, keepdims=True))
    weights = jnp.where(allowed, jnp.exp(scores - maximum), 0.0)
    denominator = lax.optimization_barrier(jnp.sum(weights, axis=-1, keepdims=True))
    log_total = maximum + jnp.log(denominator)
    probability = rounded(weights / denominator)
    attended = jnp.einsum('kgqp,pkd->qkgd', probability, values_f).astype(jnp.bfloat16).reshape(length, H * HD)
    residual = hidden + matmul(attended, w_out.T)
    normed, inverse_m = normalize(residual, gain_m)
    normed_m = normed.astype(jnp.bfloat16)
    gate_pre = matmul(normed_m, w_gate)
    up_proj = matmul(normed_m, w_up)
    sigmoid_g = jax.nn.sigmoid(gate_pre)
    active = gate_pre * sigmoid_g
    product = (active * up_proj).astype(jnp.bfloat16)
    output = (residual + matmul(product, w_down.T)).astype(jnp.bfloat16)
    g_down = matmul(upstream.T, product)
    d_product = matmul(upstream, w_down)
    d_gate = (d_product * up_proj * sigmoid_g * (1.0 + gate_pre * (1.0 - sigmoid_g))).astype(jnp.bfloat16)
    d_up = (d_product * active).astype(jnp.bfloat16)
    g_gate = matmul(normed_m.T, d_gate)
    g_up = matmul(normed_m.T, d_up)
    d_normed_m = matmul(d_gate, w_gate.T) + matmul(d_up, w_up.T)
    d_norm_m, g_gain_m = normalize_back(residual, inverse_m, gain_m, d_normed_m)
    d_residual = upstream.astype(jnp.float32) + d_norm_m
    d_res_b = d_residual.astype(jnp.bfloat16)
    g_out = matmul(d_res_b.T, attended)
    d_attended = rounded(matmul(d_res_b, w_out)).reshape(length, KVH, groups, HD)
    prob_full = jnp.where(allowed, jnp.exp(scores - log_total), 0.0)
    d_values = jnp.einsum('kgqp,qkgd->pkd', rounded(prob_full), d_attended)
    d_prob = jnp.einsum('qkgd,pkd->kgqp', d_attended, values_f)
    row_sum = lax.optimization_barrier(jnp.sum(prob_full * d_prob, axis=-1, keepdims=True))
    d_scores = rounded(prob_full * (d_prob - row_sum) * factor)
    d_query = jnp.einsum('kgqp,pkd->qkgd', d_scores, keys_f).reshape(length, H, HD)
    d_keys = jnp.einsum('kgqp,qkgd->pkd', d_scores, query_f)
    d_query_b = unrotate(d_query, cosine, sine_table).astype(jnp.bfloat16).reshape(length, H * HD)
    d_keys_b = unrotate(d_keys, cosine, sine_table).astype(jnp.bfloat16).reshape(length, KVH * HD)
    d_values_b = d_values.astype(jnp.bfloat16).reshape(length, KVH * HD)
    g_query = matmul(normed_a.T, d_query_b)
    g_key = matmul(normed_a.T, d_keys_b)
    g_value = matmul(normed_a.T, d_values_b)
    d_normed_a = matmul(d_query_b, w_query.T) + matmul(d_keys_b, w_key.T) + matmul(d_values_b, w_value.T)
    d_norm_a, g_gain_a = normalize_back(hidden, inverse_a, gain_a, d_normed_a)
    return (output, d_residual + d_norm_a, (g_gain_a, g_query, g_key, g_value, g_out, g_gain_m, g_gate, g_up, g_down))

def reference(inputs, segments, cotangent, attn_gain, w_query, w_key, w_value, w_out, mlp_gain, w_gate, w_up, w_down):
    sequence_count = MICRO * N_DP
    weight_list = (attn_gain, w_query, w_key, w_value, w_out, mlp_gain, w_gate, w_up, w_down)
    zero_grads = tuple((jnp.zeros(w.shape, jnp.float32) for w in weight_list))

    def scan_step(carried, sequence):
        tokens, segment, upstream = sequence
        output, d_input, grads_now = one_sequence(tokens, segment, upstream, *weight_list)
        return (tuple((a + b for a, b in zip(carried, grads_now))), (output, d_input))
    grad_sums, (outputs, d_inputs) = lax.scan(scan_step, zero_grads, (inputs.reshape(sequence_count, LEN, D), segments.reshape(sequence_count, LEN), cotangent.reshape(sequence_count, LEN, D)))
    return (outputs.reshape(MICRO, TOKENS, D), d_inputs.reshape(MICRO, TOKENS, D), grad_sums[0], grad_sums[1], grad_sums[2], grad_sums[3], grad_sums[4], grad_sums[5], grad_sums[6], grad_sums[7], grad_sums[8])
```

```python
import jax
import jax.numpy as jnp
from jax import lax
from jax.sharding import PartitionSpec as P

HD = 64
EPS = 1e-05
THETA = 10000.0
NEGATIVE = -1e30
BF = jnp.bfloat16
F32 = jnp.float32


def rope_tables(positions):
    half_dim = HD // 2
    frequency = THETA ** (-(jnp.arange(half_dim).astype(F32) * (2.0 / HD)))
    angles = positions.astype(F32)[:, None] * frequency[None, :]
    return (jnp.cos(angles), jnp.sin(angles))


def rotate(values, cosine, sine_table):
    half_dim = values.shape[-1] // 2
    c = cosine[:, None, :]
    s = sine_table[:, None, :]
    a = values[..., :half_dim]
    b = values[..., half_dim:]
    return jnp.concatenate([a * c - b * s, b * c + a * s], axis=-1)


def unrotate(gradient, cosine, sine_table):
    return rotate(gradient, cosine, -sine_table)


def normalize(hidden, gain_vec):
    inverse = lax.rsqrt(jnp.mean(hidden * hidden, axis=-1, keepdims=True) + EPS)
    return (hidden * inverse * gain_vec, inverse)


def normalize_back(hidden, inverse, gain_vec, gradient):
    unit_rows = hidden * inverse
    gain_grad = jnp.sum(gradient * unit_rows, axis=0)
    weighted = gradient * gain_vec
    return (
        inverse * (weighted - unit_rows * jnp.mean(weighted * unit_rows, axis=-1, keepdims=True)),
        gain_grad,
    )


def project(a, b):
    return jnp.dot(a, b, preferred_element_type=F32)


def project_back(a, b):
    return lax.dot_general(a, b, (((1,), (1,)), ((), ())), preferred_element_type=F32)


def outer_sum(a, b):
    return lax.dot_general(a, b, (((0,), (0,)), ((), ())), preferred_element_type=F32)


def per_device(
    inputs, segments, cotangent, attn_gain, w_query, w_key, w_value, w_out, mlp_gain, w_gate, w_up, w_down,
):
    micro, rows, d = inputs.shape
    seq = lax.axis_size("seq")
    length = rows * seq
    full = micro * length

    def gather_rows(x):
        return lax.all_gather(x.reshape(micro, rows, -1), "seq", axis=1, tiled=True).reshape(full, -1)

    def scatter_rows(x):
        x = x.astype(BF).reshape(micro, length, -1)
        return lax.psum_scatter(x, "seq", scatter_dimension=1, tiled=True).reshape(micro * rows, -1).astype(F32)

    def gather_w(w):
        return lax.all_gather(w, "dp", axis=0, tiled=True)

    def scatter_w(g):
        return lax.psum_scatter(g.astype(BF), "dp", scatter_dimension=0, tiled=True).astype(F32)

    gain_a = lax.all_gather(attn_gain, ("dp", "seq"), axis=0, tiled=True).astype(F32)
    gain_m = lax.all_gather(mlp_gain, ("dp", "seq"), axis=0, tiled=True).astype(F32)
    wq, wk, wv, wo = gather_w(w_query), gather_w(w_key), gather_w(w_value), gather_w(w_out)
    wg, wu, wd = gather_w(w_gate), gather_w(w_up), gather_w(w_down)
    heads = wq.shape[1] // HD
    kv_heads = wk.shape[1] // HD
    groups = heads // kv_heads

    pos = jnp.arange(length, dtype=jnp.int32)
    cosine, sine = rope_tables(pos)
    cos_f, sin_f = jnp.tile(cosine, (micro, 1)), jnp.tile(sine, (micro, 1))
    allowed = (pos[None, :] <= pos[:, None])[None] & (segments[:, :, None] == segments[:, None, :])
    allowed = allowed[:, None, None]

    hidden = inputs.reshape(micro * rows, d).astype(F32)
    upstream = cotangent.reshape(micro * rows, d)
    normed, inverse_a = normalize(hidden, gain_a)
    na = gather_rows(normed.astype(BF))
    up_full = gather_rows(upstream)

    def rope(x, n, s):
        return rotate(x.reshape(full, n, HD), cos_f, s).astype(BF).reshape(full, n * HD)

    q = rope(project(na, wq), heads, sin_f)
    k = rope(project(na, wk), kv_heads, sin_f)
    v = project(na, wv).astype(BF)
    qg = q.reshape(micro, length, kv_heads, groups, HD)
    kg = k.reshape(micro, length, kv_heads, HD)
    vg = v.reshape(micro, length, kv_heads, HD)
    scores = jnp.einsum("mqkgd,mpkd->mkgqp", qg, kg, preferred_element_type=F32) * HD ** (-0.5)
    scores = jnp.where(allowed, scores, NEGATIVE)
    maximum = jnp.max(scores, axis=-1, keepdims=True)
    weights = jnp.where(allowed, jnp.exp(scores - maximum), 0.0)
    denominator = jnp.sum(weights, axis=-1, keepdims=True)
    prob = weights / denominator
    prob_b = prob.astype(BF)
    attended = jnp.einsum("mkgqp,mpkd->mqkgd", prob_b, vg, preferred_element_type=F32)
    attended = attended.astype(BF).reshape(full, heads * HD)
    residual = hidden + scatter_rows(project_back(attended, wo))
    normed, inverse_m = normalize(residual, gain_m)
    nm = gather_rows(normed.astype(BF))
    gate_pre = project(nm, wg)
    up_proj = project(nm, wu)
    sigmoid_g = jax.nn.sigmoid(gate_pre)
    active = gate_pre * sigmoid_g
    product = (active * up_proj).astype(BF)
    output = (residual + scatter_rows(project_back(product, wd))).astype(BF)
    g_down = scatter_w(outer_sum(up_full, product))
    d_product = project(up_full, wd)
    d_gate = (d_product * up_proj * sigmoid_g * (1.0 + gate_pre * (1.0 - sigmoid_g))).astype(BF)
    d_up = (d_product * active).astype(BF)
    g_gate = scatter_w(outer_sum(nm, d_gate))
    g_up = scatter_w(outer_sum(nm, d_up))
    d_nm = scatter_rows(project_back(d_gate, wg) + project_back(d_up, wu))
    d_norm_m, g_gain_m = normalize_back(residual, inverse_m, gain_m, d_nm)
    d_residual = upstream.astype(F32) + d_norm_m
    dr = gather_rows(d_residual.astype(BF))
    g_out = scatter_w(outer_sum(dr, attended))
    d_att = project(dr, wo).astype(BF)
    dg = d_att.reshape(micro, length, kv_heads, groups, HD)
    d_values = jnp.einsum("mkgqp,mqkgd->mpkd", prob_b, dg, preferred_element_type=F32)
    d_prob = jnp.einsum("mqkgd,mpkd->mkgqp", dg, vg, preferred_element_type=F32)
    row_sum = jnp.sum(prob * d_prob, axis=-1, keepdims=True)
    d_scores = (prob * (d_prob - row_sum) * HD ** (-0.5)).astype(BF)
    d_query = jnp.einsum("mkgqp,mpkd->mqkgd", d_scores, kg, preferred_element_type=F32)
    d_keys = jnp.einsum("mkgqp,mqkgd->mpkd", d_scores, qg, preferred_element_type=F32)
    dq = rope(d_query, heads, -sin_f)
    dk = rope(d_keys, kv_heads, -sin_f)
    dv = d_values.astype(BF).reshape(full, kv_heads * HD)
    g_query = scatter_w(outer_sum(na, dq))
    g_key = scatter_w(outer_sum(na, dk))
    g_value = scatter_w(outer_sum(na, dv))
    d_na = scatter_rows(project_back(dq, wq) + project_back(dk, wk) + project_back(dv, wv))
    d_norm_a, g_gain_a = normalize_back(hidden, inverse_a, gain_a, d_na)
    d_input = d_residual + d_norm_a
    gain_grads = lax.psum_scatter(
        jnp.stack([g_gain_a, g_gain_m]), ("dp", "seq"), scatter_dimension=1, tiled=True
    )
    return (
        output.reshape(micro, rows, d),
        d_input.reshape(micro, rows, d),
        gain_grads[0],
        g_query,
        g_key,
        g_value,
        g_out,
        gain_grads[1],
        g_gate,
        g_up,
        g_down,
    )


def solution(mesh):
    tok, wt, gn = P(None, ("dp", "seq"), None), P("dp", "seq"), P(("dp", "seq"))
    return jax.shard_map(
        per_device,
        mesh=mesh,
        in_specs=(tok, P(None, "dp"), tok, gn, wt, wt, wt, wt, gn, wt, wt, wt),
        out_specs=(tok, tok, gn, wt, wt, wt, wt, gn, wt, wt, wt),
        check_vma=False,
    )
```

```python
import jax
import jax.numpy as jnp
from jax import lax
from jax.experimental import pallas as pl
from jax.experimental.pallas import tpu as pltpu
from jax.sharding import PartitionSpec as P

HD = 64
EPS = 1e-05
THETA = 10000.0
NEGATIVE = -1e30
BF = jnp.bfloat16
F32 = jnp.float32


def rope_tables(positions):
    half_dim = HD // 2
    frequency = THETA ** (-(jnp.arange(half_dim).astype(F32) * (2.0 / HD)))
    angles = positions.astype(F32)[:, None] * frequency[None, :]
    return (jnp.cos(angles), jnp.sin(angles))


def rotate(values, cosine, sine_table):
    half_dim = values.shape[-1] // 2
    c = cosine[:, None, :]
    s = sine_table[:, None, :]
    a = values[..., :half_dim]
    b = values[..., half_dim:]
    return jnp.concatenate([a * c - b * s, b * c + a * s], axis=-1)


def unrotate(gradient, cosine, sine_table):
    return rotate(gradient, cosine, -sine_table)


def normalize(hidden, gain_vec):
    inverse = lax.rsqrt(jnp.mean(hidden * hidden, axis=-1, keepdims=True) + EPS)
    return (hidden * inverse * gain_vec, inverse)


def normalize_back(hidden, inverse, gain_vec, gradient):
    unit_rows = hidden * inverse
    gain_grad = jnp.sum(gradient * unit_rows, axis=0)
    weighted = gradient * gain_vec
    return (
        inverse * (weighted - unit_rows * jnp.mean(weighted * unit_rows, axis=-1, keepdims=True)),
        gain_grad,
    )


def project(a, b):
    return jnp.dot(a, b, preferred_element_type=F32)


def project_back(a, b):
    return lax.dot_general(a, b, (((1,), (1,)), ((), ())), preferred_element_type=F32)


def outer_sum(a, b):
    return lax.dot_general(a, b, (((0,), (0,)), ((), ())), preferred_element_type=F32)


MESH_ID = pl.DeviceIdType.MESH
HBM = pl.BlockSpec(memory_space=pl.ANY)


def gather_kernel(x_ref, c_ref, *refs):
    count = (len(refs) - 5) // 2
    shards, refs = refs[:count], refs[count:]
    x_full, c_full, refs = refs[0], refs[1], refs[2:]
    fulls, (send, recv, local) = refs[:count], refs[count:]
    rows = x_ref.shape[1]
    dp, sq = lax.axis_index("dp"), lax.axis_index("seq")
    across = [(lax.rem(dp + 2 * r, 8), sq) for r in range(4)]
    x_peer = (dp + 1 - 2 * lax.rem(dp, 2), sq)
    core_peer = (dp, sq + 1 - 2 * lax.rem(sq, 2))
    y_peer = (dp, lax.rem(sq + 2, 4))
    peers = across[1:] + [x_peer, core_peer, y_peer]
    barrier = pltpu.get_barrier_semaphore()
    for peer in peers:
        pl.semaphore_signal(barrier, inc=1, device_id=peer, device_id_type=MESH_ID)
    pl.semaphore_wait(barrier, len(peers))
    remote, own = [], []

    def put(src, dst, peer):
        i = len(remote)
        copy = pltpu.make_async_remote_copy(
            src_ref=src,
            dst_ref=dst,
            send_sem=send.at[i],
            recv_sem=recv.at[i],
            device_id=peer,
            device_id_type=MESH_ID,
        )
        copy.start()
        remote.append([copy, False])
        return i

    def arrived(i):
        remote[i][0].wait_recv()
        remote[i][1] = True

    def keep(src, dst):
        copy = pltpu.make_async_copy(src, dst, local.at[len(own)])
        copy.start()
        own.append(copy)

    def part(full, k):
        return full.at[:, pl.ds(k * rows, rows)]

    def seq_start(src, full):
        i = put(src, part(full, 1), y_peer)
        put(src, part(full, 2), core_peer)
        keep(src, part(full, 0))
        return i

    def seq_forward(full, i):
        arrived(i)
        put(part(full, 1), part(full, 3), core_peer)

    def z_start(i):
        keep(shards[i], fulls[i].at[0, 0])
        copies = [put(shards[i], fulls[i].at[0, r], across[4 - r]) for r in (1, 2, 3)]
        put(shards[i], fulls[i].at[1, 0], x_peer)
        return copies

    def x_forward(i, copies):
        for r in (1, 3, 2):
            arrived(copies[r - 1])
            put(fulls[i].at[0, r], fulls[i].at[1, r], x_peer)

    xs = seq_start(x_ref, x_full)
    zs = [z_start(0), z_start(1)]
    seq_forward(x_full, xs)
    x_forward(0, zs[0])
    cs = seq_start(c_ref, c_full)
    zs.append(z_start(2))
    x_forward(1, zs[1])
    zs.append(z_start(3))
    seq_forward(c_full, cs)
    x_forward(2, zs[2])
    zs.append(z_start(4))
    x_forward(3, zs[3])
    x_forward(4, zs[4])
    for copy, seen in remote:
        copy.wait_send()
        if not seen:
            copy.wait_recv()
    for copy in own:
        copy.wait()


def gather_all(x, c, shards):
    micro, rows, d = x.shape
    tokens = jax.ShapeDtypeStruct((micro, 4 * rows, d), x.dtype)
    fulls = [jax.ShapeDtypeStruct((2, 4) + w.shape, w.dtype) for w in shards]
    outs = pl.pallas_call(
        gather_kernel,
        out_shape=[tokens, tokens] + fulls,
        in_specs=[HBM] * (2 + len(shards)),
        out_specs=[HBM] * (2 + len(shards)),
        scratch_shapes=[pltpu.SemaphoreType.DMA((48,)), pltpu.SemaphoreType.DMA((48,)), pltpu.SemaphoreType.DMA((8,))],
        compiler_params=pltpu.CompilerParams(collective_id=0, has_side_effects=True),
    )(x, c, *shards)
    return outs[0], outs[1], [w.reshape(-1, w.shape[-1]) for w in outs[2:]]


class Mesh2D:
    n = 8

    def shift_x(self, a):
        return lax.ppermute(a, "dp", [(i, i ^ 1) for i in range(8)])

    def shift_z(self, a, r):
        return lax.ppermute(a, "dp", [(i, (i + 2 * r) % 8) for i in range(8)])

    def gather(self, x, c, shards):
        return gather_all(x, c, shards)

    def gather_gains(self, g):
        g = jnp.zeros((2, 4, g.shape[1]), F32).at[:, lax.axis_index("seq")].set(g).reshape(2, -1)
        g = g + shift_core(g)
        g = g + shift_y(g)
        g = jnp.concatenate([g, self.shift_x(g)], axis=0)
        g = jnp.stack([g] + [self.shift_z(g, -r) for r in (1, 2, 3)])
        return jnp.transpose(g.reshape(4, 2, 2, -1), (2, 1, 0, 3)).reshape(2, -1)

    def scatter_gain(self, g):
        g = g.reshape(2, -1)
        g = (g[0] + self.shift_x(g[1])).reshape(4, -1)
        g = g[0] + self.shift_z(g[1], 1) + self.shift_z(g[2], 2) + self.shift_z(g[3], 3)
        g = g + shift_core(g)
        g = g + shift_y(g)
        size = g.shape[0] // 4
        return lax.dynamic_slice_in_dim(g, lax.axis_index("seq") * size, size, 0)

    def scatter(self, left, right):
        half = left.shape[1] // 2
        far = outer_sum(left[:, half:], right).astype(BF)
        got = self.shift_x(far)
        near = (outer_sum(left[:, :half], right) + got.astype(F32)).astype(BF)
        blocks = near.reshape(4, half // 4, -1)
        total = blocks[0].astype(F32)
        for r in (1, 2, 3):
            total = total + self.shift_z(blocks[r], r).astype(F32)
        return total

    def to_relative(self, a):
        dp = lax.axis_index("dp")
        z, x = dp // 2, dp % 2
        lead = a.shape[:-1]
        a = a.reshape(lead + (4, 2, -1))
        a = jnp.where(x == 0, a, jnp.flip(a, -2))
        a = lax.dynamic_slice_in_dim(jnp.concatenate([a, a], -3), z, 4, len(lead))
        return jnp.swapaxes(a, -2, -3).reshape(lead + (-1,))

    def from_relative(self, a):
        dp = lax.axis_index("dp")
        z, x = dp // 2, dp % 2
        lead = a.shape[:-1]
        a = jnp.swapaxes(a.reshape(lead + (2, 4, -1)), -2, -3)
        a = jnp.where(x == 0, a, jnp.flip(a, -2))
        a = lax.dynamic_slice_in_dim(jnp.concatenate([a, a], -3), 4 - z, 4, len(lead))
        return a.reshape(lead + (-1,))


class AnyMesh:
    def gather(self, x, c, shards):
        fulls = [lax.all_gather(w, "dp", axis=0, tiled=True) for w in shards]
        return gather_rows(x), gather_rows(c), fulls

    def gather_gains(self, g):
        return lax.all_gather(g, ("dp", "seq"), axis=1, tiled=True)

    def scatter_gain(self, g):
        return lax.psum_scatter(g, ("dp", "seq"), scatter_dimension=0, tiled=True)

    def scatter(self, left, right):
        return lax.psum_scatter(
            outer_sum(left, right).astype(BF), "dp", scatter_dimension=0, tiled=True
        ).astype(F32)

    def to_relative(self, a):
        return a

    def from_relative(self, a):
        return a


def shift_core(a):
    return lax.ppermute(a, "seq", [(i, i ^ 1) for i in range(4)])


def shift_y(a):
    return lax.ppermute(a, "seq", [(i, i ^ 2) for i in range(4)])


def gather_rows(a):
    across = shift_y(a)
    return jnp.concatenate([a, across, shift_core(a), shift_core(across)], axis=-2)


def scatter_rows(make):
    got = shift_core(make(1).astype(BF))
    near = make(0) + got.astype(F32)
    rows = near.shape[1] // 2
    got = shift_y(near[:, rows:].astype(BF))
    return near[:, :rows] + got.astype(F32)


def per_device(
    inputs, segments, cotangent, attn_gain, w_query, w_key, w_value, w_out, mlp_gain, w_gate, w_up, w_down,
):
    micro, rows, d = inputs.shape
    seq = lax.axis_size("seq")
    length = rows * seq
    full = micro * length
    half = length // 2
    grid = Mesh2D() if lax.axis_size("dp") == 8 else AnyMesh()

    nq, nk = w_query.shape[1], w_key.shape[1]
    heads, kv_heads = nq // HD, nk // HD
    groups = heads // kv_heads
    w_qkv = jnp.concatenate([w_query, w_key, w_value], axis=1)

    inputs = grid.to_relative(inputs)
    cotangent = grid.to_relative(cotangent)
    gains = grid.gather_gains(jnp.stack([attn_gain, mlp_gain]).astype(F32))
    gain_a, gain_m = gains[0], gains[1]

    shards = [w_qkv, w_out, w_gate, w_up, w_down]
    x_full, up_full, (wqkv, wo, wg, wu, wd) = grid.gather(inputs, cotangent, shards)

    me = lax.axis_index("seq")
    order = [me, me ^ 2, me ^ 1, me ^ 3]
    pos = jnp.concatenate([j * rows + jnp.arange(rows, dtype=jnp.int32) for j in order])
    segs = jnp.concatenate([lax.dynamic_slice_in_dim(segments, j * rows, rows, 1) for j in order], axis=1)
    cosine, sine = rope_tables(pos)
    cos_f, sin_f = jnp.tile(cosine, (micro, 1)), jnp.tile(sine, (micro, 1))
    allowed = (pos[None, :] <= pos[:, None])[None] & (segs[:, :, None] == segs[:, None, :])
    allowed = allowed[:, None, None]

    def pieces(make):
        return lambda i: make(slice(i * half, (i + 1) * half)).reshape(micro, half, d)

    def rows_of(a, s):
        return a.reshape(micro, length, -1)[:, s].reshape(micro * half, -1)

    hidden_full = x_full.reshape(full, d).astype(F32)
    normed, inverse_f = normalize(hidden_full, gain_a)
    na = normed.astype(BF)
    hidden = inputs.astype(F32)
    upstream = cotangent.astype(F32)
    up_full = up_full.reshape(full, d)

    def rope(x, n, s):
        return rotate(x.reshape(full, n, HD), cos_f, s).astype(BF).reshape(full, n * HD)

    qkv = project(na, wqkv)
    q = rope(qkv[:, :nq], heads, sin_f)
    k = rope(qkv[:, nq : nq + nk], kv_heads, sin_f)
    v = qkv[:, nq + nk :].astype(BF)
    qg = q.reshape(micro, length, kv_heads, groups, HD)
    kg = k.reshape(micro, length, kv_heads, HD)
    vg = v.reshape(micro, length, kv_heads, HD)
    scores = jnp.einsum("mqkgd,mpkd->mkgqp", qg, kg, preferred_element_type=F32) * HD ** (-0.5)
    scores = jnp.where(allowed, scores, NEGATIVE)
    maximum = jnp.max(scores, axis=-1, keepdims=True)
    weights = jnp.where(allowed, jnp.exp(scores - maximum), 0.0)
    denominator = jnp.sum(weights, axis=-1, keepdims=True)
    prob = weights / denominator
    prob_b = prob.astype(BF)
    attended = jnp.einsum("mkgqp,mpkd->mqkgd", prob_b, vg, preferred_element_type=F32)
    attended = attended.astype(BF).reshape(full, heads * HD)
    residual = hidden + scatter_rows(pieces(lambda s: project_back(rows_of(attended, s), wo)))
    normed, inverse_m = normalize(residual, gain_m)
    nm = gather_rows(normed.astype(BF)).reshape(full, d)
    gate_pre = project(nm, wg)
    up_proj = project(nm, wu)
    sigmoid_g = jax.nn.sigmoid(gate_pre)
    active = gate_pre * sigmoid_g
    product = (active * up_proj).astype(BF)
    g_down = grid.scatter(up_full, product)
    d_product = project(up_full, wd)
    d_gate = (d_product * up_proj * sigmoid_g * (1.0 + gate_pre * (1.0 - sigmoid_g))).astype(BF)
    d_up = (d_product * active).astype(BF)
    d_nm = scatter_rows(
        pieces(lambda s: project_back(rows_of(d_gate, s), wg) + project_back(rows_of(d_up, s), wu))
    )
    g_gate = grid.scatter(nm, d_gate)
    g_up = grid.scatter(nm, d_up)
    output = (residual + scatter_rows(pieces(lambda s: project_back(rows_of(product, s), wd)))).astype(BF)
    flat = lambda a: a.reshape(micro * rows, -1)
    d_norm_m, g_gain_m = normalize_back(flat(residual), flat(inverse_m), gain_m, flat(d_nm))
    d_residual = upstream + d_norm_m.reshape(micro, rows, d)
    dr = gather_rows(d_residual.astype(BF)).reshape(full, d)
    d_att = project(dr, wo).astype(BF)
    dg = d_att.reshape(micro, length, kv_heads, groups, HD)
    d_values = jnp.einsum("mkgqp,mqkgd->mpkd", prob_b, dg, preferred_element_type=F32)
    d_prob = jnp.einsum("mqkgd,mpkd->mkgqp", dg, vg, preferred_element_type=F32)
    row_sum = jnp.sum(prob * d_prob, axis=-1, keepdims=True)
    d_scores = (prob * (d_prob - row_sum) * HD ** (-0.5)).astype(BF)
    d_query = jnp.einsum("mkgqp,mpkd->mqkgd", d_scores, kg, preferred_element_type=F32)
    d_keys = jnp.einsum("mkgqp,mqkgd->mpkd", d_scores, qg, preferred_element_type=F32)
    dq = rope(d_query, heads, -sin_f)
    dk = rope(d_keys, kv_heads, -sin_f)
    dv = d_values.astype(BF).reshape(full, kv_heads * HD)
    dqkv = jnp.concatenate([dq, dk, dv], axis=1)
    g_out = grid.scatter(dr, attended)
    d_na = scatter_rows(pieces(lambda s: project_back(rows_of(dqkv, s), wqkv)))
    g_qkv = grid.scatter(na, dqkv)
    inverse_a = inverse_f.reshape(micro, length, 1)[:, :rows]
    d_norm_a, g_gain_a = normalize_back(flat(hidden), flat(inverse_a), gain_a, flat(d_na))
    d_input = d_residual + d_norm_a.reshape(micro, rows, d)
    return (
        grid.from_relative(output),
        grid.from_relative(d_input),
        grid.scatter_gain(g_gain_a),
        g_qkv[:, :nq],
        g_qkv[:, nq : nq + nk],
        g_qkv[:, nq + nk :],
        g_out,
        grid.scatter_gain(g_gain_m),
        g_gate,
        g_up,
        g_down,
    )


def solution(mesh):
    tok, wt, gn = P(None, ("dp", "seq"), None), P("dp", "seq"), P(("dp", "seq"))
    return jax.shard_map(
        per_device,
        mesh=mesh,
        in_specs=(tok, P(None, "dp"), tok, gn, wt, wt, wt, wt, gn, wt, wt, wt),
        out_specs=(tok, tok, gn, wt, wt, wt, wt, gn, wt, wt, wt),
        check_vma=False,
    )
```

```python
import jax
import jax.numpy as jnp
from jax import lax
from jax.experimental import pallas as pl
from jax.experimental.pallas import tpu as pltpu
from jax.sharding import PartitionSpec as P

HD = 64
EPS = 1e-05
THETA = 10000.0
NEGATIVE = -1e30
BF = jnp.bfloat16
F32 = jnp.float32


def rope_tables(positions):
    half_dim = HD // 2
    frequency = THETA ** (-(jnp.arange(half_dim).astype(F32) * (2.0 / HD)))
    angles = positions.astype(F32)[:, None] * frequency[None, :]
    return (jnp.cos(angles), jnp.sin(angles))


def rotate(values, cosine, sine_table):
    half_dim = values.shape[-1] // 2
    c = cosine[:, None, :]
    s = sine_table[:, None, :]
    a = values[..., :half_dim]
    b = values[..., half_dim:]
    return jnp.concatenate([a * c - b * s, b * c + a * s], axis=-1)


def unrotate(gradient, cosine, sine_table):
    return rotate(gradient, cosine, -sine_table)


def normalize(hidden, gain_vec):
    inverse = lax.rsqrt(jnp.mean(hidden * hidden, axis=-1, keepdims=True) + EPS)
    return (hidden * inverse * gain_vec, inverse)


def normalize_back(hidden, inverse, gain_vec, gradient):
    unit_rows = hidden * inverse
    gain_grad = jnp.sum(gradient * unit_rows, axis=0)
    weighted = gradient * gain_vec
    return (
        inverse * (weighted - unit_rows * jnp.mean(weighted * unit_rows, axis=-1, keepdims=True)),
        gain_grad,
    )


def project(a, b):
    return jnp.dot(a, b, preferred_element_type=F32)


def project_back(a, b):
    return lax.dot_general(a, b, (((1,), (1,)), ((), ())), preferred_element_type=F32)


def outer_sum(a, b):
    return lax.dot_general(a, b, (((0,), (0,)), ((), ())), preferred_element_type=F32)


MESH_ID = pl.DeviceIdType.MESH
HBM = pl.BlockSpec(memory_space=pl.ANY)
VMEM = pl.BlockSpec(memory_space=pltpu.VMEM)
ROWS = 128
LEN4 = 512
HALF = 256
DM = 2048
LIMIT = 60 * 1024 * 1024
LIMIT_B = 62 * 1024 * 1024


def nt(a, b):
    return lax.dot_general(a, b, (((1,), (1,)), ((), ())), preferred_element_type=F32)


def tn(a, b):
    return lax.dot_general(a, b, (((0,), (0,)), ((), ())), preferred_element_type=F32)


def nn(a, b):
    return jnp.dot(a, b, preferred_element_type=F32)


class Links:
    def __init__(self, send, recv, local):
        self.send, self.recv, self.local = send, recv, local
        self.remote, self.own = [], []
        self.seen, self.gone = set(), set()
        dp, sq = lax.axis_index("dp"), lax.axis_index("seq")
        self.dp, self.sq = dp, sq
        self.z = [(lax.rem(dp + 2 * r, 8), sq) for r in range(4)]
        self.x = (dp + 1 - 2 * lax.rem(dp, 2), sq)
        core = sq + 1 - 2 * lax.rem(sq, 2)
        self.core = (dp, core)
        self.y = (dp, lax.rem(sq + 2, 4))
        self.both = (dp, lax.rem(core + 2, 4))
        peers = self.z[1:] + [self.x, self.core, self.y, self.both]
        barrier = pltpu.get_barrier_semaphore()
        for peer in peers:
            pl.semaphore_signal(barrier, inc=1, device_id=peer, device_id_type=MESH_ID)
        pl.semaphore_wait(barrier, len(peers))

    def put(self, src, dst, peer):
        i = len(self.remote)
        copy = pltpu.make_async_remote_copy(
            src_ref=src,
            dst_ref=dst,
            send_sem=self.send.at[i],
            recv_sem=self.recv.at[i],
            device_id=peer,
            device_id_type=MESH_ID,
        )
        copy.start()
        self.remote.append(copy)
        return i

    def arrived(self, *ids):
        for i in ids:
            if i not in self.seen:
                self.seen.add(i)
                self.remote[i].wait_recv()

    def sent(self, *ids):
        for i in ids:
            if i not in self.gone:
                self.gone.add(i)
                self.remote[i].wait_send()

    def keep(self, src, dst):
        copy = pltpu.make_async_copy(src, dst, self.local.at[len(self.own)])
        copy.start()
        self.own.append([copy, False])
        return len(self.own) - 1

    def kept(self, *ids):
        for i in ids:
            if not self.own[i][1]:
                self.own[i][1] = True
                self.own[i][0].wait()

    def finish(self):
        self.sent(*range(len(self.remote)))
        self.arrived(*range(len(self.remote)))
        self.kept(*range(len(self.own)))


def rope_tile(t, cosine, sine):
    lane = lax.broadcasted_iota(jnp.int32, t.shape, 1)
    turned = jnp.where(lax.rem(lane, 64) < 32, pltpu.roll(t, 96, 1), pltpu.roll(t, 32, 1))
    return t * cosine + turned * sine


def forward_kernel(
    x_ref, c_ref, g_ref, table, mask, wqkv_s, wo_s, wg_s, wu_s, wd_s,
    c_full, wqkv_f, wo_f, wg_f, wu_f, wd_f, na_o, qkv_o, att_o, res_o, nm_o, gain_o, prod_o, fa_o, fb_o, down_o,
    xf, nm, wqkv_v, wo_v, qkv, att, far, far_in, near, ysend, yin, own_x, gseq, gfull, gown, prod, fa, fb, wt, lbuf, gbuf,
    send, recv, local, wsem, lsem, gsem,
):
    links = Links(send, recv, local)
    put, arrived = links.put, links.arrived
    shards = [wqkv_s, wo_s, wg_s, wu_s, wd_s]
    fulls = [wqkv_f, wo_f, wg_f, wu_f, wd_f]

    def part(full, k):
        return full.at[:, pl.ds(k * ROWS, ROWS)]

    def seq_start(src, full):
        return [put(src, part(full, 1), links.y), put(src, part(full, 2), links.core)]

    def seq_forward(full, ids):
        arrived(ids[0])
        ids.append(put(part(full, 1), part(full, 3), links.core))

    placed = []

    def z_start(i):
        placed.append(links.keep(shards[i], fulls[i].at[0, 0]))
        return [put(shards[i], fulls[i].at[0, r], links.z[4 - r]) for r in (1, 2, 3)]

    def x_own(i):
        return [put(shards[i], fulls[i].at[1, 0], links.x)]

    def x_forward(i, copies, ids, order=(1, 3, 2)):
        for r in order:
            arrived(copies[r - 1])
            ids.append(put(fulls[i].at[0, r], fulls[i].at[1, r], links.x))

    xs = seq_start(x_ref, xf)
    own0 = links.keep(x_ref, part(xf, 0))
    own1 = links.keep(x_ref, own_x)
    gs = [put(g_ref, gseq.at[k], p) for k, p in ((1, links.core), (2, links.y), (3, links.both))]
    z0 = z_start(0)
    x0 = x_own(0)
    arrived(*gs)
    gown[...] = g_ref[...] + gseq[1] + gseq[2] + gseq[3]
    gfull[0, 0] = gown[...]
    gz = [put(gown, gfull.at[0, r], links.z[4 - r]) for r in (1, 2, 3)]
    gx = [put(gown, gfull.at[1, 0], links.x)]
    z1 = z_start(1)
    for r in (1, 2, 3):
        arrived(gz[r - 1])
        gx.append(put(gfull.at[0, r], gfull.at[1, r], links.x))
    seq_forward(xf, xs)
    x_forward(0, z0, x0)
    x1 = x_own(1)
    arrived(*gx)
    for b in range(8):
        gain_o[:, b * 256 : (b + 1) * 256] = gfull[b // 4, b % 4]
    z2 = z_start(2)
    x2 = x_own(2)
    arrived(*xs)
    links.sent(xs[2])
    links.kept(own0, own1)

    @pl.loop(0, 16)
    def _(i):
        m, r = i // 8, pl.multiple_of(lax.rem(i, 8) * 64, 64)
        v = xf[m, pl.ds(r, 64), :].astype(F32)
        inverse = lax.rsqrt(jnp.mean(v * v, axis=-1, keepdims=True) + EPS)
        xf[m, pl.ds(r, 64), :] = (v * inverse * gain_o[0:1, :]).astype(BF)

    na_copy = links.keep(xf, na_o)
    x_forward(1, z1, x1)
    arrived(*x0)
    links.kept(placed[0])
    load0 = links.keep(wqkv_f, wqkv_v)
    links.kept(load0)

    @pl.loop(0, 4)
    def _(i):
        m, r = i // 2, pl.multiple_of(lax.rem(i, 2) * 256, 256)
        rows = pl.ds(r, 256)
        a = xf[m, rows, :]
        cq, sq = table[0, rows, :], table[1, rows, :]
        for n in range(2):
            t = nn(a, wqkv_v[:, :, :, n * 256 : (n + 1) * 256].reshape(DM, 256))
            for j in range(2):
                lanes = slice(n * 256 + j * 128, n * 256 + (j + 1) * 128)
                qkv[m, rows, lanes] = rope_tile(t[:, j * 128 : (j + 1) * 128], cq, sq).astype(BF)
        t = nn(a, wqkv_v[:, :, :, 512:640].reshape(DM, 128))
        qkv[m, rows, 512:640] = rope_tile(t, table[2, rows, :], table[3, rows, :]).astype(BF)

    links.keep(qkv, qkv_o)

    def attend(m):
        kv = qkv[m, :, 512:640].astype(F32)
        lane = lax.broadcasted_iota(jnp.int32, (LEN4, 128), 1)
        ka = jnp.where(lane < 64, kv, 0.0)
        vb = jnp.where(lane < 64, 0.0, kv)
        ks = [ka.astype(BF), pltpu.roll(ka, 64, 1).astype(BF)]
        vs = [pltpu.roll(vb, 64, 1).astype(BF), vb.astype(BF)]

        @pl.loop(0, 8)
        def _(i):
            lanes = pl.ds(pl.multiple_of(i // 2 * 128, 128), 128)
            rows = pl.ds(pl.multiple_of(lax.rem(i, 2) * 256, 256), 256)
            q = qkv[m, rows, lanes]
            bias = mask[m, rows, :].astype(F32)
            out = jnp.zeros((256, 128), F32)
            for k, v in zip(ks, vs):
                s = nt(q, k) * 0.125 + bias
                e = jnp.exp(s - jnp.max(s, axis=-1, keepdims=True))
                p = (e / jnp.sum(e, axis=-1, keepdims=True)).astype(BF)
                out = out + nn(p, v)
            att[m, rows, lanes] = out.astype(BF)

    attend(0)
    z3 = z_start(3)
    attend(1)
    links.keep(att, att_o)
    arrived(*x1)
    links.kept(placed[1])
    load1 = links.keep(wo_f, wo_v)
    links.kept(load1)

    def out_rows(m, row, dst, dtype):
        @pl.loop(0, 8)
        def _(n):
            w = wo_v[n // 4, lax.rem(n, 4)]
            lanes = pl.ds(pl.multiple_of(n * 256, 256), 256)
            dst[m, :, lanes] = nt(att[m, row : row + HALF, :], w).astype(dtype)

    for m in range(2):
        out_rows(m, HALF, far, BF)
    fc = put(far, far_in, links.core)
    for m in range(2):
        out_rows(m, 0, near, F32)
    arrived(fc)

    @pl.loop(0, 4)
    def _(i):
        m, r = i // 2, pl.multiple_of(lax.rem(i, 2) * 64, 64)
        rows = pl.ds(r + ROWS, 64)
        ysend[m, pl.ds(r, 64), :] = (near[m, rows, :] + far_in[m, rows, :].astype(F32)).astype(BF)

    yc = put(ysend, yin, links.y)
    x_forward(2, z2, x2)
    x3 = x_own(3)
    z4 = z_start(4)
    arrived(yc)

    @pl.loop(0, 4)
    def _(i):
        m, r = i // 2, pl.multiple_of(lax.rem(i, 2) * 64, 64)
        rows = pl.ds(r, 64)
        v = near[m, rows, :] + far_in[m, rows, :].astype(F32) + yin[m, rows, :].astype(F32) + own_x[m, rows, :].astype(F32)
        res_o[m, rows, :] = v
        inverse = lax.rsqrt(jnp.mean(v * v, axis=-1, keepdims=True) + EPS)
        nm[m, rows, :] = (v * inverse * gain_o[1:2, :]).astype(BF)

    ns = seq_start(part(nm, 0), nm)
    seq_forward(nm, ns)
    cs = seq_start(c_ref, c_full)
    c_own = links.keep(c_ref, part(c_full, 0))
    x_forward(3, z3, x3)
    x4 = x_own(4)
    arrived(*ns)
    links.keep(nm, nm_o)
    arrived(*x2)
    seq_forward(c_full, cs)
    arrived(*x3)
    links.kept(placed[2], placed[3])

    def load(t, slot):
        lanes = pl.ds(pl.multiple_of(t * 128, 128), 128)
        return [
            pltpu.make_async_copy(w.at[:, :, :, lanes], wt.at[slot, :, :, :, pl.ds(k * 128, 128)], wsem.at[slot, k])
            for k, w in enumerate((wg_f, wu_f))
        ]

    def up_tile(t, slot):
        lanes = pl.ds(pl.multiple_of(t * 128, 128), 128)

        @pl.loop(0, 4)
        def _(i):
            m, rows = i // 2, pl.ds(pl.multiple_of(lax.rem(i, 2) * 256, 256), 256)
            r = nn(nm[m, rows, :], wt[slot].reshape(DM, 256))
            g, u = r[:, :128], r[:, 128:]
            s = jax.nn.sigmoid(g)
            active = g * s
            prod[m, rows, lanes] = (active * u).astype(BF)
            fa[m, rows, lanes] = (u * s * (1.0 + g * (1.0 - s))).astype(BF)
            fb[m, rows, lanes] = active.astype(BF)

    for c in load(0, 0):
        c.start()
    tiles = wg_s.shape[1] // 128

    def tile_step(t):
        slot = lax.rem(t, 2)

        @pl.when(t + 1 < tiles)
        def _():
            for c in load(t + 1, 1 - slot):
                c.start()

        for c in load(t, slot):
            c.wait()
        up_tile(t, slot)

    pl.loop(0, 5)(tile_step)
    arrived(z4[0])
    x_forward(4, z4, x4)
    pl.loop(5, tiles)(tile_step)
    links.keep(prod, prod_o)
    links.keep(fa, fa_o)
    links.keep(fb, fb_o)
    arrived(*cs)
    links.kept(c_own)

    def load_left(b, slot):
        lanes = pl.ds(pl.multiple_of(b * 256, 256), 256)
        return pltpu.make_async_copy(c_full.at[:, :, lanes], lbuf.at[slot], lsem.at[slot])

    def store_grad(b, slot):
        return pltpu.make_async_copy(gbuf.at[slot], down_o.at[b // 4, lax.rem(b, 4)], gsem.at[slot])

    load_left(0, 0).start()

    @pl.loop(0, 8)
    def _(b):
        slot = lax.rem(b, 2)

        @pl.when(b + 1 < 8)
        def _():
            load_left(b + 1, 1 - slot).start()

        load_left(b, slot).wait()

        @pl.when(b >= 2)
        def _():
            store_grad(b - 2, slot).wait()

        gbuf[slot] = (tn(lbuf[slot, 0], prod[0]) + tn(lbuf[slot, 1], prod[1])).astype(BF)
        store_grad(b, slot).start()

    store_grad(6, 0).wait()
    store_grad(7, 1).wait()
    links.finish()


def forward(x, c, g, table, mask, shards):
    micro, rows, d = x.shape
    sd = jax.ShapeDtypeStruct
    toks = (micro, 4 * rows, d)
    nq, nf = shards[1].shape[1], shards[2].shape[1]
    fulls = [sd((2, 4) + w.shape, BF) for w in shards]
    ffn = sd((micro, 4 * rows, nf), BF)
    out_shape = [sd(toks, BF)] + fulls + [
        sd(toks, BF), sd((micro, 4 * rows, 640), BF), sd((micro, 4 * rows, nq), BF),
        sd((micro, rows, d), F32), sd(toks, BF), sd((8, d), F32), ffn, ffn, ffn, sd((2, 4, 256, nf), BF),
    ]
    v = pltpu.VMEM
    scratch = [
        v(toks, BF), v(toks, BF), v((2, 4, 256, 640), BF), v((2, 4, 256, 512), BF), v((2, 512, 640), BF),
        v((2, 512, 512), BF), v((2, 256, d), BF), v((2, 256, d), BF), v((2, 256, d), F32), v((2, 128, d), BF),
        v((2, 128, d), BF), v((2, 128, d), BF), v((4, 8, 256), F32), v((2, 4, 8, 256), F32), v((8, 256), F32),
        v((2, 512, nf), BF), v((2, 512, nf), BF), v((2, 512, nf), BF), v((2, 2, 4, 256, 256), BF), v((2, 2, 512, 256), BF), v((2, 256, nf), BF),
        pltpu.SemaphoreType.DMA((72,)), pltpu.SemaphoreType.DMA((72,)), pltpu.SemaphoreType.DMA((24,)),
        pltpu.SemaphoreType.DMA((2, 2)), pltpu.SemaphoreType.DMA((2,)), pltpu.SemaphoreType.DMA((2,)),
    ]
    return pl.pallas_call(
        forward_kernel,
        out_shape=out_shape,
        in_specs=[HBM, HBM, VMEM, VMEM, VMEM] + [HBM] * 5,
        out_specs=[HBM] * 9 + [VMEM, HBM, VMEM] + [HBM] * 4,
        scratch_shapes=scratch,
        compiler_params=pltpu.CompilerParams(collective_id=0, has_side_effects=True, vmem_limit_bytes=LIMIT),
    )(x, c, g, table, mask, *shards)


ORDER = (2, 1, 3, 0)


def backward_kernel(
    table, mask_t, gain, x_ref, c_full, wqkv_f, wo_f, wg_f, wu_f, wd_f, na_h, qkv_h, att_h, res_h, nm_h, prod_h, fa_h,
    fb_h, down_h,
    out_o, din_o, gain_o, gq_o, go_o, gg_o, gu_o, gd_o, xin_f, xin_o, xin_q, zin_f, zin_o, zin_q, fin, yin,
    cot, nm, dr, dg, du, grads, stage, ostage, wcol, wrow, far, far_st, ysend, acc_m, acc_o, res, qkv, att, datt, dqkv,
    obuf, dkacc, dvacc, gacc, gxin, gnear, gzin, gown, gsin,
    send, recv, local, csem, rsem, ssem, osem,
):
    links = Links(send, recv, local)
    put, arrived, sent, keep, kept = links.put, links.arrived, links.sent, links.keep, links.kept
    ff = fa_h.shape[2]
    prod = dr.at[:, :, pl.ds(0, ff)]

    def wide(k):
        return lambda r: grads.at[k, r]

    def cut(start, width):
        return lambda r: grads.at[0, r, :, pl.ds(start, width)]

    spec = {
        "down": (None, None, wide(0), xin_f.at[0], zin_f.at[0], ff, gd_o),
        "gate": (nm, dg, wide(1), xin_f.at[1], zin_f.at[1], ff, gg_o),
        "up": (nm, du, wide(2), xin_f.at[2], zin_f.at[2], ff, gu_o),
        "out": (dr, att, cut(0, 512), xin_o, zin_o, 512, go_o),
        "qkv": (cot, dqkv, cut(512, 640), xin_q, zin_q, 640, gq_o),
    }
    xid = {name: {} for name in spec}
    zid = {name: {} for name in spec}

    def block_of(name, b):
        left, right = spec[name][:2]
        lanes = pl.ds(b * 256, 256)
        return tn(left[0, :, lanes], right[0]) + tn(left[1, :, lanes], right[1])

    def grad_far(name):
        buffer, landing = spec[name][2:4]
        for r in ORDER:
            if name == "down":
                xid[name][r] = put(down_h.at[1, r], landing.at[r], links.x)
            else:
                buffer(r)[...] = block_of(name, 4 + r).astype(BF)
                xid[name][r] = put(buffer(r), landing.at[r], links.x)

    def grad_near(name, r):
        buffer, landing, zland, width = spec[name][2:6]
        arrived(xid[name][r])
        got = stage.at[0, :, pl.ds(0, width)]
        copies = [pltpu.make_async_copy(landing.at[r], got, ssem.at[0])]
        if name == "down":
            copies.append(pltpu.make_async_copy(down_h.at[0, r], stage.at[1], ssem.at[1]))
        for c in copies:
            c.start()
        if name != "down":
            mine = block_of(name, r)
            sent(xid[name][r])
        for c in copies:
            c.wait()
        if name == "down":
            mine = stage[1].astype(F32)
        buffer(r)[...] = (mine + got[...].astype(F32)).astype(BF)
        if r:
            zid[name][r] = put(buffer(r), zland.at[r - 1], links.z[r])

    writing = []

    def grad_final(name):
        buffer, _, zland, width, result = spec[name][2:]
        copies = []
        for r in (1, 2, 3):
            arrived(zid[name][r])
            copies.append(pltpu.make_async_copy(zland.at[r - 1], stage.at[r - 1, :, pl.ds(0, width)], ssem.at[r - 1]))
            copies[-1].start()
        for c in copies + writing:
            c.wait()
        lanes = slice(0, width)
        total = buffer(0)[...].astype(F32) + stage[0, :, lanes].astype(F32)
        ostage[:, lanes] = total + stage[1, :, lanes].astype(F32) + stage[2, :, lanes].astype(F32)
        writing[:] = [pltpu.make_async_copy(ostage.at[:, pl.ds(0, width)], result, osem.at[0])]
        writing[0].start()

    def sweep(terms, row, use):
        def load(b, slot):
            return [
                pltpu.make_async_copy(
                    w.at[b // 4, lax.rem(b, 4)], wrow.at[slot, k, :, pl.ds(0, width)], rsem.at[slot, k]
                )
                for k, (_, w, width) in enumerate(terms)
            ]

        for c in load(0, 0):
            c.start()

        @pl.loop(0, 8)
        def _(b):
            slot = lax.rem(b, 2)

            @pl.when(b + 1 < 8)
            def _():
                for c in load(b + 1, 1 - slot):
                    c.start()

            for c in load(b, slot):
                c.wait()
            lanes = pl.ds(pl.multiple_of(b * 256, 256), 256)
            for m in range(2):
                total = None
                for k, (left, _, width) in enumerate(terms):
                    t = nt(left[m, row : row + HALF, 0:width], wrow[slot, k, :, 0:width])
                    total = t if total is None else total + t
                use(m, lanes, total)

    fid, yid = [], []

    def rows_far(i, terms):
        sent(*fid)

        def use(m, lanes, total):
            far[m, :, lanes] = total.astype(BF)

        sweep(terms, HALF, use)
        fid.append(put(far, fin.at[i], links.core))

    def rows_near(i, terms, acc):
        sent(*yid)
        arrived(fid[i])
        kept(keep(fin.at[i], far_st))

        def use(m, lanes, total):
            total = total + far_st[m, :, lanes].astype(F32)
            acc[m, :, lanes] = total[:ROWS]
            ysend[m, :, lanes] = total[ROWS:].astype(BF)

        sweep(terms, 0, use)
        yid.append(put(ysend, yin.at[i], links.y))

    def rows_final(i):
        arrived(yid[i])
        kept(keep(yin.at[i], far_st.at[:, pl.ds(0, ROWS)]))

    def chunks(body):
        @pl.loop(0, 4)
        def _(i):
            body(i // 2, pl.ds(pl.multiple_of(lax.rem(i, 2) * 64, 64), 64))

    def norm_back(v, e, row):
        inverse = lax.rsqrt(jnp.mean(v * v, axis=-1, keepdims=True) + EPS)
        u = v * inverse
        gacc[row : row + 1, :] += jnp.sum(e * u, axis=0, keepdims=True)
        w = e * gain[row : row + 1, :]
        return inverse * (w - u * jnp.mean(w * u, axis=-1, keepdims=True))

    grad_far("down")
    prod_in = keep(prod_h, prod)
    cot_in = keep(c_full, cot)
    ffn_in = [keep(fa_h, dg), keep(fb_h, du)]
    late = [keep(nm_h, nm), keep(res_h, res), keep(qkv_h, qkv), keep(att_h, att)]
    gacc[...] = jnp.zeros_like(gacc)

    def load_col(t, slot):
        lanes = pl.ds(pl.multiple_of(t * 256, 256), 256)
        return pltpu.make_async_copy(wd_f.at[:, :, :, lanes], wcol.at[slot], csem.at[slot])

    load_col(0, 0).start()
    kept(prod_in)
    out_terms = [(prod, wd_f, ff)]
    rows_far(0, out_terms)
    kept(cot_in, *ffn_in)
    tiles = ff // 256
    rest = ff - tiles * 256

    def product_rows(slot, width, start):
        @pl.loop(0, 4)
        def _(i):
            m, rows = i // 2, pl.ds(pl.multiple_of(lax.rem(i, 2) * 256, 256), 256)
            lanes = pl.ds(start, width)
            d = nn(cot[m, rows, :], wcol[slot, :, :, :, 0:width].reshape(DM, width))
            dg[m, rows, lanes] = (d * dg[m, rows, lanes].astype(F32)).astype(BF)
            du[m, rows, lanes] = (d * du[m, rows, lanes].astype(F32)).astype(BF)

    last = pltpu.make_async_copy(
        wd_f.at[:, :, :, pl.ds(tiles * 256, rest)], wcol.at[tiles % 2, :, :, :, pl.ds(0, rest)], csem.at[tiles % 2]
    )

    @pl.loop(0, tiles)
    def _(t):
        slot = lax.rem(t, 2)

        @pl.when(t + 1 < tiles)
        def _():
            load_col(t + 1, 1 - slot).start()

        load_col(t, slot).wait()
        product_rows(slot, 256, pl.multiple_of(t * 256, 256))

    last.start()
    last.wait()
    product_rows(tiles % 2, rest, tiles * 256)

    rows_near(0, out_terms, acc_o)
    ffn_terms = [(dg, wg_f, ff), (du, wu_f, ff)]
    rows_far(1, ffn_terms)
    kept(*late)
    grad_far("gate")
    rows_near(1, ffn_terms, acc_m)
    grad_far("up")
    grad_near("down", 2)
    grad_near("down", 1)
    rows_final(0)

    def output_rows(m, rows):
        total = res[m, rows, :] + acc_o[m, rows, :] + far_st[m, rows, :].astype(F32)
        obuf[m, rows, :] = total.astype(BF)

    chunks(output_rows)
    keep(obuf, out_o)
    grad_near("down", 3)
    rows_final(1)

    def middle(m, rows):
        e = acc_m[m, rows, :] + far_st[m, rows, :].astype(F32)
        d = norm_back(res[m, rows, :], e, 1) + cot[m, rows, :].astype(F32)
        acc_m[m, rows, :] = d
        dr[m, rows, :] = d.astype(BF)

    chunks(middle)
    own = dr.at[:, pl.ds(0, ROWS)]
    ds = [put(own, dr.at[:, pl.ds(ROWS, ROWS)], links.y), put(own, dr.at[:, pl.ds(2 * ROWS, ROWS)], links.core)]
    na_in = keep(na_h, cot)
    wo_in = [keep(wo_f.at[:, :, :, pl.ds(k * 256, 256)], wcol.at[k]) for k in range(2)]
    grad_near("down", 0)
    arrived(ds[0])
    ds.append(put(dr.at[:, pl.ds(ROWS, ROWS)], dr.at[:, pl.ds(3 * ROWS, ROWS)], links.core))
    kept(*wo_in)
    arrived(*ds)

    @pl.loop(0, 4)
    def _(i):
        m, rows = i // 2, pl.ds(pl.multiple_of(lax.rem(i, 2) * 256, 256), 256)
        for k in range(2):
            datt[m, rows, k * 256 : (k + 1) * 256] = nn(dr[m, rows, :], wcol[k].reshape(DM, 256)).astype(BF)

    def attend_back(m):
        kv = qkv[m, :, 512:640].astype(F32)
        lane = lax.broadcasted_iota(jnp.int32, (LEN4, 128), 1)
        half = lax.broadcasted_iota(jnp.int32, (256, 128), 1) < 64
        ka = jnp.where(lane < 64, kv, 0.0)
        vb = jnp.where(lane < 64, 0.0, kv)
        kb, va = pltpu.roll(ka, 64, 1), pltpu.roll(vb, 64, 1)
        heads = [
            (k.astype(BF), k.T.astype(BF), v.astype(BF), keep_lanes)
            for k, v, keep_lanes in ((ka, va, half), (kb, vb, jnp.logical_not(half)))
        ]
        dkacc[...] = jnp.zeros_like(dkacc)
        dvacc[...] = jnp.zeros_like(dvacc)

        @pl.loop(0, 8)
        def _(i):
            lanes = pl.ds(pl.multiple_of(i // 2 * 128, 128), 128)
            rows = pl.ds(pl.multiple_of(lax.rem(i, 2) * 256, 256), 256)
            q, do = qkv[m, rows, lanes], datt[m, rows, lanes]
            bias = mask_t[m, :, rows].astype(F32)
            dq_t = jnp.zeros((128, 256), F32)
            for k, k_t, v, keep_lanes in heads:
                s = nt(k, q) * 0.125 + bias
                e = jnp.exp(s - jnp.max(s, axis=0, keepdims=True))
                p = e * (1.0 / jnp.sum(e, axis=0, keepdims=True))
                d = nt(v, do)
                ds_ = (p * (d - jnp.sum(p * d, axis=0, keepdims=True)) * 0.125).astype(BF)
                dq_t = dq_t + nn(k_t, ds_)
                zero = jnp.zeros_like(q)
                dkacc[...] += nn(ds_, jnp.where(keep_lanes, q, zero))
                dvacc[...] += nn(p.astype(BF), jnp.where(keep_lanes, do, zero))
            dqkv[m, rows, lanes] = rope_tile(dq_t.T, table[0, rows, :], -table[1, rows, :]).astype(BF)

        dk = dkacc[...] + pltpu.roll(dkacc[...], 64, 1)
        dv = dvacc[...] + pltpu.roll(dvacc[...], 64, 1)
        dk = rope_tile(dk, table[0], -table[1])
        dqkv[m, :, 512:640] = jnp.where(lane < 64, dk, dv).astype(BF)

    attend_back(0)
    grad_near("gate", 2)
    grad_near("gate", 1)
    attend_back(1)
    na_terms = [(dqkv, wqkv_f, 640)]
    rows_far(2, na_terms)
    grad_final("down")
    sent(*zid["down"].values())
    kept(na_in)
    grad_far("out")
    grad_far("qkv")
    rows_near(2, na_terms, acc_o)
    grad_near("gate", 3)
    grad_near("gate", 0)
    rows_final(2)
    own_x = far_st.at[:, pl.ds(ROWS, ROWS)]
    kept(keep(x_ref, own_x))

    def last_rows(m, rows):
        e = acc_o[m, rows, :] + far_st[m, rows, :].astype(F32)
        v = own_x[m, rows, :].astype(F32)
        acc_m[m, rows, :] += norm_back(v, e, 0)

    chunks(last_rows)
    keep(acc_m, din_o)
    gx = put(gacc.at[:, pl.ds(1024, 1024)], gxin, links.x)
    arrived(gx)
    gnear[...] = gacc[:, 0:1024] + gxin[...]
    gz = [put(gnear.at[:, pl.ds(r * 256, 256)], gzin.at[r - 1], links.z[r]) for r in (1, 2, 3)]
    grad_near("up", 2)
    arrived(*gz)
    gown[...] = gnear[:, 0:256] + gzin[0] + gzin[1] + gzin[2]
    gs = [put(gown, gsin.at[k], p) for k, p in enumerate((links.core, links.y, links.both))]
    grad_near("up", 1)
    arrived(*gs)
    gain_o[...] = gown[...] + gsin[0] + gsin[1] + gsin[2]
    grad_near("up", 3)
    grad_final("gate")
    grad_near("up", 0)
    for name in ("out", "qkv"):
        for r in ORDER:
            grad_near(name, r)
    for name in ("up", "out", "qkv"):
        grad_final(name)
    for c in writing:
        c.wait()
    links.finish()


def backward(table, mask_t, gain, x, arrays):
    micro, rows, d = x.shape
    sd = jax.ShapeDtypeStruct
    ff = arrays[-4].shape[2]
    v = pltpu.VMEM
    out_shape = [
        sd(x.shape, BF), sd(x.shape, F32), sd((8, 256), F32), sd((256, 640), F32), sd((256, 512), F32),
        sd((256, ff), F32), sd((256, ff), F32), sd((256, ff), F32), sd((3, 4, 256, ff), BF), sd((4, 256, 512), BF),
        sd((4, 256, 640), BF), sd((3, 3, 256, ff), BF), sd((3, 256, 512), BF), sd((3, 256, 640), BF),
        sd((3, 2, 256, d), BF), sd((3, 2, 128, d), BF),
    ]
    toks = (2, 512, d)
    scratch = [
        v(toks, BF), v(toks, BF), v(toks, BF), v((2, 512, ff), BF), v((2, 512, ff), BF), v((3, 4, 256, ff), BF),
        v((3, 256, ff), BF), v((256, ff), F32), v((2, 2, 4, 256, 256), BF), v((2, 2, 256, ff), BF),
        v((2, 256, d), BF), v((2, 256, d), BF), v((2, 128, d), BF), v((2, 128, d), F32), v((2, 128, d), F32),
        v((2, 128, d), F32), v((2, 512, 640), BF), v((2, 512, 512), BF), v((2, 512, 512), BF), v((2, 512, 640), BF),
        v((2, 128, d), BF), v((512, 128), F32), v((512, 128), F32), v((8, d), F32), v((8, 1024), F32),
        v((8, 1024), F32), v((3, 8, 256), F32), v((8, 256), F32), v((3, 8, 256), F32),
        pltpu.SemaphoreType.DMA((64,)), pltpu.SemaphoreType.DMA((64,)), pltpu.SemaphoreType.DMA((32,)),
        pltpu.SemaphoreType.DMA((2,)), pltpu.SemaphoreType.DMA((2, 2)), pltpu.SemaphoreType.DMA((3,)),
        pltpu.SemaphoreType.DMA((1,)),
    ]
    return pl.pallas_call(
        backward_kernel,
        out_shape=out_shape,
        in_specs=[VMEM] * 3 + [HBM] * (1 + len(arrays)),
        out_specs=[HBM] * 2 + [VMEM] + [HBM] * 13,
        scratch_shapes=scratch,
        compiler_params=pltpu.CompilerParams(collective_id=1, has_side_effects=True, vmem_limit_bytes=LIMIT_B),
    )(table, mask_t, gain, x, *arrays)


def to_relative(a):
    dp = lax.axis_index("dp")
    z, x = dp // 2, dp % 2
    lead = a.shape[:-1]
    a = a.reshape(lead + (4, 2, -1))
    a = jnp.where(x == 0, a, jnp.flip(a, -2))
    a = lax.dynamic_slice_in_dim(jnp.concatenate([a, a], -3), z, 4, len(lead))
    return jnp.swapaxes(a, -2, -3).reshape(lead + (-1,))

def from_relative(a):
    dp = lax.axis_index("dp")
    z, x = dp // 2, dp % 2
    lead = a.shape[:-1]
    a = jnp.swapaxes(a.reshape(lead + (2, 4, -1)), -2, -3)
    a = jnp.where(x == 0, a, jnp.flip(a, -2))
    a = lax.dynamic_slice_in_dim(jnp.concatenate([a, a], -3), 4 - z, 4, len(lead))
    return a.reshape(lead + (-1,))


def per_device_grid(
    inputs, segments, cotangent, attn_gain, w_query, w_key, w_value, w_out, mlp_gain, w_gate, w_up, w_down,
):
    rows = inputs.shape[1]
    nq, nk = w_query.shape[1], w_key.shape[1]
    w_qkv = jnp.concatenate([w_query, w_key, w_value], axis=1)
    x = to_relative(inputs)
    c = to_relative(cotangent)
    me = lax.axis_index("seq")
    order = [me, me ^ 2, me ^ 1, me ^ 3]
    pos = jnp.concatenate([j * rows + jnp.arange(rows, dtype=jnp.int32) for j in order])
    segs = jnp.concatenate([lax.dynamic_slice_in_dim(segments, j * rows, rows, 1) for j in order], axis=1)
    cosine, sine = rope_tables(pos)
    c4 = jnp.tile(cosine, (1, 4))
    s4 = jnp.concatenate([-sine, sine, -sine, sine], axis=1)
    one, zero = jnp.ones_like(c4[:, :64]), jnp.zeros_like(c4[:, :64])
    table = jnp.stack(
        [c4, s4, jnp.concatenate([c4[:, :64], one], axis=1), jnp.concatenate([s4[:, :64], zero], axis=1)]
    )
    same = segs[:, :, None] == segs[:, None, :]
    mask = jnp.where((pos[None, :] <= pos[:, None])[None] & same, 0.0, NEGATIVE).astype(BF)
    mask_t = jnp.where((pos[None, :] >= pos[:, None])[None] & same, 0.0, NEGATIVE).astype(BF)
    size = attn_gain.shape[0]
    g = jnp.zeros((8, 4, size), F32).at[:2, me].set(jnp.stack([attn_gain, mlp_gain]).astype(F32))
    made = forward(x, c, g.reshape(8, 4 * size), table, mask, [w_qkv, w_out, w_gate, w_up, w_down])
    c_full, wqkv, wo, wg, wu, wd, na, qkv, att, res, nm, gain, prod, fa, fb, down = made
    arrays = [c_full, wqkv, wo, wg, wu, wd, na, qkv, att, res, nm, prod, fa, fb, down]
    back = backward(table, mask_t, gain, x, arrays)
    output, d_input, gains, gq, go, gg, gu, gd = back[:8]
    gains = lax.dynamic_slice_in_dim(gains, me * size, size, 1)
    return (
        from_relative(output), from_relative(d_input), gains[0], gq[:, :nq], gq[:, nq : nq + nk], gq[:, nq + nk :],
        go, gains[1], gg, gu, gd,
    )


class AnyMesh:
    def gather(self, x, c, shards):
        fulls = [lax.all_gather(w, "dp", axis=0, tiled=True) for w in shards]
        return gather_rows(x), gather_rows(c), fulls

    def gather_gains(self, g):
        return lax.all_gather(g, ("dp", "seq"), axis=1, tiled=True)

    def scatter_gain(self, g):
        return lax.psum_scatter(g, ("dp", "seq"), scatter_dimension=0, tiled=True)

    def scatter(self, left, right):
        return lax.psum_scatter(
            outer_sum(left, right).astype(BF), "dp", scatter_dimension=0, tiled=True
        ).astype(F32)

    def to_relative(self, a):
        return a

    def from_relative(self, a):
        return a


def shift_core(a):
    return lax.ppermute(a, "seq", [(i, i ^ 1) for i in range(4)])


def shift_y(a):
    return lax.ppermute(a, "seq", [(i, i ^ 2) for i in range(4)])


def gather_rows(a):
    across = shift_y(a)
    return jnp.concatenate([a, across, shift_core(a), shift_core(across)], axis=-2)


def scatter_rows(make):
    got = shift_core(make(1).astype(BF))
    near = make(0) + got.astype(F32)
    rows = near.shape[1] // 2
    got = shift_y(near[:, rows:].astype(BF))
    return near[:, :rows] + got.astype(F32)


def per_device(
    inputs, segments, cotangent, attn_gain, w_query, w_key, w_value, w_out, mlp_gain, w_gate, w_up, w_down,
):
    micro, rows, d = inputs.shape
    seq = lax.axis_size("seq")
    length = rows * seq
    full = micro * length
    half = length // 2
    grid = AnyMesh()

    nq, nk = w_query.shape[1], w_key.shape[1]
    heads, kv_heads = nq // HD, nk // HD
    groups = heads // kv_heads
    w_qkv = jnp.concatenate([w_query, w_key, w_value], axis=1)

    inputs = grid.to_relative(inputs)
    cotangent = grid.to_relative(cotangent)
    gains = grid.gather_gains(jnp.stack([attn_gain, mlp_gain]).astype(F32))
    gain_a, gain_m = gains[0], gains[1]

    shards = [w_qkv, w_out, w_gate, w_up, w_down]
    x_full, up_full, (wqkv, wo, wg, wu, wd) = grid.gather(inputs, cotangent, shards)

    me = lax.axis_index("seq")
    order = [me, me ^ 2, me ^ 1, me ^ 3]
    pos = jnp.concatenate([j * rows + jnp.arange(rows, dtype=jnp.int32) for j in order])
    segs = jnp.concatenate([lax.dynamic_slice_in_dim(segments, j * rows, rows, 1) for j in order], axis=1)
    cosine, sine = rope_tables(pos)
    cos_f, sin_f = jnp.tile(cosine, (micro, 1)), jnp.tile(sine, (micro, 1))
    allowed = (pos[None, :] <= pos[:, None])[None] & (segs[:, :, None] == segs[:, None, :])
    allowed = allowed[:, None, None]

    def pieces(make):
        return lambda i: make(slice(i * half, (i + 1) * half)).reshape(micro, half, d)

    def rows_of(a, s):
        return a.reshape(micro, length, -1)[:, s].reshape(micro * half, -1)

    hidden_full = x_full.reshape(full, d).astype(F32)
    normed, inverse_f = normalize(hidden_full, gain_a)
    na = normed.astype(BF)
    hidden = inputs.astype(F32)
    upstream = cotangent.astype(F32)
    up_full = up_full.reshape(full, d)

    def rope(x, n, s):
        return rotate(x.reshape(full, n, HD), cos_f, s).astype(BF).reshape(full, n * HD)

    qkv = project(na, wqkv)
    q = rope(qkv[:, :nq], heads, sin_f)
    k = rope(qkv[:, nq : nq + nk], kv_heads, sin_f)
    v = qkv[:, nq + nk :].astype(BF)
    qg = q.reshape(micro, length, kv_heads, groups, HD)
    kg = k.reshape(micro, length, kv_heads, HD)
    vg = v.reshape(micro, length, kv_heads, HD)
    scores = jnp.einsum("mqkgd,mpkd->mkgqp", qg, kg, preferred_element_type=F32) * HD ** (-0.5)
    scores = jnp.where(allowed, scores, NEGATIVE)
    maximum = jnp.max(scores, axis=-1, keepdims=True)
    weights = jnp.where(allowed, jnp.exp(scores - maximum), 0.0)
    denominator = jnp.sum(weights, axis=-1, keepdims=True)
    prob = weights / denominator
    prob_b = prob.astype(BF)
    attended = jnp.einsum("mkgqp,mpkd->mqkgd", prob_b, vg, preferred_element_type=F32)
    attended = attended.astype(BF).reshape(full, heads * HD)
    residual = hidden + scatter_rows(pieces(lambda s: project_back(rows_of(attended, s), wo)))
    normed, inverse_m = normalize(residual, gain_m)
    nm = gather_rows(normed.astype(BF)).reshape(full, d)
    gate_pre = project(nm, wg)
    up_proj = project(nm, wu)
    sigmoid_g = jax.nn.sigmoid(gate_pre)
    active = gate_pre * sigmoid_g
    product = (active * up_proj).astype(BF)
    g_down = grid.scatter(up_full, product)
    d_product = project(up_full, wd)
    d_gate = (d_product * up_proj * sigmoid_g * (1.0 + gate_pre * (1.0 - sigmoid_g))).astype(BF)
    d_up = (d_product * active).astype(BF)
    d_nm = scatter_rows(
        pieces(lambda s: project_back(rows_of(d_gate, s), wg) + project_back(rows_of(d_up, s), wu))
    )
    g_gate = grid.scatter(nm, d_gate)
    g_up = grid.scatter(nm, d_up)
    output = (residual + scatter_rows(pieces(lambda s: project_back(rows_of(product, s), wd)))).astype(BF)
    flat = lambda a: a.reshape(micro * rows, -1)
    d_norm_m, g_gain_m = normalize_back(flat(residual), flat(inverse_m), gain_m, flat(d_nm))
    d_residual = upstream + d_norm_m.reshape(micro, rows, d)
    dr = gather_rows(d_residual.astype(BF)).reshape(full, d)
    d_att = project(dr, wo).astype(BF)
    dg = d_att.reshape(micro, length, kv_heads, groups, HD)
    d_values = jnp.einsum("mkgqp,mqkgd->mpkd", prob_b, dg, preferred_element_type=F32)
    d_prob = jnp.einsum("mqkgd,mpkd->mkgqp", dg, vg, preferred_element_type=F32)
    row_sum = jnp.sum(prob * d_prob, axis=-1, keepdims=True)
    d_scores = (prob * (d_prob - row_sum) * HD ** (-0.5)).astype(BF)
    d_query = jnp.einsum("mkgqp,mpkd->mqkgd", d_scores, kg, preferred_element_type=F32)
    d_keys = jnp.einsum("mkgqp,mqkgd->mpkd", d_scores, qg, preferred_element_type=F32)
    dq = rope(d_query, heads, -sin_f)
    dk = rope(d_keys, kv_heads, -sin_f)
    dv = d_values.astype(BF).reshape(full, kv_heads * HD)
    dqkv = jnp.concatenate([dq, dk, dv], axis=1)
    g_out = grid.scatter(dr, attended)
    d_na = scatter_rows(pieces(lambda s: project_back(rows_of(dqkv, s), wqkv)))
    g_qkv = grid.scatter(na, dqkv)
    inverse_a = inverse_f.reshape(micro, length, 1)[:, :rows]
    d_norm_a, g_gain_a = normalize_back(flat(hidden), flat(inverse_a), gain_a, flat(d_na))
    d_input = d_residual + d_norm_a.reshape(micro, rows, d)
    return (
        grid.from_relative(output),
        grid.from_relative(d_input),
        grid.scatter_gain(g_gain_a),
        g_qkv[:, :nq],
        g_qkv[:, nq : nq + nk],
        g_qkv[:, nq + nk :],
        g_out,
        grid.scatter_gain(g_gain_m),
        g_gate,
        g_up,
        g_down,
    )


def solution(mesh):
    tok, wt, gn = P(None, ("dp", "seq"), None), P("dp", "seq"), P(("dp", "seq"))
    grid = mesh.shape["dp"] == 8 and mesh.shape["seq"] == 4
    return jax.shard_map(
        per_device_grid if grid else per_device,
        mesh=mesh,
        in_specs=(tok, P(None, "dp"), tok, gn, wt, wt, wt, wt, gn, wt, wt, wt),
        out_specs=(tok, tok, gn, wt, wt, wt, wt, gn, wt, wt, wt),
        check_vma=False,
    )
```

```python
import jax
import jax.numpy as jnp
import numpy as np
from jax import lax
from jax.experimental import pallas as pl
from jax.experimental.pallas import tpu as pltpu
from jax.sharding import PartitionSpec as P

HD = 64
EPS = 1e-05
THETA = 10000.0
NEGATIVE = -1e30
BF = jnp.bfloat16
F32 = jnp.float32


def rope_tables(positions):
    half_dim = HD // 2
    frequency = THETA ** (-(jnp.arange(half_dim).astype(F32) * (2.0 / HD)))
    angles = positions.astype(F32)[:, None] * frequency[None, :]
    return (jnp.cos(angles), jnp.sin(angles))


def rotate(values, cosine, sine_table):
    half_dim = values.shape[-1] // 2
    c = cosine[:, None, :]
    s = sine_table[:, None, :]
    a = values[..., :half_dim]
    b = values[..., half_dim:]
    return jnp.concatenate([a * c - b * s, b * c + a * s], axis=-1)


def unrotate(gradient, cosine, sine_table):
    return rotate(gradient, cosine, -sine_table)


def normalize(hidden, gain_vec):
    inverse = lax.rsqrt(jnp.mean(hidden * hidden, axis=-1, keepdims=True) + EPS)
    return (hidden * inverse * gain_vec, inverse)


def normalize_back(hidden, inverse, gain_vec, gradient):
    unit_rows = hidden * inverse
    gain_grad = jnp.sum(gradient * unit_rows, axis=0)
    weighted = gradient * gain_vec
    return (
        inverse * (weighted - unit_rows * jnp.mean(weighted * unit_rows, axis=-1, keepdims=True)),
        gain_grad,
    )


def project(a, b):
    return jnp.dot(a, b, preferred_element_type=F32)


def project_back(a, b):
    return lax.dot_general(a, b, (((1,), (1,)), ((), ())), preferred_element_type=F32)


def outer_sum(a, b):
    return lax.dot_general(a, b, (((0,), (0,)), ((), ())), preferred_element_type=F32)


MESH_ID = pl.DeviceIdType.MESH
HBM = pl.BlockSpec(memory_space=pl.ANY)
VMEM = pl.BlockSpec(memory_space=pltpu.VMEM)
ROWS = 128
LEN4 = 512
HALF = 256
DM = 2048
LIMIT = 60 * 1024 * 1024
LIMIT_B = 62 * 1024 * 1024


def nt(a, b):
    return lax.dot_general(a, b, (((1,), (1,)), ((), ())), preferred_element_type=F32)


def tn(a, b):
    return lax.dot_general(a, b, (((0,), (0,)), ((), ())), preferred_element_type=F32)


def nn(a, b):
    return jnp.dot(a, b, preferred_element_type=F32)


class Links:
    def __init__(self, send, recv, local):
        self.send, self.recv, self.local = send, recv, local
        self.remote, self.own = [], []
        self.seen, self.gone, self.middle_only = set(), set(), set()
        dp, sq = lax.axis_index("dp"), lax.axis_index("seq")
        self.dp, self.sq = dp, sq
        height = lax.div(dp, 2)
        self.middle = jnp.logical_and(height >= 1, height <= 2)
        self.low = height <= 1
        self.z = [(lax.rem(dp + 2 * r, 8), sq) for r in range(4)]
        self.x = (dp + 1 - 2 * lax.rem(dp, 2), sq)
        core = sq + 1 - 2 * lax.rem(sq, 2)
        self.core = (dp, core)
        self.y = (dp, lax.rem(sq + 2, 4))
        self.both = (dp, lax.rem(core + 2, 4))
        peers = self.z[1:] + [self.x, self.core, self.y, self.both]
        barrier = pltpu.get_barrier_semaphore()
        for peer in peers:
            pl.semaphore_signal(barrier, inc=1, device_id=peer, device_id_type=MESH_ID)
        pl.semaphore_wait(barrier, len(peers))

    def lanes(self, b):
        z, x = lax.div(self.dp, 2), lax.rem(self.dp, 2)
        at = lax.rem(z + b % 4, 4) * 2 + (x if b < 4 else 1 - x)
        return pl.ds(pl.multiple_of(at * 256, 256), 256)

    def order(self, k):
        return (self.sq, self.y[1], self.core[1], self.both[1])[k]

    def describe(self, src, dst, peer, landing=None):
        i = len(self.remote)
        copy = pltpu.make_async_remote_copy(
            src_ref=src,
            dst_ref=dst,
            send_sem=self.send.at[i],
            recv_sem=self.recv.at[i if landing is None else landing],
            device_id=peer,
            device_id_type=MESH_ID,
        )
        self.remote.append(copy)
        return i

    def put(self, src, dst, peer):
        i = self.describe(src, dst, peer)
        self.remote[i].start()
        return i

    def start_in_middle(self, i):
        self.middle_only.add(i)
        pl.when(self.middle)(self.remote[i].start)

    def arrived(self, *ids):
        for i in ids:
            if i not in self.seen:
                self.seen.add(i)
                self.remote[i].wait_recv()

    def sent(self, *ids):
        for i in ids:
            if i not in self.gone:
                self.gone.add(i)
                if i in self.middle_only:
                    pl.when(self.middle)(self.remote[i].wait_send)
                else:
                    self.remote[i].wait_send()

    def keep(self, src, dst):
        copy = pltpu.make_async_copy(src, dst, self.local.at[len(self.own)])
        copy.start()
        self.own.append([copy, False])
        return len(self.own) - 1

    def kept(self, *ids):
        for i in ids:
            if not self.own[i][1]:
                self.own[i][1] = True
                self.own[i][0].wait()

    def finish(self):
        self.sent(*range(len(self.remote)))
        self.arrived(*range(len(self.remote)))
        self.kept(*range(len(self.own)))


def load_table(links, table_h, table):
    return [
        links.keep(
            table_h.at[:, pl.ds(pl.multiple_of(links.order(k) * ROWS, ROWS), ROWS)],
            table.at[:, pl.ds(k * ROWS, ROWS)],
        )
        for k in range(4)
    ]


def make_mask(links, seg, keys, mask, by_key):
    for k in range(4):
        at = pl.ds(k * ROWS, ROWS)
        place = links.order(k) * ROWS
        keys[0:2, at] = seg[:, pl.ds(pl.multiple_of(place, ROWS), ROWS)].astype(F32)
        keys[2:3, at] = (lax.broadcasted_iota(jnp.int32, (1, ROWS), 1) + place).astype(F32)
    columns = keys[...].T
    for m in range(2):
        for k in range(4):
            at = slice(k * ROWS, (k + 1) * ROWS)
            same = columns[at, m : m + 1] == keys[m : m + 1, :]
            a, b = columns[at, 2:3], keys[2:3, :]
            ahead = (a <= b) if by_key else (b <= a)
            mask[m, at, :] = jnp.where(jnp.logical_and(same, ahead), 0.0, NEGATIVE).astype(BF)


def rope_tile(t, cosine, sine):
    lane = lax.broadcasted_iota(jnp.int32, t.shape, 1)
    turned = jnp.where(lax.rem(lane, 64) < 32, pltpu.roll(t, 96, 1), pltpu.roll(t, 32, 1))
    return t * cosine + turned * sine


def forward_kernel(
    x_ref, c_ref, g_ref, seg, table_h, wqkv_s, wo_s, wg_s, wu_s, wd_s,
    c_full, wqkv_f, wo_f, wg_f, wu_f, wd_f, na_o, qkv_o, att_o, res_o, nm_o, gain_o, prod_o, fa_o, fb_o, down_o,
    xf, nm, wqkv_v, wo_v, qkv, att, far, far_in, near, ysend, yin, own_x, gseq, gfull, gown, prod, fa, fb, wt, lbuf, gbuf, table, mask, keys,
    send, recv, local, wsem, lsem, gsem,
):
    links = Links(send, recv, local)
    put, arrived = links.put, links.arrived
    first, rest = pl.ds(0, 768), pl.ds(768, wg_s.shape[1] - 768)
    shards = [wqkv_s, wo_s] + [w.at[:, s] for s in (first, rest) for w in (wg_s, wu_s)] + [wd_s]
    fulls = [wqkv_f, wo_f] + [w.at[:, :, :, s] for s in (first, rest) for w in (wg_f, wu_f)] + [wd_f]

    def part(full, k):
        return full.at[:, pl.ds(k * ROWS, ROWS)]

    def seq_start(src, full):
        return [put(src, part(full, 1), links.y), put(src, part(full, 2), links.core)]

    def seq_forward(full, ids):
        arrived(ids[0])
        ids.append(put(part(full, 1), part(full, 3), links.core))

    placed = []

    def z_start(i):
        placed.append(links.keep(shards[i], fulls[i].at[0, 0]))
        return {r: put(shards[i], fulls[i].at[0, r], links.z[4 - r]) for r in (1, 3)}

    def x_own(i):
        return [put(shards[i], fulls[i].at[1, 0], links.x)]

    def x_near(i, copies, ids):
        full = fulls[i]
        relay = {1: links.describe(full.at[0, 1], full.at[0, 2], links.z[3])}
        copies[2] = relay[1]
        relay[3] = links.describe(full.at[0, 3], full.at[0, 2], links.z[1], relay[1])
        links.seen.add(relay[3])
        for r in (1, 3):
            arrived(copies[r])
            links.start_in_middle(relay[r])
            ids.append(put(full.at[0, r], full.at[1, r], links.x))

    def x_far(i, copies, ids):
        arrived(copies[2])
        ids.append(put(fulls[i].at[0, 2], fulls[i].at[1, 2], links.x))

    placing = [links.keep(x_ref.at[:, :, links.lanes(b)], xf.at[:, pl.ds(0, ROWS), pl.ds(b * 256, 256)]) for b in range(8)]
    c_own = [links.keep(c_ref.at[:, :, links.lanes(b)], c_full.at[:, pl.ds(0, ROWS), pl.ds(b * 256, 256)]) for b in range(8)]
    table_in = load_table(links, table_h, table)
    gs = [put(g_ref, gseq.at[k], p) for k, p in ((1, links.core), (2, links.y), (3, links.both))]
    zs, xd = {}, {}

    def start(i):
        zs[i] = z_start(i)

    def across(i):
        xd[i] = x_own(i)

    def near_blocks(i):
        x_near(i, zs[i], xd[i])

    def far_block(i):
        x_far(i, zs[i], xd[i])

    start(0)
    across(0)
    links.kept(*placing)
    xs = seq_start(part(xf, 0), xf)
    own1 = links.keep(part(xf, 0), own_x)
    arrived(*gs)
    gown[...] = g_ref[...] + gseq[1] + gseq[2] + gseq[3]
    gfull[0, 0] = gown[...]
    gz = [put(gown, gfull.at[0, r], links.z[4 - r]) for r in (1, 2, 3)]
    gx = [put(gown, gfull.at[1, 0], links.x)]
    start(1)
    near_blocks(0)
    make_mask(links, seg, keys, mask, False)
    links.kept(*table_in)
    for r in (1, 2, 3):
        arrived(gz[r - 1])
        gx.append(put(gfull.at[0, r], gfull.at[1, r], links.x))
    far_block(0)
    across(1)
    start(2)
    seq_forward(xf, xs)
    arrived(*gx)
    for b in range(8):
        gain_o[:, b * 256 : (b + 1) * 256] = gfull[b // 4, b % 4]
    arrived(*xs)
    links.sent(*xs)
    links.kept(own1)

    @pl.loop(0, 16)
    def _(i):
        m, r = i // 8, pl.multiple_of(lax.rem(i, 8) * 64, 64)
        v = xf[m, pl.ds(r, 64), :].astype(F32)
        inverse = lax.rsqrt(jnp.mean(v * v, axis=-1, keepdims=True) + EPS)
        xf[m, pl.ds(r, 64), :] = (v * inverse * gain_o[0:1, :]).astype(BF)

    na_copy = links.keep(xf, na_o)
    near_blocks(1)
    arrived(*xd[0])
    links.kept(placed[0])
    load0 = links.keep(wqkv_f, wqkv_v)
    links.kept(load0)

    @pl.loop(0, 4)
    def _(i):
        m, r = i // 2, pl.multiple_of(lax.rem(i, 2) * 256, 256)
        rows = pl.ds(r, 256)
        a = xf[m, rows, :]
        cq, sq = table[0, rows, :], table[1, rows, :]
        for n in range(2):
            t = nn(a, wqkv_v[:, :, :, n * 256 : (n + 1) * 256].reshape(DM, 256))
            for j in range(2):
                lanes = slice(n * 256 + j * 128, n * 256 + (j + 1) * 128)
                qkv[m, rows, lanes] = rope_tile(t[:, j * 128 : (j + 1) * 128], cq, sq).astype(BF)
        t = nn(a, wqkv_v[:, :, :, 512:640].reshape(DM, 128))
        qkv[m, rows, 512:640] = rope_tile(t, table[2, rows, :], table[3, rows, :]).astype(BF)

    links.keep(qkv, qkv_o)
    far_block(1)
    across(2)
    start(3)
    across(3)

    def attend(m):
        kv = qkv[m, :, 512:640].astype(F32)
        lane = lax.broadcasted_iota(jnp.int32, (LEN4, 128), 1)
        ka = jnp.where(lane < 64, kv, 0.0)
        vb = jnp.where(lane < 64, 0.0, kv)
        ks = [ka.astype(BF), pltpu.roll(ka, 64, 1).astype(BF)]
        vs = [pltpu.roll(vb, 64, 1).astype(BF), vb.astype(BF)]

        @pl.loop(0, 8)
        def _(i):
            lanes = pl.ds(pl.multiple_of(i // 2 * 128, 128), 128)
            rows = pl.ds(pl.multiple_of(lax.rem(i, 2) * 256, 256), 256)
            q = qkv[m, rows, lanes]
            bias = mask[m, rows, :].astype(F32)
            out = jnp.zeros((256, 128), F32)
            for k, v in zip(ks, vs):
                s = nt(q, k) * 0.125 + bias
                e = jnp.exp(s - jnp.max(s, axis=-1, keepdims=True))
                p = (e / jnp.sum(e, axis=-1, keepdims=True)).astype(BF)
                out = out + nn(p, v)
            att[m, rows, lanes] = out.astype(BF)

    attend(0)
    near_blocks(2)
    start(4)
    attend(1)
    far_block(2)
    links.keep(att, att_o)
    arrived(*xd[1])
    links.kept(placed[1])
    load1 = links.keep(wo_f, wo_v)
    links.kept(load1)

    def out_rows(m, row, dst, dtype):
        @pl.loop(0, 8)
        def _(n):
            w = wo_v[n // 4, lax.rem(n, 4)]
            lanes = pl.ds(pl.multiple_of(n * 256, 256), 256)
            dst[m, :, lanes] = nt(att[m, row : row + HALF, :], w).astype(dtype)

    for m in range(2):
        out_rows(m, HALF, far, BF)
    fc = put(far, far_in, links.core)
    near_blocks(3)
    for m in range(2):
        out_rows(m, 0, near, F32)
    arrived(fc)

    @pl.loop(0, 4)
    def _(i):
        m, r = i // 2, pl.multiple_of(lax.rem(i, 2) * 64, 64)
        rows = pl.ds(r + ROWS, 64)
        ysend[m, pl.ds(r, 64), :] = (near[m, rows, :] + far_in[m, rows, :].astype(F32)).astype(BF)

    yc = put(ysend, yin, links.y)
    far_block(3)
    across(4)
    start(5)
    across(5)
    arrived(yc)

    @pl.loop(0, 4)
    def _(i):
        m, r = i // 2, pl.multiple_of(lax.rem(i, 2) * 64, 64)
        rows = pl.ds(r, 64)
        v = near[m, rows, :] + far_in[m, rows, :].astype(F32) + yin[m, rows, :].astype(F32) + own_x[m, rows, :].astype(F32)
        res_o[m, rows, :] = v
        inverse = lax.rsqrt(jnp.mean(v * v, axis=-1, keepdims=True) + EPS)
        nm[m, rows, :] = (v * inverse * gain_o[1:2, :]).astype(BF)

    ns = seq_start(part(nm, 0), nm)
    near_blocks(4)
    far_block(4)
    start(6)
    seq_forward(nm, ns)
    links.kept(*c_own)
    cs = seq_start(part(c_full, 0), c_full)
    arrived(*ns)
    links.keep(nm, nm_o)
    arrived(*xd[2], *xd[3])
    links.kept(placed[2], placed[3])

    def load(t, slot):
        lanes = pl.ds(pl.multiple_of(t * 128, 128), 128)
        return [
            pltpu.make_async_copy(w.at[:, :, :, lanes], wt.at[slot, :, :, :, pl.ds(k * 128, 128)], wsem.at[slot, k])
            for k, w in enumerate((wg_f, wu_f))
        ]

    def up_tile(t, slot):
        lanes = pl.ds(pl.multiple_of(t * 128, 128), 128)

        @pl.loop(0, 4)
        def _(i):
            m, rows = i // 2, pl.ds(pl.multiple_of(lax.rem(i, 2) * 256, 256), 256)
            r = nn(nm[m, rows, :], wt[slot].reshape(DM, 256))
            g, u = r[:, :128], r[:, 128:]
            s = jax.nn.sigmoid(g)
            active = g * s
            prod[m, rows, lanes] = (active * u).astype(BF)
            fa[m, rows, lanes] = (u * s * (1.0 + g * (1.0 - s))).astype(BF)
            fb[m, rows, lanes] = active.astype(BF)

    for c in load(0, 0):
        c.start()
    tiles = wg_s.shape[1] // 128

    def tile_step(t):
        slot = lax.rem(t, 2)

        @pl.when(t + 1 < tiles)
        def _():
            for c in load(t + 1, 1 - slot):
                c.start()

        for c in load(t, slot):
            c.wait()
        up_tile(t, slot)

    pl.loop(0, 3)(tile_step)
    near_blocks(5)
    far_block(5)
    across(6)
    pl.loop(3, 5)(tile_step)
    near_blocks(6)
    seq_forward(c_full, cs)
    arrived(*xd[4], *xd[5])
    links.kept(placed[4], placed[5])
    pl.loop(5, 7)(tile_step)
    far_block(6)
    pl.loop(7, tiles)(tile_step)
    links.keep(prod, prod_o)
    links.keep(fa, fa_o)
    links.keep(fb, fb_o)
    arrived(*cs)

    def load_left(b, slot):
        lanes = pl.ds(pl.multiple_of(b * 256, 256), 256)
        return pltpu.make_async_copy(c_full.at[:, :, lanes], lbuf.at[slot], lsem.at[slot])

    def store_grad(b, slot):
        return pltpu.make_async_copy(gbuf.at[slot], down_o.at[b // 4, lax.rem(b, 4)], gsem.at[slot])

    load_left(0, 0).start()

    @pl.loop(0, 8)
    def _(b):
        slot = lax.rem(b, 2)

        @pl.when(b + 1 < 8)
        def _():
            load_left(b + 1, 1 - slot).start()

        load_left(b, slot).wait()

        @pl.when(b >= 2)
        def _():
            store_grad(b - 2, slot).wait()

        gbuf[slot] = (tn(lbuf[slot, 0], prod[0]) + tn(lbuf[slot, 1], prod[1])).astype(BF)
        store_grad(b, slot).start()

    store_grad(6, 0).wait()
    store_grad(7, 1).wait()
    links.finish()


def forward(x, c, g, seg, table, shards):
    micro, rows, d = x.shape
    sd = jax.ShapeDtypeStruct
    toks = (micro, 4 * rows, d)
    nq, nf = shards[1].shape[1], shards[2].shape[1]
    fulls = [sd((2, 4) + w.shape, BF) for w in shards]
    ffn = sd((micro, 4 * rows, nf), BF)
    out_shape = [sd(toks, BF)] + fulls + [
        sd(toks, BF), sd((micro, 4 * rows, 640), BF), sd((micro, 4 * rows, nq), BF),
        sd((micro, rows, d), F32), sd(toks, BF), sd((8, d), F32), ffn, ffn, ffn, sd((2, 4, 256, nf), BF),
    ]
    v = pltpu.VMEM
    scratch = [
        v(toks, BF), v(toks, BF), v((2, 4, 256, 640), BF), v((2, 4, 256, 512), BF), v((2, 512, 640), BF),
        v((2, 512, 512), BF), v((2, 256, d), BF), v((2, 256, d), BF), v((2, 256, d), F32), v((2, 128, d), BF),
        v((2, 128, d), BF), v((2, 128, d), BF), v((4, 8, 256), F32), v((2, 4, 8, 256), F32), v((8, 256), F32),
        v((2, 512, nf), BF), v((2, 512, nf), BF), v((2, 512, nf), BF), v((2, 2, 4, 256, 256), BF), v((2, 2, 512, 256), BF), v((2, 256, nf), BF),
        v((4, 512, 128), F32), v((2, 512, 512), BF), v((8, 512), F32),
        pltpu.SemaphoreType.DMA((96,)), pltpu.SemaphoreType.DMA((96,)), pltpu.SemaphoreType.DMA((56,)),
        pltpu.SemaphoreType.DMA((2, 2)), pltpu.SemaphoreType.DMA((2,)), pltpu.SemaphoreType.DMA((2,)),
    ]
    return pl.pallas_call(
        forward_kernel,
        out_shape=out_shape,
        in_specs=[HBM, HBM, VMEM, VMEM, HBM] + [HBM] * 5,
        out_specs=[HBM] * 9 + [VMEM, HBM, VMEM] + [HBM] * 4,
        scratch_shapes=scratch,
        compiler_params=pltpu.CompilerParams(collective_id=0, has_side_effects=True, vmem_limit_bytes=LIMIT),
    )(x, c, g, seg, table, *shards)


ORDER = (2, 1, 3, 0)


def backward_kernel(
    seg, gain, table_h, x_ref, c_full, wqkv_f, wo_f, wg_f, wu_f, wd_f, na_h, qkv_h, att_h, res_h, nm_h, prod_h, fa_h,
    fb_h, down_h,
    out_o, din_o, gain_o, gq_o, go_o, gg_o, gu_o, gd_o, xin_f, xin_o, xin_q, zin_f, zin_o, zin_q, fin, yin,
    cot, nm, dr, dg, du, grads, stage, ostage, wcol, wrow, far, far_st, ysend, acc_m, acc_o, res, qkv, att, datt, dqkv,
    obuf, dkacc, dvacc, gacc, gxin, gnear, gzin, gown, gsin, table, mask_t, keys,
    send, recv, local, csem, rsem, ssem, osem,
):
    links = Links(send, recv, local)
    put, arrived, sent, keep, kept = links.put, links.arrived, links.sent, links.keep, links.kept
    ff = fa_h.shape[2]
    prod = dr.at[:, :, pl.ds(0, ff)]

    def wide(k):
        return lambda r: grads.at[k, r]

    def cut(start, width):
        return lambda r: grads.at[0, r, :, pl.ds(start, width)]

    spec = {
        "down": (None, None, wide(0), xin_f.at[0], zin_f.at[0], ff, gd_o),
        "gate": (nm, dg, wide(1), xin_f.at[1], zin_f.at[1], ff, gg_o),
        "up": (nm, du, wide(2), xin_f.at[2], zin_f.at[2], ff, gu_o),
        "out": (dr, att, cut(0, 512), xin_o, zin_o, 512, go_o),
        "qkv": (cot, dqkv, cut(512, 640), xin_q, zin_q, 640, gq_o),
    }
    relays = {}
    xid = {name: {} for name in spec}
    zid = {name: {} for name in spec}

    def block_of(name, b):
        left, right = spec[name][:2]
        lanes = pl.ds(b * 256, 256)
        return tn(left[0, :, lanes], right[0]) + tn(left[1, :, lanes], right[1])

    def grad_far(name):
        buffer, landing = spec[name][2:4]
        for r in ORDER:
            if name == "down":
                xid[name][r] = put(down_h.at[1, r], landing.at[r], links.x)
            else:
                buffer(r)[...] = block_of(name, 4 + r).astype(BF)
                xid[name][r] = put(buffer(r), landing.at[r], links.x)

    def grad_near(name, r):
        buffer, landing, zland, width = spec[name][2:6]
        arrived(xid[name][r])
        got = stage.at[0, :, pl.ds(0, width)]
        copies = [pltpu.make_async_copy(landing.at[r], got, ssem.at[0])]
        if name == "down":
            copies.append(pltpu.make_async_copy(down_h.at[0, r], stage.at[1], ssem.at[1]))
        for c in copies:
            c.start()
        if name != "down":
            mine = block_of(name, r)
            sent(xid[name][r])
        for c in copies:
            c.wait()
        if name == "down":
            mine = stage[1].astype(F32)
        buffer(r)[...] = (mine + got[...].astype(F32)).astype(BF)
        if r == 2:
            low = links.describe(buffer(2), zland.at[2], links.z[1])
            high = links.describe(buffer(2), zland.at[3], links.z[3])
            pl.when(links.low)(links.remote[low].start)
            pl.when(jnp.logical_not(links.low))(links.remote[high].start)
            links.seen.update((low, high))
            links.gone.update((low, high))
            relays[name] = (low, high)

    def grad_on(name):
        buffer, _, zland, width = spec[name][2:6]
        got = stage.at[0, :, pl.ds(0, width)]
        for k, r in enumerate((1, 3)):
            copy = pltpu.make_async_copy(zland.at[2 + k], got, ssem.at[0])

            @pl.when(links.middle)
            def _():
                links.remote[relays[name][k]].wait_recv()
                copy.start()
                copy.wait()
                buffer(r)[...] = (buffer(r)[...].astype(F32) + got[...].astype(F32)).astype(BF)

            zid[name][r] = put(buffer(r), zland.at[k], links.z[r])

    def far_sent(name):
        low, high = relays[name]
        pl.when(links.low)(links.remote[low].wait_send)
        pl.when(jnp.logical_not(links.low))(links.remote[high].wait_send)

    writing = []

    def grad_final(name):
        buffer, _, zland, width, result = spec[name][2:]
        copies = []
        for k, r in enumerate((1, 3)):
            arrived(zid[name][r])
            copies.append(pltpu.make_async_copy(zland.at[k], stage.at[k, :, pl.ds(0, width)], ssem.at[k]))
            copies[-1].start()
        for c in copies + writing:
            c.wait()
        lanes = slice(0, width)
        total = buffer(0)[...].astype(F32) + stage[0, :, lanes].astype(F32)
        ostage[:, lanes] = total + stage[1, :, lanes].astype(F32)
        writing[:] = [pltpu.make_async_copy(ostage.at[:, pl.ds(0, width)], result, osem.at[0])]
        writing[0].start()

    def sweep(terms, row, use):
        def load(b, slot):
            return [
                pltpu.make_async_copy(
                    w.at[b // 4, lax.rem(b, 4)], wrow.at[slot, k, :, pl.ds(0, width)], rsem.at[slot, k]
                )
                for k, (_, w, width) in enumerate(terms)
            ]

        for c in load(0, 0):
            c.start()

        @pl.loop(0, 8)
        def _(b):
            slot = lax.rem(b, 2)

            @pl.when(b + 1 < 8)
            def _():
                for c in load(b + 1, 1 - slot):
                    c.start()

            for c in load(b, slot):
                c.wait()
            lanes = pl.ds(pl.multiple_of(b * 256, 256), 256)
            for m in range(2):
                total = None
                for k, (left, _, width) in enumerate(terms):
                    t = nt(left[m, row : row + HALF, 0:width], wrow[slot, k, :, 0:width])
                    total = t if total is None else total + t
                use(m, lanes, total)

    fid, yid = [], []

    def rows_far(i, terms):
        sent(*fid)

        def use(m, lanes, total):
            far[m, :, lanes] = total.astype(BF)

        sweep(terms, HALF, use)
        fid.append(put(far, fin.at[i], links.core))

    def rows_near(i, terms, acc):
        sent(*yid)
        arrived(fid[i])
        kept(keep(fin.at[i], far_st))

        def use(m, lanes, total):
            total = total + far_st[m, :, lanes].astype(F32)
            acc[m, :, lanes] = total[:ROWS]
            ysend[m, :, lanes] = total[ROWS:].astype(BF)

        sweep(terms, 0, use)
        yid.append(put(ysend, yin.at[i], links.y))

    def rows_final(i):
        arrived(yid[i])
        kept(keep(yin.at[i], far_st.at[:, pl.ds(0, ROWS)]))

    def chunks(body):
        @pl.loop(0, 4)
        def _(i):
            body(i // 2, pl.ds(pl.multiple_of(lax.rem(i, 2) * 64, 64), 64))

    def norm_back(v, e, row):
        inverse = lax.rsqrt(jnp.mean(v * v, axis=-1, keepdims=True) + EPS)
        u = v * inverse
        gacc[row : row + 1, :] += jnp.sum(e * u, axis=0, keepdims=True)
        w = e * gain[row : row + 1, :]
        return inverse * (w - u * jnp.mean(w * u, axis=-1, keepdims=True))

    grad_far("down")
    prod_in = keep(prod_h, prod)
    cot_in = keep(c_full, cot)
    ffn_in = [keep(fa_h, dg), keep(fb_h, du)]
    late = [keep(nm_h, nm), keep(res_h, res), keep(qkv_h, qkv), keep(att_h, att)]
    late += load_table(links, table_h, table)
    gacc[...] = jnp.zeros_like(gacc)

    def load_col(t, slot):
        lanes = pl.ds(pl.multiple_of(t * 256, 256), 256)
        return pltpu.make_async_copy(wd_f.at[:, :, :, lanes], wcol.at[slot], csem.at[slot])

    load_col(0, 0).start()
    kept(prod_in)
    out_terms = [(prod, wd_f, ff)]
    rows_far(0, out_terms)
    kept(cot_in, *ffn_in)
    tiles = ff // 256
    rest = ff - tiles * 256

    def product_rows(slot, width, start):
        @pl.loop(0, 4)
        def _(i):
            m, rows = i // 2, pl.ds(pl.multiple_of(lax.rem(i, 2) * 256, 256), 256)
            lanes = pl.ds(start, width)
            d = nn(cot[m, rows, :], wcol[slot, :, :, :, 0:width].reshape(DM, width))
            dg[m, rows, lanes] = (d * dg[m, rows, lanes].astype(F32)).astype(BF)
            du[m, rows, lanes] = (d * du[m, rows, lanes].astype(F32)).astype(BF)

    last = pltpu.make_async_copy(
        wd_f.at[:, :, :, pl.ds(tiles * 256, rest)], wcol.at[tiles % 2, :, :, :, pl.ds(0, rest)], csem.at[tiles % 2]
    )

    @pl.loop(0, tiles)
    def _(t):
        slot = lax.rem(t, 2)

        @pl.when(t + 1 < tiles)
        def _():
            load_col(t + 1, 1 - slot).start()

        load_col(t, slot).wait()
        product_rows(slot, 256, pl.multiple_of(t * 256, 256))

    last.start()
    last.wait()
    product_rows(tiles % 2, rest, tiles * 256)

    kept(*late)
    grad_far("gate")
    grad_near("down", 2)
    rows_near(0, out_terms, acc_o)
    grad_near("down", 1)
    ffn_terms = [(dg, wg_f, ff), (du, wu_f, ff)]
    rows_far(1, ffn_terms)
    grad_far("up")
    grad_near("down", 3)
    rows_near(1, ffn_terms, acc_m)
    grad_near("down", 0)
    make_mask(links, seg, keys, mask_t, True)
    rows_final(0)

    def output_rows(m, rows):
        total = res[m, rows, :] + acc_o[m, rows, :] + far_st[m, rows, :].astype(F32)
        obuf[m, rows, :] = total.astype(BF)

    chunks(output_rows)
    for b in range(8):
        keep(obuf.at[:, :, pl.ds(b * 256, 256)], out_o.at[:, :, links.lanes(b)])
    grad_on("down")
    rows_final(1)

    def middle(m, rows):
        e = acc_m[m, rows, :] + far_st[m, rows, :].astype(F32)
        d = norm_back(res[m, rows, :], e, 1) + cot[m, rows, :].astype(F32)
        acc_m[m, rows, :] = d
        dr[m, rows, :] = d.astype(BF)

    chunks(middle)
    own = dr.at[:, pl.ds(0, ROWS)]
    ds = [put(own, dr.at[:, pl.ds(ROWS, ROWS)], links.y), put(own, dr.at[:, pl.ds(2 * ROWS, ROWS)], links.core)]
    na_in = keep(na_h, cot)
    wo_in = [keep(wo_f.at[:, :, :, pl.ds(k * 256, 256)], wcol.at[k]) for k in range(2)]
    grad_near("gate", 2)
    grad_near("gate", 1)
    arrived(ds[0])
    ds.append(put(dr.at[:, pl.ds(ROWS, ROWS)], dr.at[:, pl.ds(3 * ROWS, ROWS)], links.core))
    kept(*wo_in)
    arrived(*ds)

    @pl.loop(0, 4)
    def _(i):
        m, rows = i // 2, pl.ds(pl.multiple_of(lax.rem(i, 2) * 256, 256), 256)
        for k in range(2):
            datt[m, rows, k * 256 : (k + 1) * 256] = nn(dr[m, rows, :], wcol[k].reshape(DM, 256)).astype(BF)

    def attend_back(m):
        kv = qkv[m, :, 512:640].astype(F32)
        lane = lax.broadcasted_iota(jnp.int32, (LEN4, 128), 1)
        half = lax.broadcasted_iota(jnp.int32, (256, 128), 1) < 64
        ka = jnp.where(lane < 64, kv, 0.0)
        vb = jnp.where(lane < 64, 0.0, kv)
        kb, va = pltpu.roll(ka, 64, 1), pltpu.roll(vb, 64, 1)
        heads = [
            (k.astype(BF), k.T.astype(BF), v.astype(BF), keep_lanes)
            for k, v, keep_lanes in ((ka, va, half), (kb, vb, jnp.logical_not(half)))
        ]
        dkacc[...] = jnp.zeros_like(dkacc)
        dvacc[...] = jnp.zeros_like(dvacc)

        @pl.loop(0, 8)
        def _(i):
            lanes = pl.ds(pl.multiple_of(i // 2 * 128, 128), 128)
            rows = pl.ds(pl.multiple_of(lax.rem(i, 2) * 256, 256), 256)
            q, do = qkv[m, rows, lanes], datt[m, rows, lanes]
            bias = mask_t[m, :, rows].astype(F32)
            dq_t = jnp.zeros((128, 256), F32)
            for k, k_t, v, keep_lanes in heads:
                s = nt(k, q) * 0.125 + bias
                e = jnp.exp(s - jnp.max(s, axis=0, keepdims=True))
                p = e * (1.0 / jnp.sum(e, axis=0, keepdims=True))
                d = nt(v, do)
                ds_ = (p * (d - jnp.sum(p * d, axis=0, keepdims=True)) * 0.125).astype(BF)
                dq_t = dq_t + nn(k_t, ds_)
                zero = jnp.zeros_like(q)
                dkacc[...] += nn(ds_, jnp.where(keep_lanes, q, zero))
                dvacc[...] += nn(p.astype(BF), jnp.where(keep_lanes, do, zero))
            dqkv[m, rows, lanes] = rope_tile(dq_t.T, table[0, rows, :], -table[1, rows, :]).astype(BF)

        dk = dkacc[...] + pltpu.roll(dkacc[...], 64, 1)
        dv = dvacc[...] + pltpu.roll(dvacc[...], 64, 1)
        dk = rope_tile(dk, table[0], -table[1])
        dqkv[m, :, 512:640] = jnp.where(lane < 64, dk, dv).astype(BF)

    attend_back(0)
    grad_near("gate", 3)
    grad_near("gate", 0)
    grad_on("gate")
    attend_back(1)
    na_terms = [(dqkv, wqkv_f, 640)]
    rows_far(2, na_terms)
    grad_final("down")
    far_sent("down")
    sent(*zid["down"].values())
    kept(na_in)
    grad_far("out")
    grad_far("qkv")
    rows_near(2, na_terms, acc_o)
    grad_near("up", 2)
    grad_near("up", 1)
    grad_near("up", 3)
    rows_final(2)
    own_x = far_st.at[:, pl.ds(ROWS, ROWS)]
    kept(*[keep(x_ref.at[:, :, links.lanes(b)], own_x.at[:, :, pl.ds(b * 256, 256)]) for b in range(8)])

    def last_rows(m, rows):
        e = acc_o[m, rows, :] + far_st[m, rows, :].astype(F32)
        v = own_x[m, rows, :].astype(F32)
        acc_m[m, rows, :] += norm_back(v, e, 0)

    chunks(last_rows)
    for b in range(8):
        keep(acc_m.at[:, :, pl.ds(b * 256, 256)], din_o.at[:, :, links.lanes(b)])
    gx = put(gacc.at[:, pl.ds(1024, 1024)], gxin, links.x)
    arrived(gx)
    gnear[...] = gacc[:, 0:1024] + gxin[...]
    gz = [put(gnear.at[:, pl.ds(r * 256, 256)], gzin.at[r - 1], links.z[r]) for r in (1, 2, 3)]
    grad_near("up", 0)
    grad_on("up")
    arrived(*gz)
    gown[...] = gnear[:, 0:256] + gzin[0] + gzin[1] + gzin[2]
    gs = [put(gown, gsin.at[k], p) for k, p in enumerate((links.core, links.y, links.both))]
    grad_final("gate")
    arrived(*gs)
    gain_o[...] = gown[...] + gsin[0] + gsin[1] + gsin[2]
    for name in ("out", "qkv"):
        for r in ORDER:
            grad_near(name, r)
        grad_on(name)
    for name in ("up", "out", "qkv"):
        grad_final(name)
    for c in writing:
        c.wait()
    for name in ("gate", "up", "out", "qkv"):
        far_sent(name)
    links.finish()


def backward(seg, gain, table, x, arrays):
    micro, rows, d = x.shape
    sd = jax.ShapeDtypeStruct
    ff = arrays[-4].shape[2]
    v = pltpu.VMEM
    out_shape = [
        sd(x.shape, BF), sd(x.shape, F32), sd((8, 256), F32), sd((256, 640), F32), sd((256, 512), F32),
        sd((256, ff), F32), sd((256, ff), F32), sd((256, ff), F32), sd((3, 4, 256, ff), BF), sd((4, 256, 512), BF),
        sd((4, 256, 640), BF), sd((3, 4, 256, ff), BF), sd((4, 256, 512), BF), sd((4, 256, 640), BF),
        sd((3, 2, 256, d), BF), sd((3, 2, 128, d), BF),
    ]
    toks = (2, 512, d)
    scratch = [
        v(toks, BF), v(toks, BF), v(toks, BF), v((2, 512, ff), BF), v((2, 512, ff), BF), v((3, 4, 256, ff), BF),
        v((3, 256, ff), BF), v((256, ff), F32), v((2, 2, 4, 256, 256), BF), v((2, 2, 256, ff), BF),
        v((2, 256, d), BF), v((2, 256, d), BF), v((2, 128, d), BF), v((2, 128, d), F32), v((2, 128, d), F32),
        v((2, 128, d), F32), v((2, 512, 640), BF), v((2, 512, 512), BF), v((2, 512, 512), BF), v((2, 512, 640), BF),
        v((2, 128, d), BF), v((512, 128), F32), v((512, 128), F32), v((8, d), F32), v((8, 1024), F32),
        v((8, 1024), F32), v((3, 8, 256), F32), v((8, 256), F32), v((3, 8, 256), F32),
        v((4, 512, 128), F32), v((2, 512, 512), BF), v((8, 512), F32),
        pltpu.SemaphoreType.DMA((80,)), pltpu.SemaphoreType.DMA((80,)), pltpu.SemaphoreType.DMA((64,)),
        pltpu.SemaphoreType.DMA((2,)), pltpu.SemaphoreType.DMA((2, 2)), pltpu.SemaphoreType.DMA((3,)),
        pltpu.SemaphoreType.DMA((1,)),
    ]
    return pl.pallas_call(
        backward_kernel,
        out_shape=out_shape,
        in_specs=[VMEM] * 2 + [HBM] * (2 + len(arrays)),
        out_specs=[HBM] * 2 + [VMEM] + [HBM] * 13,
        scratch_shapes=scratch,
        compiler_params=pltpu.CompilerParams(collective_id=1, has_side_effects=True, vmem_limit_bytes=LIMIT_B),
    )(seg, gain, table, x, *arrays)


def rope_table():
    frequency = THETA ** (-(np.arange(HD // 2) * (2.0 / HD)))
    angles = np.arange(LEN4)[:, None] * frequency[None, :]
    cosine, sine = np.cos(angles), np.sin(angles)
    c4 = np.tile(cosine, (1, 4))
    s4 = np.concatenate([-sine, sine, -sine, sine], axis=1)
    one, zero = np.ones((LEN4, HD)), np.zeros((LEN4, HD))
    ck, sk = np.concatenate([c4[:, :HD], one], axis=1), np.concatenate([s4[:, :HD], zero], axis=1)
    return np.stack([c4, s4, ck, sk]).astype(np.float32)


def per_device_grid(
    inputs, segments, cotangent, attn_gain, w_query, w_key, w_value, w_out, mlp_gain, w_gate, w_up, w_down,
):
    nq, nk = w_query.shape[1], w_key.shape[1]
    w_qkv = jnp.concatenate([w_query, w_key, w_value], axis=1)
    me = lax.axis_index("seq")
    size = attn_gain.shape[0]
    row = lax.broadcasted_iota(jnp.int32, (8, 4 * size), 0)
    lane = lax.broadcasted_iota(jnp.int32, (8, 4 * size), 1)
    g = jnp.where(row == 0, jnp.tile(attn_gain, 4)[None].astype(F32), jnp.tile(mlp_gain, 4)[None].astype(F32))
    g = jnp.where(jnp.logical_and(row < 2, lane // size == me), g, 0.0)
    table = jnp.asarray(rope_table())
    made = forward(inputs, cotangent, g, segments, table, [w_qkv, w_out, w_gate, w_up, w_down])
    c_full, wqkv, wo, wg, wu, wd, na, qkv, att, res, nm, gain, prod, fa, fb, down = made
    arrays = [c_full, wqkv, wo, wg, wu, wd, na, qkv, att, res, nm, prod, fa, fb, down]
    back = backward(segments, gain, table, inputs, arrays)
    output, d_input, gains, gq, go, gg, gu, gd = back[:8]
    gains = lax.dynamic_slice_in_dim(gains, me * size, size, 1)
    return (
        output, d_input, gains[0], gq[:, :nq], gq[:, nq : nq + nk], gq[:, nq + nk :], go, gains[1], gg, gu, gd,
    )


class AnyMesh:
    def gather(self, x, c, shards):
        fulls = [lax.all_gather(w, "dp", axis=0, tiled=True) for w in shards]
        return gather_rows(x), gather_rows(c), fulls

    def gather_gains(self, g):
        return lax.all_gather(g, ("dp", "seq"), axis=1, tiled=True)

    def scatter_gain(self, g):
        return lax.psum_scatter(g, ("dp", "seq"), scatter_dimension=0, tiled=True)

    def scatter(self, left, right):
        return lax.psum_scatter(
            outer_sum(left, right).astype(BF), "dp", scatter_dimension=0, tiled=True
        ).astype(F32)

    def to_relative(self, a):
        return a

    def from_relative(self, a):
        return a


def shift_core(a):
    return lax.ppermute(a, "seq", [(i, i ^ 1) for i in range(4)])


def shift_y(a):
    return lax.ppermute(a, "seq", [(i, i ^ 2) for i in range(4)])


def gather_rows(a):
    across = shift_y(a)
    return jnp.concatenate([a, across, shift_core(a), shift_core(across)], axis=-2)


def scatter_rows(make):
    got = shift_core(make(1).astype(BF))
    near = make(0) + got.astype(F32)
    rows = near.shape[1] // 2
    got = shift_y(near[:, rows:].astype(BF))
    return near[:, :rows] + got.astype(F32)


def per_device(
    inputs, segments, cotangent, attn_gain, w_query, w_key, w_value, w_out, mlp_gain, w_gate, w_up, w_down,
):
    micro, rows, d = inputs.shape
    seq = lax.axis_size("seq")
    length = rows * seq
    full = micro * length
    half = length // 2
    grid = AnyMesh()

    nq, nk = w_query.shape[1], w_key.shape[1]
    heads, kv_heads = nq // HD, nk // HD
    groups = heads // kv_heads
    w_qkv = jnp.concatenate([w_query, w_key, w_value], axis=1)

    inputs = grid.to_relative(inputs)
    cotangent = grid.to_relative(cotangent)
    gains = grid.gather_gains(jnp.stack([attn_gain, mlp_gain]).astype(F32))
    gain_a, gain_m = gains[0], gains[1]

    shards = [w_qkv, w_out, w_gate, w_up, w_down]
    x_full, up_full, (wqkv, wo, wg, wu, wd) = grid.gather(inputs, cotangent, shards)

    me = lax.axis_index("seq")
    order = [me, me ^ 2, me ^ 1, me ^ 3]
    pos = jnp.concatenate([j * rows + jnp.arange(rows, dtype=jnp.int32) for j in order])
    segs = jnp.concatenate([lax.dynamic_slice_in_dim(segments, j * rows, rows, 1) for j in order], axis=1)
    cosine, sine = rope_tables(pos)
    cos_f, sin_f = jnp.tile(cosine, (micro, 1)), jnp.tile(sine, (micro, 1))
    allowed = (pos[None, :] <= pos[:, None])[None] & (segs[:, :, None] == segs[:, None, :])
    allowed = allowed[:, None, None]

    def pieces(make):
        return lambda i: make(slice(i * half, (i + 1) * half)).reshape(micro, half, d)

    def rows_of(a, s):
        return a.reshape(micro, length, -1)[:, s].reshape(micro * half, -1)

    hidden_full = x_full.reshape(full, d).astype(F32)
    normed, inverse_f = normalize(hidden_full, gain_a)
    na = normed.astype(BF)
    hidden = inputs.astype(F32)
    upstream = cotangent.astype(F32)
    up_full = up_full.reshape(full, d)

    def rope(x, n, s):
        return rotate(x.reshape(full, n, HD), cos_f, s).astype(BF).reshape(full, n * HD)

    qkv = project(na, wqkv)
    q = rope(qkv[:, :nq], heads, sin_f)
    k = rope(qkv[:, nq : nq + nk], kv_heads, sin_f)
    v = qkv[:, nq + nk :].astype(BF)
    qg = q.reshape(micro, length, kv_heads, groups, HD)
    kg = k.reshape(micro, length, kv_heads, HD)
    vg = v.reshape(micro, length, kv_heads, HD)
    scores = jnp.einsum("mqkgd,mpkd->mkgqp", qg, kg, preferred_element_type=F32) * HD ** (-0.5)
    scores = jnp.where(allowed, scores, NEGATIVE)
    maximum = jnp.max(scores, axis=-1, keepdims=True)
    weights = jnp.where(allowed, jnp.exp(scores - maximum), 0.0)
    denominator = jnp.sum(weights, axis=-1, keepdims=True)
    prob = weights / denominator
    prob_b = prob.astype(BF)
    attended = jnp.einsum("mkgqp,mpkd->mqkgd", prob_b, vg, preferred_element_type=F32)
    attended = attended.astype(BF).reshape(full, heads * HD)
    residual = hidden + scatter_rows(pieces(lambda s: project_back(rows_of(attended, s), wo)))
    normed, inverse_m = normalize(residual, gain_m)
    nm = gather_rows(normed.astype(BF)).reshape(full, d)
    gate_pre = project(nm, wg)
    up_proj = project(nm, wu)
    sigmoid_g = jax.nn.sigmoid(gate_pre)
    active = gate_pre * sigmoid_g
    product = (active * up_proj).astype(BF)
    g_down = grid.scatter(up_full, product)
    d_product = project(up_full, wd)
    d_gate = (d_product * up_proj * sigmoid_g * (1.0 + gate_pre * (1.0 - sigmoid_g))).astype(BF)
    d_up = (d_product * active).astype(BF)
    d_nm = scatter_rows(
        pieces(lambda s: project_back(rows_of(d_gate, s), wg) + project_back(rows_of(d_up, s), wu))
    )
    g_gate = grid.scatter(nm, d_gate)
    g_up = grid.scatter(nm, d_up)
    output = (residual + scatter_rows(pieces(lambda s: project_back(rows_of(product, s), wd)))).astype(BF)
    flat = lambda a: a.reshape(micro * rows, -1)
    d_norm_m, g_gain_m = normalize_back(flat(residual), flat(inverse_m), gain_m, flat(d_nm))
    d_residual = upstream + d_norm_m.reshape(micro, rows, d)
    dr = gather_rows(d_residual.astype(BF)).reshape(full, d)
    d_att = project(dr, wo).astype(BF)
    dg = d_att.reshape(micro, length, kv_heads, groups, HD)
    d_values = jnp.einsum("mkgqp,mqkgd->mpkd", prob_b, dg, preferred_element_type=F32)
    d_prob = jnp.einsum("mqkgd,mpkd->mkgqp", dg, vg, preferred_element_type=F32)
    row_sum = jnp.sum(prob * d_prob, axis=-1, keepdims=True)
    d_scores = (prob * (d_prob - row_sum) * HD ** (-0.5)).astype(BF)
    d_query = jnp.einsum("mkgqp,mpkd->mqkgd", d_scores, kg, preferred_element_type=F32)
    d_keys = jnp.einsum("mkgqp,mqkgd->mpkd", d_scores, qg, preferred_element_type=F32)
    dq = rope(d_query, heads, -sin_f)
    dk = rope(d_keys, kv_heads, -sin_f)
    dv = d_values.astype(BF).reshape(full, kv_heads * HD)
    dqkv = jnp.concatenate([dq, dk, dv], axis=1)
    g_out = grid.scatter(dr, attended)
    d_na = scatter_rows(pieces(lambda s: project_back(rows_of(dqkv, s), wqkv)))
    g_qkv = grid.scatter(na, dqkv)
    inverse_a = inverse_f.reshape(micro, length, 1)[:, :rows]
    d_norm_a, g_gain_a = normalize_back(flat(hidden), flat(inverse_a), gain_a, flat(d_na))
    d_input = d_residual + d_norm_a.reshape(micro, rows, d)
    return (
        grid.from_relative(output),
        grid.from_relative(d_input),
        grid.scatter_gain(g_gain_a),
        g_qkv[:, :nq],
        g_qkv[:, nq : nq + nk],
        g_qkv[:, nq + nk :],
        g_out,
        grid.scatter_gain(g_gain_m),
        g_gate,
        g_up,
        g_down,
    )


def solution(mesh):
    tok, wt, gn = P(None, ("dp", "seq"), None), P("dp", "seq"), P(("dp", "seq"))
    grid = mesh.shape["dp"] == 8 and mesh.shape["seq"] == 4
    return jax.shard_map(
        per_device_grid if grid else per_device,
        mesh=mesh,
        in_specs=(tok, P(None, "dp"), tok, gn, wt, wt, wt, wt, gn, wt, wt, wt),
        out_specs=(tok, tok, gn, wt, wt, wt, wt, gn, wt, wt, wt),
        check_vma=False,
    )
```

```python
import jax
import jax.numpy as jnp
import numpy as np
from jax import lax
from jax.experimental import pallas as pl
from jax.experimental.pallas import tpu as pltpu
from jax.sharding import PartitionSpec as P

HD = 64
EPS = 1e-05
THETA = 10000.0
NEGATIVE = -1e30
BF = jnp.bfloat16
F32 = jnp.float32


def rope_tables(positions):
    half_dim = HD // 2
    frequency = THETA ** (-(jnp.arange(half_dim).astype(F32) * (2.0 / HD)))
    angles = positions.astype(F32)[:, None] * frequency[None, :]
    return (jnp.cos(angles), jnp.sin(angles))


def rotate(values, cosine, sine_table):
    half_dim = values.shape[-1] // 2
    c = cosine[:, None, :]
    s = sine_table[:, None, :]
    a = values[..., :half_dim]
    b = values[..., half_dim:]
    return jnp.concatenate([a * c - b * s, b * c + a * s], axis=-1)


def unrotate(gradient, cosine, sine_table):
    return rotate(gradient, cosine, -sine_table)


def normalize(hidden, gain_vec):
    inverse = lax.rsqrt(jnp.mean(hidden * hidden, axis=-1, keepdims=True) + EPS)
    return (hidden * inverse * gain_vec, inverse)


def normalize_back(hidden, inverse, gain_vec, gradient):
    unit_rows = hidden * inverse
    gain_grad = jnp.sum(gradient * unit_rows, axis=0)
    weighted = gradient * gain_vec
    return (
        inverse * (weighted - unit_rows * jnp.mean(weighted * unit_rows, axis=-1, keepdims=True)),
        gain_grad,
    )


def project(a, b):
    return jnp.dot(a, b, preferred_element_type=F32)


def project_back(a, b):
    return lax.dot_general(a, b, (((1,), (1,)), ((), ())), preferred_element_type=F32)


def outer_sum(a, b):
    return lax.dot_general(a, b, (((0,), (0,)), ((), ())), preferred_element_type=F32)


MESH_ID = pl.DeviceIdType.MESH
HBM = pl.BlockSpec(memory_space=pl.ANY)
VMEM = pl.BlockSpec(memory_space=pltpu.VMEM)
ROWS = 128
LEN4 = 512
HALF = 256
DM = 2048
LIMIT = 60 * 1024 * 1024
LIMIT_B = 62 * 1024 * 1024


def nt(a, b):
    return lax.dot_general(a, b, (((1,), (1,)), ((), ())), preferred_element_type=F32)


def tn(a, b):
    return lax.dot_general(a, b, (((0,), (0,)), ((), ())), preferred_element_type=F32)


def nn(a, b):
    return jnp.dot(a, b, preferred_element_type=F32)


class Links:
    def __init__(self, send, recv, local):
        self.send, self.recv, self.local = send, recv, local
        self.remote, self.own = [], []
        self.seen, self.gone, self.middle_only = set(), set(), set()
        dp, sq = lax.axis_index("dp"), lax.axis_index("seq")
        self.dp, self.sq = dp, sq
        height = lax.div(dp, 2)
        self.middle = jnp.logical_and(height >= 1, height <= 2)
        self.low = height <= 1
        self.z = [(lax.rem(dp + 2 * r, 8), sq) for r in range(4)]
        self.x = (dp + 1 - 2 * lax.rem(dp, 2), sq)
        core = sq + 1 - 2 * lax.rem(sq, 2)
        self.core = (dp, core)
        self.y = (dp, lax.rem(sq + 2, 4))
        self.both = (dp, lax.rem(core + 2, 4))
        peers = self.z[1:] + [self.x, self.core, self.y, self.both]
        barrier = pltpu.get_barrier_semaphore()
        for peer in peers:
            pl.semaphore_signal(barrier, inc=1, device_id=peer, device_id_type=MESH_ID)
        pl.semaphore_wait(barrier, len(peers))

    def lanes(self, b):
        z, x = lax.div(self.dp, 2), lax.rem(self.dp, 2)
        at = lax.rem(z + b % 4, 4) * 2 + (x if b < 4 else 1 - x)
        return pl.ds(pl.multiple_of(at * 256, 256), 256)

    def order(self, k):
        return (self.sq, self.y[1], self.core[1], self.both[1])[k]

    def describe(self, src, dst, peer, landing=None):
        i = len(self.remote)
        copy = pltpu.make_async_remote_copy(
            src_ref=src,
            dst_ref=dst,
            send_sem=self.send.at[i],
            recv_sem=self.recv.at[i if landing is None else landing],
            device_id=peer,
            device_id_type=MESH_ID,
        )
        self.remote.append(copy)
        return i

    def put(self, src, dst, peer):
        i = self.describe(src, dst, peer)
        self.remote[i].start()
        return i

    def start_in_middle(self, i):
        self.middle_only.add(i)
        pl.when(self.middle)(self.remote[i].start)

    def arrived(self, *ids):
        for i in ids:
            if i not in self.seen:
                self.seen.add(i)
                self.remote[i].wait_recv()

    def sent(self, *ids):
        for i in ids:
            if i not in self.gone:
                self.gone.add(i)
                if i in self.middle_only:
                    pl.when(self.middle)(self.remote[i].wait_send)
                else:
                    self.remote[i].wait_send()

    def keep(self, src, dst):
        copy = pltpu.make_async_copy(src, dst, self.local.at[len(self.own)])
        copy.start()
        self.own.append([copy, False])
        return len(self.own) - 1

    def kept(self, *ids):
        for i in ids:
            if not self.own[i][1]:
                self.own[i][1] = True
                self.own[i][0].wait()

    def finish(self):
        self.sent(*range(len(self.remote)))
        self.arrived(*range(len(self.remote)))
        self.kept(*range(len(self.own)))


def load_table(links, table_h, table):
    return [
        links.keep(
            table_h.at[:, pl.ds(pl.multiple_of(links.order(k) * ROWS, ROWS), ROWS)],
            table.at[:, pl.ds(k * ROWS, ROWS)],
        )
        for k in range(4)
    ]


def make_mask(links, seg, keys, mask, by_key):
    for k in range(4):
        at = pl.ds(k * ROWS, ROWS)
        place = links.order(k) * ROWS
        keys[0:2, at] = seg[:, pl.ds(pl.multiple_of(place, ROWS), ROWS)].astype(F32)
        keys[2:3, at] = (lax.broadcasted_iota(jnp.int32, (1, ROWS), 1) + place).astype(F32)
    columns = keys[...].T
    for m in range(2):
        for k in range(4):
            at = slice(k * ROWS, (k + 1) * ROWS)
            same = columns[at, m : m + 1] == keys[m : m + 1, :]
            a, b = columns[at, 2:3], keys[2:3, :]
            ahead = (a <= b) if by_key else (b <= a)
            mask[m, at, :] = jnp.where(jnp.logical_and(same, ahead), 0.0, NEGATIVE).astype(BF)


def rope_tile(t, cosine, sine):
    lane = lax.broadcasted_iota(jnp.int32, t.shape, 1)
    turned = jnp.where(lax.rem(lane, 64) < 32, pltpu.roll(t, 96, 1), pltpu.roll(t, 32, 1))
    return t * cosine + turned * sine


def forward_kernel(
    x_ref, c_ref, g_ref, seg, table_h, wqkv_s, wo_s, wg_s, wu_s, wd_s,
    c_full, wqkv_f, wo_f, wg_f, wu_f, wd_f, na_o, qkv_o, att_o, res_o, nm_o, gain_o, prod_o, fa_o, fb_o, down_o,
    xf, nm, wqkv_v, wo_v, qkv, att, far, far_in, near, ysend, yin, own_x, gseq, gfull, gown, prod, fa, fb, wt, lbuf, gbuf, table, mask, keys,
    send, recv, local, wsem, lsem, gsem,
):
    links = Links(send, recv, local)
    put, arrived = links.put, links.arrived
    first, rest = pl.ds(0, 768), pl.ds(768, wg_s.shape[1] - 768)
    sixth, seventh = pl.ds(0, 640), pl.ds(640, wd_s.shape[1] - 640)
    shards = [wqkv_s, wo_s] + [w.at[:, s] for s in (first, rest) for w in (wg_s, wu_s)]
    fulls = [wqkv_f, wo_f] + [w.at[:, :, :, s] for s in (first, rest) for w in (wg_f, wu_f)]
    shards += [wd_s.at[:, sixth], wd_s.at[:, seventh]]
    fulls += [wd_f.at[:, :, :, sixth], wd_f.at[:, :, :, seventh]]

    def part(full, k):
        return full.at[:, pl.ds(k * ROWS, ROWS)]

    def seq_start(src, full):
        return [put(src, part(full, 1), links.y), put(src, part(full, 2), links.core)]

    def seq_forward(full, ids):
        arrived(ids[0])
        ids.append(put(part(full, 1), part(full, 3), links.core))

    placed = []

    def z_start(i):
        placed.append(links.keep(shards[i], fulls[i].at[0, 0]))
        return {r: put(shards[i], fulls[i].at[0, r], links.z[4 - r]) for r in (1, 3)}

    def x_own(i):
        return [put(shards[i], fulls[i].at[1, 0], links.x)]

    def relays(full, rx, copies):
        copies[2] = links.describe(full.at[rx, 1], full.at[rx, 2], links.z[3])
        other = links.describe(full.at[rx, 3], full.at[rx, 2], links.z[1], copies[2])
        links.seen.add(other)
        return {1: copies[2], 3: other}

    def x_near(i, copies, ids):
        full = fulls[i]
        relay = relays(full, 0, copies)
        for r in (1, 3):
            arrived(copies[r])
            links.start_in_middle(relay[r])
            ids.append(put(full.at[0, r], full.at[1, r], links.x))

    def pair_start(i, ids):
        full = fulls[i]
        placed.append(links.keep(shards[i], full.at[0, 0]))
        arrived(*ids)
        return [
            {r: put(src, full.at[rx, r], links.z[4 - r]) for r in (1, 3)}
            for rx, src in enumerate((shards[i], full.at[1, 0]))
        ]

    def pair_on(i, pair):
        for rx, copies in enumerate(pair):
            relay = relays(fulls[i], rx, copies)
            for r in (1, 3):
                arrived(copies[r])
                links.start_in_middle(relay[r])

    def x_far(i, copies, ids):
        arrived(copies[2])
        ids.append(put(fulls[i].at[0, 2], fulls[i].at[1, 2], links.x))

    placing = [links.keep(x_ref.at[:, :, links.lanes(b)], xf.at[:, pl.ds(0, ROWS), pl.ds(b * 256, 256)]) for b in range(8)]
    c_own = [links.keep(c_ref.at[:, :, links.lanes(b)], c_full.at[:, pl.ds(0, ROWS), pl.ds(b * 256, 256)]) for b in range(8)]
    table_in = load_table(links, table_h, table)
    gs = [put(g_ref, gseq.at[k], p) for k, p in ((1, links.core), (2, links.y), (3, links.both))]
    zs, xd = {}, {}

    def start(i):
        zs[i] = z_start(i)

    def across(i):
        xd[i] = x_own(i)

    def near_blocks(i):
        x_near(i, zs[i], xd[i])

    def far_block(i):
        x_far(i, zs[i], xd[i])

    start(0)
    across(0)
    links.kept(*placing)
    xs = seq_start(part(xf, 0), xf)
    own1 = links.keep(part(xf, 0), own_x)
    arrived(*gs)
    gown[...] = g_ref[...] + gseq[1] + gseq[2] + gseq[3]
    gfull[0, 0] = gown[...]
    gz = [put(gown, gfull.at[0, r], links.z[4 - r]) for r in (1, 2, 3)]
    gx = [put(gown, gfull.at[1, 0], links.x)]
    start(1)
    near_blocks(0)
    make_mask(links, seg, keys, mask, False)
    links.kept(*table_in)
    for r in (1, 2, 3):
        arrived(gz[r - 1])
        gx.append(put(gfull.at[0, r], gfull.at[1, r], links.x))
    far_block(0)
    across(1)
    start(2)
    seq_forward(xf, xs)
    arrived(*gx)
    for b in range(8):
        gain_o[:, b * 256 : (b + 1) * 256] = gfull[b // 4, b % 4]
    arrived(*xs)
    links.sent(*xs)
    links.kept(own1)

    @pl.loop(0, 16)
    def _(i):
        m, r = i // 8, pl.multiple_of(lax.rem(i, 8) * 64, 64)
        v = xf[m, pl.ds(r, 64), :].astype(F32)
        inverse = lax.rsqrt(jnp.mean(v * v, axis=-1, keepdims=True) + EPS)
        xf[m, pl.ds(r, 64), :] = (v * inverse * gain_o[0:1, :]).astype(BF)

    na_copy = links.keep(xf, na_o)
    near_blocks(1)
    arrived(*xd[0])
    links.kept(placed[0])
    load0 = links.keep(wqkv_f, wqkv_v)
    links.kept(load0)

    @pl.loop(0, 4)
    def _(i):
        m, r = i // 2, pl.multiple_of(lax.rem(i, 2) * 256, 256)
        rows = pl.ds(r, 256)
        a = xf[m, rows, :]
        cq, sq = table[0, rows, :], table[1, rows, :]
        for n in range(2):
            t = nn(a, wqkv_v[:, :, :, n * 256 : (n + 1) * 256].reshape(DM, 256))
            for j in range(2):
                lanes = slice(n * 256 + j * 128, n * 256 + (j + 1) * 128)
                qkv[m, rows, lanes] = rope_tile(t[:, j * 128 : (j + 1) * 128], cq, sq).astype(BF)
        t = nn(a, wqkv_v[:, :, :, 512:640].reshape(DM, 128))
        qkv[m, rows, 512:640] = rope_tile(t, table[2, rows, :], table[3, rows, :]).astype(BF)

    links.keep(qkv, qkv_o)
    far_block(1)
    across(2)
    start(3)
    across(3)

    def attend(m):
        kv = qkv[m, :, 512:640].astype(F32)
        lane = lax.broadcasted_iota(jnp.int32, (LEN4, 128), 1)
        ka = jnp.where(lane < 64, kv, 0.0)
        vb = jnp.where(lane < 64, 0.0, kv)
        ks = [ka.astype(BF), pltpu.roll(ka, 64, 1).astype(BF)]
        vs = [pltpu.roll(vb, 64, 1).astype(BF), vb.astype(BF)]

        @pl.loop(0, 8)
        def _(i):
            lanes = pl.ds(pl.multiple_of(i // 2 * 128, 128), 128)
            rows = pl.ds(pl.multiple_of(lax.rem(i, 2) * 256, 256), 256)
            q = qkv[m, rows, lanes]
            bias = mask[m, rows, :].astype(F32)
            out = jnp.zeros((256, 128), F32)
            for k, v in zip(ks, vs):
                s = nt(q, k) * 0.125 + bias
                e = jnp.exp(s - jnp.max(s, axis=-1, keepdims=True))
                p = (e / jnp.sum(e, axis=-1, keepdims=True)).astype(BF)
                out = out + nn(p, v)
            att[m, rows, lanes] = out.astype(BF)

    attend(0)
    near_blocks(2)
    start(4)
    attend(1)
    far_block(2)
    links.keep(att, att_o)
    arrived(*xd[1])
    links.kept(placed[1])
    load1 = links.keep(wo_f, wo_v)
    links.kept(load1)

    def out_rows(m, row, dst, dtype):
        @pl.loop(0, 8)
        def _(n):
            w = wo_v[n // 4, lax.rem(n, 4)]
            lanes = pl.ds(pl.multiple_of(n * 256, 256), 256)
            dst[m, :, lanes] = nt(att[m, row : row + HALF, :], w).astype(dtype)

    for m in range(2):
        out_rows(m, HALF, far, BF)
    fc = put(far, far_in, links.core)
    near_blocks(3)
    for m in range(2):
        out_rows(m, 0, near, F32)
    arrived(fc)

    @pl.loop(0, 4)
    def _(i):
        m, r = i // 2, pl.multiple_of(lax.rem(i, 2) * 64, 64)
        rows = pl.ds(r + ROWS, 64)
        ysend[m, pl.ds(r, 64), :] = (near[m, rows, :] + far_in[m, rows, :].astype(F32)).astype(BF)

    yc = put(ysend, yin, links.y)
    far_block(3)
    across(4)
    start(5)
    across(5)
    across(7)
    arrived(yc)

    @pl.loop(0, 4)
    def _(i):
        m, r = i // 2, pl.multiple_of(lax.rem(i, 2) * 64, 64)
        rows = pl.ds(r, 64)
        v = near[m, rows, :] + far_in[m, rows, :].astype(F32) + yin[m, rows, :].astype(F32) + own_x[m, rows, :].astype(F32)
        res_o[m, rows, :] = v
        inverse = lax.rsqrt(jnp.mean(v * v, axis=-1, keepdims=True) + EPS)
        nm[m, rows, :] = (v * inverse * gain_o[1:2, :]).astype(BF)

    ns = seq_start(part(nm, 0), nm)
    near_blocks(4)
    far_block(4)
    start(6)
    seq_forward(nm, ns)
    links.kept(*c_own)
    cs = seq_start(part(c_full, 0), c_full)
    arrived(*ns)
    links.keep(nm, nm_o)
    arrived(*xd[2], *xd[3])
    links.kept(placed[2], placed[3])

    def load(t, slot):
        lanes = pl.ds(pl.multiple_of(t * 128, 128), 128)
        return [
            pltpu.make_async_copy(w.at[:, :, :, lanes], wt.at[slot, :, :, :, pl.ds(k * 128, 128)], wsem.at[slot, k])
            for k, w in enumerate((wg_f, wu_f))
        ]

    def up_tile(t, slot):
        lanes = pl.ds(pl.multiple_of(t * 128, 128), 128)

        @pl.loop(0, 4)
        def _(i):
            m, rows = i // 2, pl.ds(pl.multiple_of(lax.rem(i, 2) * 256, 256), 256)
            r = nn(nm[m, rows, :], wt[slot].reshape(DM, 256))
            g, u = r[:, :128], r[:, 128:]
            s = jax.nn.sigmoid(g)
            active = g * s
            prod[m, rows, lanes] = (active * u).astype(BF)
            fa[m, rows, lanes] = (u * s * (1.0 + g * (1.0 - s))).astype(BF)
            fb[m, rows, lanes] = active.astype(BF)

    for c in load(0, 0):
        c.start()
    tiles = wg_s.shape[1] // 128

    def tile_step(t):
        slot = lax.rem(t, 2)

        @pl.when(t + 1 < tiles)
        def _():
            for c in load(t + 1, 1 - slot):
                c.start()

        for c in load(t, slot):
            c.wait()
        up_tile(t, slot)

    pl.loop(0, 3)(tile_step)
    near_blocks(5)
    far_block(5)
    across(6)
    pair = pair_start(7, xd[7])
    pl.loop(3, 5)(tile_step)
    near_blocks(6)
    seq_forward(c_full, cs)
    arrived(*xd[4], *xd[5])
    links.kept(placed[4], placed[5])
    far_block(6)
    pl.loop(5, 8)(tile_step)
    pair_on(7, pair)
    pl.loop(8, tiles)(tile_step)
    links.keep(prod, prod_o)
    links.keep(fa, fa_o)
    links.keep(fb, fb_o)
    arrived(*cs)

    def load_left(b, slot):
        lanes = pl.ds(pl.multiple_of(b * 256, 256), 256)
        return pltpu.make_async_copy(c_full.at[:, :, lanes], lbuf.at[slot], lsem.at[slot])

    def store_grad(b, slot):
        return pltpu.make_async_copy(gbuf.at[slot], down_o.at[b // 4, lax.rem(b, 4)], gsem.at[slot])

    load_left(0, 0).start()

    @pl.loop(0, 8)
    def _(b):
        slot = lax.rem(b, 2)

        @pl.when(b + 1 < 8)
        def _():
            load_left(b + 1, 1 - slot).start()

        load_left(b, slot).wait()

        @pl.when(b >= 2)
        def _():
            store_grad(b - 2, slot).wait()

        gbuf[slot] = (tn(lbuf[slot, 0], prod[0]) + tn(lbuf[slot, 1], prod[1])).astype(BF)
        store_grad(b, slot).start()

    store_grad(6, 0).wait()
    store_grad(7, 1).wait()
    links.finish()


def forward(x, c, g, seg, table, shards):
    micro, rows, d = x.shape
    sd = jax.ShapeDtypeStruct
    toks = (micro, 4 * rows, d)
    nq, nf = shards[1].shape[1], shards[2].shape[1]
    fulls = [sd((2, 4) + w.shape, BF) for w in shards]
    ffn = sd((micro, 4 * rows, nf), BF)
    out_shape = [sd(toks, BF)] + fulls + [
        sd(toks, BF), sd((micro, 4 * rows, 640), BF), sd((micro, 4 * rows, nq), BF),
        sd((micro, rows, d), F32), sd(toks, BF), sd((8, d), F32), ffn, ffn, ffn, sd((2, 4, 256, nf), BF),
    ]
    v = pltpu.VMEM
    scratch = [
        v(toks, BF), v(toks, BF), v((2, 4, 256, 640), BF), v((2, 4, 256, 512), BF), v((2, 512, 640), BF),
        v((2, 512, 512), BF), v((2, 256, d), BF), v((2, 256, d), BF), v((2, 256, d), F32), v((2, 128, d), BF),
        v((2, 128, d), BF), v((2, 128, d), BF), v((4, 8, 256), F32), v((2, 4, 8, 256), F32), v((8, 256), F32),
        v((2, 512, nf), BF), v((2, 512, nf), BF), v((2, 512, nf), BF), v((2, 2, 4, 256, 256), BF), v((2, 2, 512, 256), BF), v((2, 256, nf), BF),
        v((4, 512, 128), F32), v((2, 512, 512), BF), v((8, 512), F32),
        pltpu.SemaphoreType.DMA((96,)), pltpu.SemaphoreType.DMA((96,)), pltpu.SemaphoreType.DMA((56,)),
        pltpu.SemaphoreType.DMA((2, 2)), pltpu.SemaphoreType.DMA((2,)), pltpu.SemaphoreType.DMA((2,)),
    ]
    return pl.pallas_call(
        forward_kernel,
        out_shape=out_shape,
        in_specs=[HBM, HBM, VMEM, VMEM, HBM] + [HBM] * 5,
        out_specs=[HBM] * 9 + [VMEM, HBM, VMEM] + [HBM] * 4,
        scratch_shapes=scratch,
        compiler_params=pltpu.CompilerParams(collective_id=0, has_side_effects=True, vmem_limit_bytes=LIMIT),
    )(x, c, g, seg, table, *shards)


ORDER = (2, 1, 3, 0)


def backward_kernel(
    seg, gain, table_h, x_ref, c_full, wqkv_f, wo_f, wg_f, wu_f, wd_f, na_h, qkv_h, att_h, res_h, nm_h, prod_h, fa_h,
    fb_h, down_h,
    out_o, din_o, gain_o, gq_o, go_o, gg_o, gu_o, gd_o, xin_f, xin_o, xin_q, zin_f, zin_o, zin_q, fin, yin, pin, pxin,
    cot, nm, dr, dg, du, grads, grads_a, stage, ostage, wcol, wrow, far, far_st, ysend, ysend_o, acc_m, acc_o, res, qkv, att, datt, dqkv,
    obuf, dkacc, dvacc, gacc, gxin, gnear, gzin, gown, gsin, table, mask_t, keys,
    send, recv, local, csem, rsem, ssem, osem,
):
    links = Links(send, recv, local)
    put, arrived, sent, keep, kept = links.put, links.arrived, links.sent, links.keep, links.kept
    ff = fa_h.shape[2]
    prod = cot.at[:, :, pl.ds(0, ff)]

    def wide(k):
        return lambda r: grads.at[k, r]

    def cut(start, width):
        return lambda r: grads_a.at[r, :, pl.ds(start, width)]

    ahead = 640
    behind = ff - ahead
    low_lanes, high_lanes = pl.ds(0, ahead), pl.ds(ahead, behind)

    def down_block(r):
        return grads.at[0, r, :, low_lanes]

    spec = {
        "down": (None, None, down_block, xin_f.at[0, :, :, low_lanes], zin_f.at[0, :, :, low_lanes], ahead, gd_o),
        "gate": (nm, dg, wide(1), xin_f.at[1], zin_f.at[1], ff, gg_o),
        "up": (nm, du, wide(2), xin_f.at[2], zin_f.at[2], ff, gu_o),
        "out": (dr, att, cut(0, 512), xin_o, zin_o, 512, go_o),
        "qkv": (cot, dqkv, cut(512, 640), xin_q, zin_q, 640, gq_o),
    }
    relays, pairs = {}, []
    xid = {name: {} for name in spec}
    zid = {name: {} for name in spec}

    def block_of(name, b):
        left, right = spec[name][:2]
        lanes = pl.ds(b * 256, 256)
        return tn(left[0, :, lanes], right[0]) + tn(left[1, :, lanes], right[1])

    def two_away(name, src, zland):
        low = links.describe(src, zland.at[2], links.z[1])
        high = links.describe(src, zland.at[3], links.z[3])
        pl.when(links.low)(links.remote[low].start)
        pl.when(jnp.logical_not(links.low))(links.remote[high].start)
        links.seen.update((low, high))
        links.gone.update((low, high))
        relays[name] = (low, high)

    def pair_start():
        for rx in range(2):
            two_away(("pair", rx), down_h.at[rx, 2, :, high_lanes], pin.at[rx])

    def pair_on():
        for rx in range(2):
            for k, r in enumerate((1, 3)):
                got, mine = stage.at[0, :, pl.ds(0, behind)], grads.at[0, rx * 2 + k, :, high_lanes]
                load = pltpu.make_async_copy(down_h.at[rx, r, :, high_lanes], mine, ssem.at[1])
                copy = pltpu.make_async_copy(pin.at[rx, 2 + k], got, ssem.at[0])
                load.start()
                load.wait()

                @pl.when(links.middle)
                def _():
                    links.remote[relays["pair", rx][k]].wait_recv()
                    copy.start()
                    copy.wait()
                    mine[...] = (mine[...].astype(F32) + got[...].astype(F32)).astype(BF)

                pairs.append(put(mine, pin.at[rx, k], links.z[r]))

    def pair_sum():
        for rx in (1, 0):
            arrived(*pairs[2 * rx : 2 * rx + 2])
            sent(*pairs[2 * rx : 2 * rx + 2])
            copies = [
                pltpu.make_async_copy(src, stage.at[k, :, pl.ds(0, behind)], ssem.at[k])
                for k, src in enumerate((down_h.at[rx, 0, :, high_lanes], pin.at[rx, 0], pin.at[rx, 1]))
            ]
            for c in copies:
                c.start()
            for c in copies:
                c.wait()
            total = stage[0, :, 0:behind].astype(F32) + stage[1, :, 0:behind].astype(F32)
            mine = grads.at[0, rx * 2, :, high_lanes]
            mine[...] = (total + stage[2, :, 0:behind].astype(F32)).astype(BF)
            if rx:
                pairs.append(put(mine, pxin, links.x))

    def grad_far(name):
        buffer, landing = spec[name][2:4]
        for r in ORDER:
            if name == "down":
                xid[name][r] = put(down_h.at[1, r, :, low_lanes], landing.at[r], links.x)
            else:
                buffer(r)[...] = block_of(name, 4 + r).astype(BF)
                xid[name][r] = put(buffer(r), landing.at[r], links.x)

    def grad_near(name, r):
        buffer, landing, zland, width = spec[name][2:6]
        arrived(xid[name][r])
        got = stage.at[0, :, pl.ds(0, width)]
        copies = [pltpu.make_async_copy(landing.at[r], got, ssem.at[0])]
        if name == "down":
            copies.append(pltpu.make_async_copy(down_h.at[0, r, :, low_lanes], stage.at[1, :, low_lanes], ssem.at[1]))
        for c in copies:
            c.start()
        if name != "down":
            mine = block_of(name, r)
            sent(xid[name][r])
        for c in copies:
            c.wait()
        if name == "down":
            mine = stage[1, :, low_lanes].astype(F32)
        buffer(r)[...] = (mine + got[...].astype(F32)).astype(BF)
        if r == 2:
            two_away(name, buffer(2), zland)

    def grad_on(name):
        buffer, _, zland, width = spec[name][2:6]
        got = stage.at[0, :, pl.ds(0, width)]
        for k, r in enumerate((1, 3)):
            copy = pltpu.make_async_copy(zland.at[2 + k], got, ssem.at[0])

            @pl.when(links.middle)
            def _():
                links.remote[relays[name][k]].wait_recv()
                copy.start()
                copy.wait()
                buffer(r)[...] = (buffer(r)[...].astype(F32) + got[...].astype(F32)).astype(BF)

            zid[name][r] = put(buffer(r), zland.at[k], links.z[r])

    def far_sent(name):
        low, high = relays[name]
        pl.when(links.low)(links.remote[low].wait_send)
        pl.when(jnp.logical_not(links.low))(links.remote[high].wait_send)

    writing = []

    def grad_final(name):
        buffer, _, zland, width, result = spec[name][2:]
        copies = []
        for k, r in enumerate((1, 3)):
            arrived(zid[name][r])
            copies.append(pltpu.make_async_copy(zland.at[k], stage.at[k, :, pl.ds(0, width)], ssem.at[k]))
            copies[-1].start()
        if name == "down":
            arrived(pairs[4])
            copies.append(pltpu.make_async_copy(pxin, stage.at[2, :, pl.ds(0, behind)], ssem.at[2]))
            copies[-1].start()
        for c in copies + writing:
            c.wait()
        lanes = slice(0, width)
        total = buffer(0)[...].astype(F32) + stage[0, :, lanes].astype(F32)
        ostage[:, lanes] = total + stage[1, :, lanes].astype(F32)
        if name == "down":
            width = ff
            ostage[:, high_lanes] = grads[0, 0, :, high_lanes].astype(F32) + stage[2, :, 0:behind].astype(F32)
        writing[:] = [pltpu.make_async_copy(ostage.at[:, pl.ds(0, width)], result, osem.at[0])]
        writing[0].start()

    def sweep(terms, row, use):
        def load(b, slot):
            return [
                pltpu.make_async_copy(
                    w.at[b // 4, lax.rem(b, 4)], wrow.at[slot, k, :, pl.ds(0, width)], rsem.at[slot, k]
                )
                for k, (_, w, width) in enumerate(terms)
            ]

        for c in load(0, 0):
            c.start()

        @pl.loop(0, 8)
        def _(b):
            slot = lax.rem(b, 2)

            @pl.when(b + 1 < 8)
            def _():
                for c in load(b + 1, 1 - slot):
                    c.start()

            for c in load(b, slot):
                c.wait()
            lanes = pl.ds(pl.multiple_of(b * 256, 256), 256)
            for m in range(2):
                total = None
                for k, (left, _, width) in enumerate(terms):
                    t = nt(left[m, row : row + HALF, 0:width], wrow[slot, k, :, 0:width])
                    total = t if total is None else total + t
                use(m, lanes, total)

    fid, yid = {}, {}

    def rows_far(i, terms):
        sent(*fid.values())

        def use(m, lanes, total):
            far[m, :, lanes] = total.astype(BF)

        sweep(terms, HALF, use)
        fid[i] = put(far, fin.at[i], links.core)

    def rows_near(i, terms, acc, leaving):
        arrived(fid[i])
        kept(keep(fin.at[i], far_st))

        def use(m, lanes, total):
            total = total + far_st[m, :, lanes].astype(F32)
            acc[m, :, lanes] = total[:ROWS]
            leaving[m, :, lanes] = total[ROWS:].astype(BF)

        sweep(terms, 0, use)

    def rows_on(i, leaving):
        yid[i] = put(leaving, yin.at[i], links.y)

    def rows_final(i):
        arrived(yid[i])
        kept(keep(yin.at[i], far_st.at[:, pl.ds(0, ROWS)]))

    def chunks(body):
        @pl.loop(0, 4)
        def _(i):
            body(i // 2, pl.ds(pl.multiple_of(lax.rem(i, 2) * 64, 64), 64))

    def norm_back(v, e, row):
        inverse = lax.rsqrt(jnp.mean(v * v, axis=-1, keepdims=True) + EPS)
        u = v * inverse
        gacc[row : row + 1, :] += jnp.sum(e * u, axis=0, keepdims=True)
        w = e * gain[row : row + 1, :]
        return inverse * (w - u * jnp.mean(w * u, axis=-1, keepdims=True))

    grad_far("down")
    pair_start()
    cot_in = keep(c_full, cot)
    ffn_in = [keep(fa_h, dg), keep(fb_h, du)]
    own_in = keep(c_full.at[:, pl.ds(0, ROWS)], obuf)
    late = [keep(nm_h, nm), keep(res_h, res), keep(qkv_h, qkv), keep(att_h, att)]
    late += load_table(links, table_h, table)
    gacc[...] = jnp.zeros_like(gacc)

    def load_col(t, slot):
        lanes = pl.ds(pl.multiple_of(t * 256, 256), 256)
        return pltpu.make_async_copy(wd_f.at[:, :, :, lanes], wcol.at[slot], csem.at[slot])

    load_col(0, 0).start()
    kept(cot_in, *ffn_in)
    tiles = ff // 256
    rest = ff - tiles * 256

    def product_rows(slot, width, start):
        @pl.loop(0, 4)
        def _(i):
            m, rows = i // 2, pl.ds(pl.multiple_of(lax.rem(i, 2) * 256, 256), 256)
            lanes = pl.ds(start, width)
            d = nn(cot[m, rows, :], wcol[slot, :, :, :, 0:width].reshape(DM, width))
            dg[m, rows, lanes] = (d * dg[m, rows, lanes].astype(F32)).astype(BF)
            du[m, rows, lanes] = (d * du[m, rows, lanes].astype(F32)).astype(BF)

    last = pltpu.make_async_copy(
        wd_f.at[:, :, :, pl.ds(tiles * 256, rest)], wcol.at[tiles % 2, :, :, :, pl.ds(0, rest)], csem.at[tiles % 2]
    )

    @pl.loop(0, tiles)
    def _(t):
        slot = lax.rem(t, 2)

        @pl.when(t + 1 < tiles)
        def _():
            load_col(t + 1, 1 - slot).start()

        load_col(t, slot).wait()
        product_rows(slot, 256, pl.multiple_of(t * 256, 256))

    last.start()
    last.wait()
    product_rows(tiles % 2, rest, tiles * 256)

    prod_in = keep(prod_h, prod)
    kept(*late)
    ffn_terms = [(dg, wg_f, ff), (du, wu_f, ff)]
    rows_far(1, ffn_terms)
    grad_far("gate")
    rows_near(1, ffn_terms, acc_m, ysend)
    rows_on(1, ysend)
    grad_near("down", 2)
    grad_near("down", 1)
    grad_far("up")
    pair_on()
    grad_near("down", 3)
    grad_near("down", 0)
    grad_on("down")
    kept(prod_in)
    out_terms = [(prod, wd_f, ff)]
    rows_far(0, out_terms)
    make_mask(links, seg, keys, mask_t, True)
    kept(own_in)
    rows_final(1)

    def output_rows(m, rows):
        total = res[m, rows, :] + acc_o[m, rows, :] + far_st[m, rows, :].astype(F32)
        obuf[m, rows, :] = total.astype(BF)

    def middle(m, rows):
        e = acc_m[m, rows, :] + far_st[m, rows, :].astype(F32)
        d = norm_back(res[m, rows, :], e, 1) + obuf[m, rows, :].astype(F32)
        acc_m[m, rows, :] = d
        dr[m, rows, :] = d.astype(BF)

    chunks(middle)
    own = dr.at[:, pl.ds(0, ROWS)]
    ds = [put(own, dr.at[:, pl.ds(ROWS, ROWS)], links.y), put(own, dr.at[:, pl.ds(2 * ROWS, ROWS)], links.core)]
    wo_in = [keep(wo_f.at[:, :, :, pl.ds(k * 256, 256)], wcol.at[k]) for k in range(2)]
    rows_near(0, out_terms, acc_o, ysend_o)
    rows_on(0, ysend_o)
    na_in = keep(na_h, cot)
    grad_near("gate", 2)
    pair_sum()
    arrived(ds[0])
    ds.append(put(dr.at[:, pl.ds(ROWS, ROWS)], dr.at[:, pl.ds(3 * ROWS, ROWS)], links.core))
    grad_near("gate", 1)
    kept(*wo_in)
    arrived(*ds)

    @pl.loop(0, 4)
    def _(i):
        m, rows = i // 2, pl.ds(pl.multiple_of(lax.rem(i, 2) * 256, 256), 256)
        for k in range(2):
            datt[m, rows, k * 256 : (k + 1) * 256] = nn(dr[m, rows, :], wcol[k].reshape(DM, 256)).astype(BF)

    def attend_back(m):
        kv = qkv[m, :, 512:640].astype(F32)
        lane = lax.broadcasted_iota(jnp.int32, (LEN4, 128), 1)
        half = lax.broadcasted_iota(jnp.int32, (256, 128), 1) < 64
        ka = jnp.where(lane < 64, kv, 0.0)
        vb = jnp.where(lane < 64, 0.0, kv)
        kb, va = pltpu.roll(ka, 64, 1), pltpu.roll(vb, 64, 1)
        heads = [
            (k.astype(BF), k.T.astype(BF), v.astype(BF), keep_lanes)
            for k, v, keep_lanes in ((ka, va, half), (kb, vb, jnp.logical_not(half)))
        ]
        dkacc[...] = jnp.zeros_like(dkacc)
        dvacc[...] = jnp.zeros_like(dvacc)

        @pl.loop(0, 8)
        def _(i):
            lanes = pl.ds(pl.multiple_of(i // 2 * 128, 128), 128)
            rows = pl.ds(pl.multiple_of(lax.rem(i, 2) * 256, 256), 256)
            q, do = qkv[m, rows, lanes], datt[m, rows, lanes]
            bias = mask_t[m, :, rows].astype(F32)
            dq_t = jnp.zeros((128, 256), F32)
            for k, k_t, v, keep_lanes in heads:
                s = nt(k, q) * 0.125 + bias
                e = jnp.exp(s - jnp.max(s, axis=0, keepdims=True))
                p = e * (1.0 / jnp.sum(e, axis=0, keepdims=True))
                d = nt(v, do)
                ds_ = (p * (d - jnp.sum(p * d, axis=0, keepdims=True)) * 0.125).astype(BF)
                dq_t = dq_t + nn(k_t, ds_)
                zero = jnp.zeros_like(q)
                dkacc[...] += nn(ds_, jnp.where(keep_lanes, q, zero))
                dvacc[...] += nn(p.astype(BF), jnp.where(keep_lanes, do, zero))
            dqkv[m, rows, lanes] = rope_tile(dq_t.T, table[0, rows, :], -table[1, rows, :]).astype(BF)

        dk = dkacc[...] + pltpu.roll(dkacc[...], 64, 1)
        dv = dvacc[...] + pltpu.roll(dvacc[...], 64, 1)
        dk = rope_tile(dk, table[0], -table[1])
        dqkv[m, :, 512:640] = jnp.where(lane < 64, dk, dv).astype(BF)

    grad_far("out")
    attend_back(0)
    grad_near("gate", 3)
    grad_near("gate", 0)
    grad_on("gate")
    attend_back(1)
    na_terms = [(dqkv, wqkv_f, 640)]
    rows_far(2, na_terms)
    kept(na_in)
    grad_far("qkv")
    rows_final(0)
    chunks(output_rows)
    for b in range(8):
        keep(obuf.at[:, :, pl.ds(b * 256, 256)], out_o.at[:, :, links.lanes(b)])
    sent(yid[1])
    rows_near(2, na_terms, acc_o, ysend)
    rows_on(2, ysend)
    grad_final("down")
    grad_near("up", 2)
    grad_near("up", 1)
    grad_near("up", 3)
    rows_final(2)
    own_x = far_st.at[:, pl.ds(ROWS, ROWS)]
    kept(*[keep(x_ref.at[:, :, links.lanes(b)], own_x.at[:, :, pl.ds(b * 256, 256)]) for b in range(8)])

    def last_rows(m, rows):
        e = acc_o[m, rows, :] + far_st[m, rows, :].astype(F32)
        v = own_x[m, rows, :].astype(F32)
        acc_m[m, rows, :] += norm_back(v, e, 0)

    chunks(last_rows)
    for b in range(8):
        keep(acc_m.at[:, :, pl.ds(b * 256, 256)], din_o.at[:, :, links.lanes(b)])
    gx = put(gacc.at[:, pl.ds(1024, 1024)], gxin, links.x)
    grad_near("up", 0)
    grad_on("up")
    grad_final("gate")
    for name in ("out", "qkv"):
        for r in ORDER:
            grad_near(name, r)
        if name == "out":
            grad_on(name)
    arrived(gx)
    gnear[...] = gacc[:, 0:1024] + gxin[...]
    gz = [put(gnear.at[:, pl.ds(r * 256, 256)], gzin.at[r - 1], links.z[r]) for r in (1, 2, 3)]
    grad_on("qkv")
    grad_final("up")
    arrived(*gz)
    gown[...] = gnear[:, 0:256] + gzin[0] + gzin[1] + gzin[2]
    gs = [put(gown, gsin.at[k], p) for k, p in enumerate((links.core, links.y, links.both))]
    grad_final("out")
    arrived(*gs)
    gain_o[...] = gown[...] + gsin[0] + gsin[1] + gsin[2]
    grad_final("qkv")
    for c in writing:
        c.wait()
    for name in relays:
        far_sent(name)
    links.finish()


def backward(seg, gain, table, x, arrays):
    micro, rows, d = x.shape
    sd = jax.ShapeDtypeStruct
    ff = arrays[-4].shape[2]
    v = pltpu.VMEM
    behind = ff - 640
    out_shape = [
        sd(x.shape, BF), sd(x.shape, F32), sd((8, 256), F32), sd((256, 640), F32), sd((256, 512), F32),
        sd((256, ff), F32), sd((256, ff), F32), sd((256, ff), F32), sd((3, 4, 256, ff), BF), sd((4, 256, 512), BF),
        sd((4, 256, 640), BF), sd((3, 4, 256, ff), BF), sd((4, 256, 512), BF), sd((4, 256, 640), BF),
        sd((3, 2, 256, d), BF), sd((3, 2, 128, d), BF), sd((2, 4, 256, behind), BF), sd((256, behind), BF),
    ]
    toks = (2, 512, d)
    scratch = [
        v(toks, BF), v(toks, BF), v(toks, BF), v((2, 512, ff), BF), v((2, 512, ff), BF), v((3, 4, 256, ff), BF),
        v((4, 256, 1152), BF), v((3, 256, ff), BF), v((256, ff), F32), v((2, 2, 4, 256, 256), BF), v((2, 2, 256, ff), BF),
        v((2, 256, d), BF), v((2, 256, d), BF), v((2, 128, d), BF), v((2, 128, d), BF), v((2, 128, d), F32), v((2, 128, d), F32),
        v((2, 128, d), F32), v((2, 512, 640), BF), v((2, 512, 512), BF), v((2, 512, 512), BF), v((2, 512, 640), BF),
        v((2, 128, d), BF), v((512, 128), F32), v((512, 128), F32), v((8, d), F32), v((8, 1024), F32),
        v((8, 1024), F32), v((3, 8, 256), F32), v((8, 256), F32), v((3, 8, 256), F32),
        v((4, 512, 128), F32), v((2, 512, 512), BF), v((8, 512), F32),
        pltpu.SemaphoreType.DMA((80,)), pltpu.SemaphoreType.DMA((80,)), pltpu.SemaphoreType.DMA((64,)),
        pltpu.SemaphoreType.DMA((2,)), pltpu.SemaphoreType.DMA((2, 2)), pltpu.SemaphoreType.DMA((3,)),
        pltpu.SemaphoreType.DMA((1,)),
    ]
    return pl.pallas_call(
        backward_kernel,
        out_shape=out_shape,
        in_specs=[VMEM] * 2 + [HBM] * (2 + len(arrays)),
        out_specs=[HBM] * 2 + [VMEM] + [HBM] * 15,
        scratch_shapes=scratch,
        compiler_params=pltpu.CompilerParams(collective_id=1, has_side_effects=True, vmem_limit_bytes=LIMIT_B),
    )(seg, gain, table, x, *arrays)


def rope_table():
    frequency = THETA ** (-(np.arange(HD // 2) * (2.0 / HD)))
    angles = np.arange(LEN4)[:, None] * frequency[None, :]
    cosine, sine = np.cos(angles), np.sin(angles)
    c4 = np.tile(cosine, (1, 4))
    s4 = np.concatenate([-sine, sine, -sine, sine], axis=1)
    one, zero = np.ones((LEN4, HD)), np.zeros((LEN4, HD))
    ck, sk = np.concatenate([c4[:, :HD], one], axis=1), np.concatenate([s4[:, :HD], zero], axis=1)
    return np.stack([c4, s4, ck, sk]).astype(np.float32)


def per_device_grid(
    inputs, segments, cotangent, attn_gain, w_query, w_key, w_value, w_out, mlp_gain, w_gate, w_up, w_down,
):
    nq, nk = w_query.shape[1], w_key.shape[1]
    w_qkv = jnp.concatenate([w_query, w_key, w_value], axis=1)
    me = lax.axis_index("seq")
    size = attn_gain.shape[0]
    row = lax.broadcasted_iota(jnp.int32, (8, 4 * size), 0)
    lane = lax.broadcasted_iota(jnp.int32, (8, 4 * size), 1)
    g = jnp.where(row == 0, jnp.tile(attn_gain, 4)[None].astype(F32), jnp.tile(mlp_gain, 4)[None].astype(F32))
    g = jnp.where(jnp.logical_and(row < 2, lane // size == me), g, 0.0)
    table = jnp.asarray(rope_table())
    made = forward(inputs, cotangent, g, segments, table, [w_qkv, w_out, w_gate, w_up, w_down])
    c_full, wqkv, wo, wg, wu, wd, na, qkv, att, res, nm, gain, prod, fa, fb, down = made
    arrays = [c_full, wqkv, wo, wg, wu, wd, na, qkv, att, res, nm, prod, fa, fb, down]
    back = backward(segments, gain, table, inputs, arrays)
    output, d_input, gains, gq, go, gg, gu, gd = back[:8]
    gains = lax.dynamic_slice_in_dim(gains, me * size, size, 1)
    return (
        output, d_input, gains[0], gq[:, :nq], gq[:, nq : nq + nk], gq[:, nq + nk :], go, gains[1], gg, gu, gd,
    )


class AnyMesh:
    def gather(self, x, c, shards):
        fulls = [lax.all_gather(w, "dp", axis=0, tiled=True) for w in shards]
        return gather_rows(x), gather_rows(c), fulls

    def gather_gains(self, g):
        return lax.all_gather(g, ("dp", "seq"), axis=1, tiled=True)

    def scatter_gain(self, g):
        return lax.psum_scatter(g, ("dp", "seq"), scatter_dimension=0, tiled=True)

    def scatter(self, left, right):
        return lax.psum_scatter(
            outer_sum(left, right).astype(BF), "dp", scatter_dimension=0, tiled=True
        ).astype(F32)

    def to_relative(self, a):
        return a

    def from_relative(self, a):
        return a


def shift_core(a):
    return lax.ppermute(a, "seq", [(i, i ^ 1) for i in range(4)])


def shift_y(a):
    return lax.ppermute(a, "seq", [(i, i ^ 2) for i in range(4)])


def gather_rows(a):
    across = shift_y(a)
    return jnp.concatenate([a, across, shift_core(a), shift_core(across)], axis=-2)


def scatter_rows(make):
    got = shift_core(make(1).astype(BF))
    near = make(0) + got.astype(F32)
    rows = near.shape[1] // 2
    got = shift_y(near[:, rows:].astype(BF))
    return near[:, :rows] + got.astype(F32)


def per_device(
    inputs, segments, cotangent, attn_gain, w_query, w_key, w_value, w_out, mlp_gain, w_gate, w_up, w_down,
):
    micro, rows, d = inputs.shape
    seq = lax.axis_size("seq")
    length = rows * seq
    full = micro * length
    half = length // 2
    grid = AnyMesh()

    nq, nk = w_query.shape[1], w_key.shape[1]
    heads, kv_heads = nq // HD, nk // HD
    groups = heads // kv_heads
    w_qkv = jnp.concatenate([w_query, w_key, w_value], axis=1)

    inputs = grid.to_relative(inputs)
    cotangent = grid.to_relative(cotangent)
    gains = grid.gather_gains(jnp.stack([attn_gain, mlp_gain]).astype(F32))
    gain_a, gain_m = gains[0], gains[1]

    shards = [w_qkv, w_out, w_gate, w_up, w_down]
    x_full, up_full, (wqkv, wo, wg, wu, wd) = grid.gather(inputs, cotangent, shards)

    me = lax.axis_index("seq")
    order = [me, me ^ 2, me ^ 1, me ^ 3]
    pos = jnp.concatenate([j * rows + jnp.arange(rows, dtype=jnp.int32) for j in order])
    segs = jnp.concatenate([lax.dynamic_slice_in_dim(segments, j * rows, rows, 1) for j in order], axis=1)
    cosine, sine = rope_tables(pos)
    cos_f, sin_f = jnp.tile(cosine, (micro, 1)), jnp.tile(sine, (micro, 1))
    allowed = (pos[None, :] <= pos[:, None])[None] & (segs[:, :, None] == segs[:, None, :])
    allowed = allowed[:, None, None]

    def pieces(make):
        return lambda i: make(slice(i * half, (i + 1) * half)).reshape(micro, half, d)

    def rows_of(a, s):
        return a.reshape(micro, length, -1)[:, s].reshape(micro * half, -1)

    hidden_full = x_full.reshape(full, d).astype(F32)
    normed, inverse_f = normalize(hidden_full, gain_a)
    na = normed.astype(BF)
    hidden = inputs.astype(F32)
    upstream = cotangent.astype(F32)
    up_full = up_full.reshape(full, d)

    def rope(x, n, s):
        return rotate(x.reshape(full, n, HD), cos_f, s).astype(BF).reshape(full, n * HD)

    qkv = project(na, wqkv)
    q = rope(qkv[:, :nq], heads, sin_f)
    k = rope(qkv[:, nq : nq + nk], kv_heads, sin_f)
    v = qkv[:, nq + nk :].astype(BF)
    qg = q.reshape(micro, length, kv_heads, groups, HD)
    kg = k.reshape(micro, length, kv_heads, HD)
    vg = v.reshape(micro, length, kv_heads, HD)
    scores = jnp.einsum("mqkgd,mpkd->mkgqp", qg, kg, preferred_element_type=F32) * HD ** (-0.5)
    scores = jnp.where(allowed, scores, NEGATIVE)
    maximum = jnp.max(scores, axis=-1, keepdims=True)
    weights = jnp.where(allowed, jnp.exp(scores - maximum), 0.0)
    denominator = jnp.sum(weights, axis=-1, keepdims=True)
    prob = weights / denominator
    prob_b = prob.astype(BF)
    attended = jnp.einsum("mkgqp,mpkd->mqkgd", prob_b, vg, preferred_element_type=F32)
    attended = attended.astype(BF).reshape(full, heads * HD)
    residual = hidden + scatter_rows(pieces(lambda s: project_back(rows_of(attended, s), wo)))
    normed, inverse_m = normalize(residual, gain_m)
    nm = gather_rows(normed.astype(BF)).reshape(full, d)
    gate_pre = project(nm, wg)
    up_proj = project(nm, wu)
    sigmoid_g = jax.nn.sigmoid(gate_pre)
    active = gate_pre * sigmoid_g
    product = (active * up_proj).astype(BF)
    g_down = grid.scatter(up_full, product)
    d_product = project(up_full, wd)
    d_gate = (d_product * up_proj * sigmoid_g * (1.0 + gate_pre * (1.0 - sigmoid_g))).astype(BF)
    d_up = (d_product * active).astype(BF)
    d_nm = scatter_rows(
        pieces(lambda s: project_back(rows_of(d_gate, s), wg) + project_back(rows_of(d_up, s), wu))
    )
    g_gate = grid.scatter(nm, d_gate)
    g_up = grid.scatter(nm, d_up)
    output = (residual + scatter_rows(pieces(lambda s: project_back(rows_of(product, s), wd)))).astype(BF)
    flat = lambda a: a.reshape(micro * rows, -1)
    d_norm_m, g_gain_m = normalize_back(flat(residual), flat(inverse_m), gain_m, flat(d_nm))
    d_residual = upstream + d_norm_m.reshape(micro, rows, d)
    dr = gather_rows(d_residual.astype(BF)).reshape(full, d)
    d_att = project(dr, wo).astype(BF)
    dg = d_att.reshape(micro, length, kv_heads, groups, HD)
    d_values = jnp.einsum("mkgqp,mqkgd->mpkd", prob_b, dg, preferred_element_type=F32)
    d_prob = jnp.einsum("mqkgd,mpkd->mkgqp", dg, vg, preferred_element_type=F32)
    row_sum = jnp.sum(prob * d_prob, axis=-1, keepdims=True)
    d_scores = (prob * (d_prob - row_sum) * HD ** (-0.5)).astype(BF)
    d_query = jnp.einsum("mkgqp,mpkd->mqkgd", d_scores, kg, preferred_element_type=F32)
    d_keys = jnp.einsum("mkgqp,mqkgd->mpkd", d_scores, qg, preferred_element_type=F32)
    dq = rope(d_query, heads, -sin_f)
    dk = rope(d_keys, kv_heads, -sin_f)
    dv = d_values.astype(BF).reshape(full, kv_heads * HD)
    dqkv = jnp.concatenate([dq, dk, dv], axis=1)
    g_out = grid.scatter(dr, attended)
    d_na = scatter_rows(pieces(lambda s: project_back(rows_of(dqkv, s), wqkv)))
    g_qkv = grid.scatter(na, dqkv)
    inverse_a = inverse_f.reshape(micro, length, 1)[:, :rows]
    d_norm_a, g_gain_a = normalize_back(flat(hidden), flat(inverse_a), gain_a, flat(d_na))
    d_input = d_residual + d_norm_a.reshape(micro, rows, d)
    return (
        grid.from_relative(output),
        grid.from_relative(d_input),
        grid.scatter_gain(g_gain_a),
        g_qkv[:, :nq],
        g_qkv[:, nq : nq + nk],
        g_qkv[:, nq + nk :],
        g_out,
        grid.scatter_gain(g_gain_m),
        g_gate,
        g_up,
        g_down,
    )


def solution(mesh):
    tok, wt, gn = P(None, ("dp", "seq"), None), P("dp", "seq"), P(("dp", "seq"))
    grid = mesh.shape["dp"] == 8 and mesh.shape["seq"] == 4
    return jax.shard_map(
        per_device_grid if grid else per_device,
        mesh=mesh,
        in_specs=(tok, P(None, "dp"), tok, gn, wt, wt, wt, wt, gn, wt, wt, wt),
        out_specs=(tok, tok, gn, wt, wt, wt, wt, gn, wt, wt, wt),
        check_vma=False,
    )
```

```python
import jax
import jax.numpy as jnp
import numpy as np
from jax import lax
from jax.experimental import pallas as pl
from jax.experimental.pallas import tpu as pltpu
from jax.sharding import PartitionSpec as P

HD = 64
EPS = 1e-05
THETA = 10000.0
NEGATIVE = -1e30
BF = jnp.bfloat16
F32 = jnp.float32


def rope_tables(positions):
    half_dim = HD // 2
    frequency = THETA ** (-(jnp.arange(half_dim).astype(F32) * (2.0 / HD)))
    angles = positions.astype(F32)[:, None] * frequency[None, :]
    return (jnp.cos(angles), jnp.sin(angles))


def rotate(values, cosine, sine_table):
    half_dim = values.shape[-1] // 2
    c = cosine[:, None, :]
    s = sine_table[:, None, :]
    a = values[..., :half_dim]
    b = values[..., half_dim:]
    return jnp.concatenate([a * c - b * s, b * c + a * s], axis=-1)


def unrotate(gradient, cosine, sine_table):
    return rotate(gradient, cosine, -sine_table)


def normalize(hidden, gain_vec):
    inverse = lax.rsqrt(jnp.mean(hidden * hidden, axis=-1, keepdims=True) + EPS)
    return (hidden * inverse * gain_vec, inverse)


def normalize_back(hidden, inverse, gain_vec, gradient):
    unit_rows = hidden * inverse
    gain_grad = jnp.sum(gradient * unit_rows, axis=0)
    weighted = gradient * gain_vec
    return (
        inverse * (weighted - unit_rows * jnp.mean(weighted * unit_rows, axis=-1, keepdims=True)),
        gain_grad,
    )


def project(a, b):
    return jnp.dot(a, b, preferred_element_type=F32)


def project_back(a, b):
    return lax.dot_general(a, b, (((1,), (1,)), ((), ())), preferred_element_type=F32)


def outer_sum(a, b):
    return lax.dot_general(a, b, (((0,), (0,)), ((), ())), preferred_element_type=F32)


MESH_ID = pl.DeviceIdType.MESH
HBM = pl.BlockSpec(memory_space=pl.ANY)
VMEM = pl.BlockSpec(memory_space=pltpu.VMEM)
ROWS = 128
LEN4 = 512
HALF = 256
DM = 2048
LIMIT = 60 * 1024 * 1024
LIMIT_B = 62 * 1024 * 1024


def nt(a, b):
    return lax.dot_general(a, b, (((1,), (1,)), ((), ())), preferred_element_type=F32)


def tn(a, b):
    return lax.dot_general(a, b, (((0,), (0,)), ((), ())), preferred_element_type=F32)


def nn(a, b):
    return jnp.dot(a, b, preferred_element_type=F32)


class Links:
    def __init__(self, send, recv, local):
        self.send, self.recv, self.local = send, recv, local
        self.remote, self.own = [], []
        self.seen, self.gone, self.middle_only = set(), set(), set()
        dp, sq = lax.axis_index("dp"), lax.axis_index("seq")
        self.dp, self.sq = dp, sq
        height = lax.div(dp, 2)
        self.middle = jnp.logical_and(height >= 1, height <= 2)
        self.low = height <= 1
        self.z = [(lax.rem(dp + 2 * r, 8), sq) for r in range(4)]
        self.x = (dp + 1 - 2 * lax.rem(dp, 2), sq)
        core = sq + 1 - 2 * lax.rem(sq, 2)
        self.core = (dp, core)
        self.y = (dp, lax.rem(sq + 2, 4))
        self.both = (dp, lax.rem(core + 2, 4))
        peers = self.z[1:] + [self.x, self.core, self.y, self.both]
        barrier = pltpu.get_barrier_semaphore()
        for peer in peers:
            pl.semaphore_signal(barrier, inc=1, device_id=peer, device_id_type=MESH_ID)
        pl.semaphore_wait(barrier, len(peers))

    def lanes(self, b):
        z, x = lax.div(self.dp, 2), lax.rem(self.dp, 2)
        at = lax.rem(z + b % 4, 4) * 2 + (x if b < 4 else 1 - x)
        return pl.ds(pl.multiple_of(at * 256, 256), 256)

    def order(self, k):
        return (self.sq, self.y[1], self.core[1], self.both[1])[k]

    def describe(self, src, dst, peer, landing=None):
        i = len(self.remote)
        copy = pltpu.make_async_remote_copy(
            src_ref=src,
            dst_ref=dst,
            send_sem=self.send.at[i],
            recv_sem=self.recv.at[i if landing is None else landing],
            device_id=peer,
            device_id_type=MESH_ID,
        )
        self.remote.append(copy)
        return i

    def put(self, src, dst, peer):
        i = self.describe(src, dst, peer)
        self.remote[i].start()
        return i

    def start_in_middle(self, i):
        self.middle_only.add(i)
        pl.when(self.middle)(self.remote[i].start)

    def arrived(self, *ids):
        for i in ids:
            if i not in self.seen:
                self.seen.add(i)
                self.remote[i].wait_recv()

    def sent(self, *ids):
        for i in ids:
            if i not in self.gone:
                self.gone.add(i)
                if i in self.middle_only:
                    pl.when(self.middle)(self.remote[i].wait_send)
                else:
                    self.remote[i].wait_send()

    def keep(self, src, dst):
        copy = pltpu.make_async_copy(src, dst, self.local.at[len(self.own)])
        copy.start()
        self.own.append([copy, False])
        return len(self.own) - 1

    def kept(self, *ids):
        for i in ids:
            if not self.own[i][1]:
                self.own[i][1] = True
                self.own[i][0].wait()

    def finish(self):
        self.sent(*range(len(self.remote)))
        self.arrived(*range(len(self.remote)))
        self.kept(*range(len(self.own)))


def load_table(links, table_h, table):
    return [
        links.keep(
            table_h.at[:, pl.ds(pl.multiple_of(links.order(k) * ROWS, ROWS), ROWS)],
            table.at[:, pl.ds(k * ROWS, ROWS)],
        )
        for k in range(4)
    ]


def make_mask(links, seg, keys, mask, by_key):
    for k in range(4):
        at = pl.ds(k * ROWS, ROWS)
        place = links.order(k) * ROWS
        keys[0:2, at] = seg[:, pl.ds(pl.multiple_of(place, ROWS), ROWS)].astype(F32)
        keys[2:3, at] = (lax.broadcasted_iota(jnp.int32, (1, ROWS), 1) + place).astype(F32)
    columns = keys[...].T
    for m in range(2):
        for k in range(4):
            at = slice(k * ROWS, (k + 1) * ROWS)
            same = columns[at, m : m + 1] == keys[m : m + 1, :]
            a, b = columns[at, 2:3], keys[2:3, :]
            ahead = (a <= b) if by_key else (b <= a)
            mask[m, at, :] = jnp.where(jnp.logical_and(same, ahead), 0.0, NEGATIVE).astype(BF)


def rope_tile(t, cosine, sine):
    lane = lax.broadcasted_iota(jnp.int32, t.shape, 1)
    turned = jnp.where(lax.rem(lane, 64) < 32, pltpu.roll(t, 96, 1), pltpu.roll(t, 32, 1))
    return t * cosine + turned * sine


def forward_kernel(
    x_ref, c_ref, g_ref, seg, table_h, wqkv_s, wo_s, wg_s, wu_s, wd_s,
    c_full, wqkv_f, wo_f, wg_f, wu_f, wd_f, na_o, qkv_o, att_o, res_o, nm_o, gain_o, prod_o, fa_o, fb_o, down_o,
    xf, nm, wqkv_v, wo_v, qkv, att, far, far_in, near, ysend, yin, own_x, gseq, gfull, gown, prod, fa, fb, wt, lbuf, gbuf, table, mask, keys,
    send, recv, local, wsem, lsem, gsem,
):
    links = Links(send, recv, local)
    put, arrived = links.put, links.arrived
    first, rest = pl.ds(0, 768), pl.ds(768, wg_s.shape[1] - 768)
    sixth, seventh = pl.ds(0, 640), pl.ds(640, wd_s.shape[1] - 640)
    shards = [wqkv_s, wo_s] + [w.at[:, s] for s in (first, rest) for w in (wg_s, wu_s)]
    fulls = [wqkv_f, wo_f] + [w.at[:, :, :, s] for s in (first, rest) for w in (wg_f, wu_f)]
    shards += [wd_s.at[:, sixth], wd_s.at[:, seventh]]
    fulls += [wd_f.at[:, :, :, sixth], wd_f.at[:, :, :, seventh]]

    def part(full, k):
        return full.at[:, pl.ds(k * ROWS, ROWS)]

    def seq_start(src, full):
        return [put(src, part(full, 1), links.y), put(src, part(full, 2), links.core)]

    def seq_forward(full, ids):
        arrived(ids[0])
        ids.append(put(part(full, 1), part(full, 3), links.core))

    placed = []

    def z_start(i):
        placed.append(links.keep(shards[i], fulls[i].at[0, 0]))
        return {r: put(shards[i], fulls[i].at[0, r], links.z[4 - r]) for r in (1, 3)}

    def x_own(i):
        return [put(shards[i], fulls[i].at[1, 0], links.x)]

    def relays(full, rx, copies):
        copies[2] = links.describe(full.at[rx, 1], full.at[rx, 2], links.z[3])
        other = links.describe(full.at[rx, 3], full.at[rx, 2], links.z[1], copies[2])
        links.seen.add(other)
        return {1: copies[2], 3: other}

    def x_near(i, copies, ids):
        full = fulls[i]
        relay = relays(full, 0, copies)
        for r in (1, 3):
            arrived(copies[r])
            links.start_in_middle(relay[r])
            ids.append(put(full.at[0, r], full.at[1, r], links.x))

    def pair_start(i, ids):
        full = fulls[i]
        placed.append(links.keep(shards[i], full.at[0, 0]))
        arrived(*ids)
        return [
            {r: put(src, full.at[rx, r], links.z[4 - r]) for r in (1, 3)}
            for rx, src in enumerate((shards[i], full.at[1, 0]))
        ]

    def pair_on(i, pair):
        for rx, copies in enumerate(pair):
            relay = relays(fulls[i], rx, copies)
            for r in (1, 3):
                arrived(copies[r])
                links.start_in_middle(relay[r])

    def x_far(i, copies, ids):
        arrived(copies[2])
        ids.append(put(fulls[i].at[0, 2], fulls[i].at[1, 2], links.x))

    placing = [links.keep(x_ref.at[:, :, links.lanes(b)], xf.at[:, pl.ds(0, ROWS), pl.ds(b * 256, 256)]) for b in range(8)]
    c_own = [links.keep(c_ref.at[:, :, links.lanes(b)], c_full.at[:, pl.ds(0, ROWS), pl.ds(b * 256, 256)]) for b in range(8)]
    table_in = load_table(links, table_h, table)
    gs = [put(g_ref, gseq.at[k], p) for k, p in ((1, links.core), (2, links.y), (3, links.both))]
    zs, xd = {}, {}

    def start(i):
        zs[i] = z_start(i)

    def across(i):
        xd[i] = x_own(i)

    def near_blocks(i):
        x_near(i, zs[i], xd[i])

    def far_block(i):
        x_far(i, zs[i], xd[i])

    start(0)
    across(0)
    links.kept(*placing)
    xs = seq_start(part(xf, 0), xf)
    own1 = links.keep(part(xf, 0), own_x)
    arrived(*gs)
    gown[...] = g_ref[...] + gseq[1] + gseq[2] + gseq[3]
    gfull[0, 0] = gown[...]
    gz = [put(gown, gfull.at[0, r], links.z[4 - r]) for r in (1, 2, 3)]
    gx = [put(gown, gfull.at[1, 0], links.x)]
    start(1)
    near_blocks(0)
    make_mask(links, seg, keys, mask, False)
    links.kept(*table_in)
    for r in (1, 2, 3):
        arrived(gz[r - 1])
        gx.append(put(gfull.at[0, r], gfull.at[1, r], links.x))
    far_block(0)
    across(1)
    start(2)
    seq_forward(xf, xs)
    arrived(*gx)
    for b in range(8):
        gain_o[:, b * 256 : (b + 1) * 256] = gfull[b // 4, b % 4]
    arrived(*xs)
    links.sent(*xs)
    links.kept(own1)

    @pl.loop(0, 16)
    def _(i):
        m, r = i // 8, pl.multiple_of(lax.rem(i, 8) * 64, 64)
        v = xf[m, pl.ds(r, 64), :].astype(F32)
        inverse = lax.rsqrt(jnp.mean(v * v, axis=-1, keepdims=True) + EPS)
        xf[m, pl.ds(r, 64), :] = (v * inverse * gain_o[0:1, :]).astype(BF)

    na_copy = links.keep(xf, na_o)
    near_blocks(1)
    arrived(*xd[0])
    links.kept(placed[0])
    load0 = links.keep(wqkv_f, wqkv_v)
    links.kept(load0)

    @pl.loop(0, 4)
    def _(i):
        m, r = i // 2, pl.multiple_of(lax.rem(i, 2) * 256, 256)
        rows = pl.ds(r, 256)
        a = xf[m, rows, :]
        cq, sq = table[0, rows, :], table[1, rows, :]
        for n in range(2):
            t = nn(a, wqkv_v[:, :, :, n * 256 : (n + 1) * 256].reshape(DM, 256))
            for j in range(2):
                lanes = slice(n * 256 + j * 128, n * 256 + (j + 1) * 128)
                qkv[m, rows, lanes] = rope_tile(t[:, j * 128 : (j + 1) * 128], cq, sq).astype(BF)
        t = nn(a, wqkv_v[:, :, :, 512:640].reshape(DM, 128))
        qkv[m, rows, 512:640] = rope_tile(t, table[2, rows, :], table[3, rows, :]).astype(BF)

    links.keep(qkv, qkv_o)
    far_block(1)
    across(2)
    start(3)
    across(3)

    def attend(m):
        kv = qkv[m, :, 512:640].astype(F32)
        lane = lax.broadcasted_iota(jnp.int32, (LEN4, 128), 1)
        ka = jnp.where(lane < 64, kv, 0.0)
        vb = jnp.where(lane < 64, 0.0, kv)
        ka = ka * 0.125
        ks = [ka.astype(BF), pltpu.roll(ka, 64, 1).astype(BF)]
        vs = [pltpu.roll(vb, 64, 1).astype(BF), vb.astype(BF)]

        @pl.loop(0, 8)
        def _(i):
            lanes = pl.ds(pl.multiple_of(i // 2 * 128, 128), 128)
            rows = pl.ds(pl.multiple_of(lax.rem(i, 2) * 256, 256), 256)
            q = qkv[m, rows, lanes]
            bias = mask[m, rows, :].astype(F32)
            out = jnp.zeros((256, 128), F32)
            for k, v in zip(ks, vs):
                s = nt(q, k) + bias
                e = jnp.exp(s - jnp.max(s, axis=-1, keepdims=True))
                p = (e * (1.0 / jnp.sum(e, axis=-1, keepdims=True))).astype(BF)
                out = out + nn(p, v)
            att[m, rows, lanes] = out.astype(BF)

    attend(0)
    near_blocks(2)
    start(4)
    attend(1)
    far_block(2)
    links.keep(att, att_o)
    arrived(*xd[1])
    links.kept(placed[1])
    load1 = links.keep(wo_f, wo_v)
    links.kept(load1)

    def out_rows(m, row, dst, dtype):
        @pl.loop(0, 8)
        def _(n):
            w = wo_v[n // 4, lax.rem(n, 4)]
            lanes = pl.ds(pl.multiple_of(n * 256, 256), 256)
            dst[m, :, lanes] = nt(att[m, row : row + HALF, :], w).astype(dtype)

    for m in range(2):
        out_rows(m, HALF, far, BF)
    fc = put(far, far_in, links.core)
    near_blocks(3)
    for m in range(2):
        out_rows(m, 0, near, F32)
    arrived(fc)

    @pl.loop(0, 4)
    def _(i):
        m, r = i // 2, pl.multiple_of(lax.rem(i, 2) * 64, 64)
        rows = pl.ds(r + ROWS, 64)
        ysend[m, pl.ds(r, 64), :] = (near[m, rows, :] + far_in[m, rows, :].astype(F32)).astype(BF)

    yc = put(ysend, yin, links.y)
    far_block(3)
    across(4)
    start(5)
    across(5)
    across(7)
    arrived(yc)

    @pl.loop(0, 4)
    def _(i):
        m, r = i // 2, pl.multiple_of(lax.rem(i, 2) * 64, 64)
        rows = pl.ds(r, 64)
        v = near[m, rows, :] + far_in[m, rows, :].astype(F32) + yin[m, rows, :].astype(F32) + own_x[m, rows, :].astype(F32)
        res_o[m, rows, :] = v
        inverse = lax.rsqrt(jnp.mean(v * v, axis=-1, keepdims=True) + EPS)
        nm[m, rows, :] = (v * inverse * gain_o[1:2, :]).astype(BF)

    ns = seq_start(part(nm, 0), nm)
    near_blocks(4)
    far_block(4)
    start(6)
    seq_forward(nm, ns)
    links.kept(*c_own)
    cs = seq_start(part(c_full, 0), c_full)
    arrived(*ns)
    links.keep(nm, nm_o)
    arrived(*xd[2], *xd[3])
    links.kept(placed[2], placed[3])

    def load(t, slot):
        lanes = pl.ds(pl.multiple_of(t * 128, 128), 128)
        return [
            pltpu.make_async_copy(w.at[:, :, :, lanes], wt.at[slot, :, :, :, pl.ds(k * 128, 128)], wsem.at[slot, k])
            for k, w in enumerate((wg_f, wu_f))
        ]

    def up_tile(t, slot):
        lanes = pl.ds(pl.multiple_of(t * 128, 128), 128)

        @pl.loop(0, 2)
        def _(m):
            r = nn(nm[m], wt[slot].reshape(DM, 256))
            g, u = r[:, :128], r[:, 128:]
            s = jax.nn.sigmoid(g)
            active = g * s
            prod[m, :, lanes] = (active * u).astype(BF)
            fa[m, :, lanes] = (u * s * (1.0 + g * (1.0 - s))).astype(BF)
            fb[m, :, lanes] = active.astype(BF)

    for c in load(0, 0):
        c.start()
    tiles = wg_s.shape[1] // 128

    def tile_step(t):
        slot = lax.rem(t, 2)

        @pl.when(t + 1 < tiles)
        def _():
            for c in load(t + 1, 1 - slot):
                c.start()

        for c in load(t, slot):
            c.wait()
        up_tile(t, slot)

    pl.loop(0, 3)(tile_step)
    near_blocks(5)
    far_block(5)
    across(6)
    pair = pair_start(7, xd[7])
    pl.loop(3, 5)(tile_step)
    near_blocks(6)
    seq_forward(c_full, cs)
    arrived(*xd[4], *xd[5])
    links.kept(placed[4], placed[5])
    far_block(6)
    pl.loop(5, tiles)(tile_step)
    pair_on(7, pair)
    links.keep(prod, prod_o)
    links.keep(fa, fa_o)
    links.keep(fb, fb_o)
    arrived(*cs)

    def load_left(b, slot):
        lanes = pl.ds(pl.multiple_of(b * 256, 256), 256)
        return pltpu.make_async_copy(c_full.at[:, :, lanes], lbuf.at[slot], lsem.at[slot])

    def store_grad(b, slot):
        return pltpu.make_async_copy(gbuf.at[slot], down_o.at[b // 4, lax.rem(b, 4)], gsem.at[slot])

    load_left(0, 0).start()

    @pl.loop(0, 8)
    def _(b):
        slot = lax.rem(b, 2)

        @pl.when(b + 1 < 8)
        def _():
            load_left(b + 1, 1 - slot).start()

        load_left(b, slot).wait()

        @pl.when(b >= 2)
        def _():
            store_grad(b - 2, slot).wait()

        gbuf[slot] = (tn(lbuf[slot, 0], prod[0]) + tn(lbuf[slot, 1], prod[1])).astype(BF)
        store_grad(b, slot).start()

    store_grad(6, 0).wait()
    store_grad(7, 1).wait()
    links.finish()


def forward(x, c, g, seg, table, shards):
    micro, rows, d = x.shape
    sd = jax.ShapeDtypeStruct
    toks = (micro, 4 * rows, d)
    nq, nf = shards[1].shape[1], shards[2].shape[1]
    fulls = [sd((2, 4) + w.shape, BF) for w in shards]
    ffn = sd((micro, 4 * rows, nf), BF)
    out_shape = [sd(toks, BF)] + fulls + [
        sd(toks, BF), sd((micro, 4 * rows, 640), BF), sd((micro, 4 * rows, nq), BF),
        sd((micro, rows, d), F32), sd(toks, BF), sd((8, d), F32), ffn, ffn, ffn, sd((2, 4, 256, nf), BF),
    ]
    v = pltpu.VMEM
    scratch = [
        v(toks, BF), v(toks, BF), v((2, 4, 256, 640), BF), v((2, 4, 256, 512), BF), v((2, 512, 640), BF),
        v((2, 512, 512), BF), v((2, 256, d), BF), v((2, 256, d), BF), v((2, 256, d), F32), v((2, 128, d), BF),
        v((2, 128, d), BF), v((2, 128, d), BF), v((4, 8, 256), F32), v((2, 4, 8, 256), F32), v((8, 256), F32),
        v((2, 512, nf), BF), v((2, 512, nf), BF), v((2, 512, nf), BF), v((2, 2, 4, 256, 256), BF), v((2, 2, 512, 256), BF), v((2, 256, nf), BF),
        v((4, 512, 128), F32), v((2, 512, 512), BF), v((8, 512), F32),
        pltpu.SemaphoreType.DMA((96,)), pltpu.SemaphoreType.DMA((96,)), pltpu.SemaphoreType.DMA((56,)),
        pltpu.SemaphoreType.DMA((2, 2)), pltpu.SemaphoreType.DMA((2,)), pltpu.SemaphoreType.DMA((2,)),
    ]
    return pl.pallas_call(
        forward_kernel,
        out_shape=out_shape,
        in_specs=[HBM, HBM, VMEM, VMEM, HBM] + [HBM] * 5,
        out_specs=[HBM] * 9 + [VMEM, HBM, VMEM] + [HBM] * 4,
        scratch_shapes=scratch,
        compiler_params=pltpu.CompilerParams(collective_id=0, has_side_effects=True, vmem_limit_bytes=LIMIT),
    )(x, c, g, seg, table, *shards)


ORDER = (2, 1, 3, 0)


def backward_kernel(
    seg, gain, table_h, x_ref, c_full, wqkv_f, wo_f, wg_f, wu_f, wd_f, na_h, qkv_h, att_h, res_h, nm_h, prod_h, fa_h,
    fb_h, down_h,
    out_o, din_o, gain_o, gq_o, go_o, gg_o, gu_o, gd_o, xin_f, xin_o, xin_q, zin_f, zin_o, zin_q, fin, yin, pin, pxin,
    cot, nm, dr, dg, du, grads, grads_a, stage, ostage, wcol, wrow, far, far_st, ysend, ysend_o, acc_m, acc_o, res, qkv, att, datt, dqkv,
    obuf, dkacc, dvacc, gacc, gxin, gnear, gzin, gown, gsin, table, mask_t, keys,
    send, recv, local, csem, rsem, ssem, osem,
):
    links = Links(send, recv, local)
    put, arrived, sent, keep, kept = links.put, links.arrived, links.sent, links.keep, links.kept
    ff = fa_h.shape[2]
    prod = cot.at[:, :, pl.ds(0, ff)]

    def wide(k):
        return lambda r: grads.at[k, r]

    def cut(start, width):
        return lambda r: grads_a.at[r, :, pl.ds(start, width)]

    ahead = 640
    behind = ff - ahead
    low_lanes, high_lanes = pl.ds(0, ahead), pl.ds(ahead, behind)

    def down_block(r):
        return grads.at[0, r, :, low_lanes]

    spec = {
        "down": (None, None, down_block, xin_f.at[0, :, :, low_lanes], zin_f.at[0, :, :, low_lanes], ahead, gd_o),
        "gate": (nm, dg, wide(1), xin_f.at[1], zin_f.at[1], ff, gg_o),
        "up": (nm, du, wide(2), xin_f.at[2], zin_f.at[2], ff, gu_o),
        "out": (dr, att, cut(0, 512), xin_o, zin_o, 512, go_o),
        "qkv": (cot, dqkv, cut(512, 640), xin_q, zin_q, 640, gq_o),
    }
    relays, pairs = {}, []
    xid = {name: {} for name in spec}
    zid = {name: {} for name in spec}

    def block_of(name, b):
        left, right = spec[name][:2]
        lanes = pl.ds(b * 256, 256)
        return tn(left[0, :, lanes], right[0]) + tn(left[1, :, lanes], right[1])

    def two_away(name, src, zland):
        low = links.describe(src, zland.at[2], links.z[1])
        high = links.describe(src, zland.at[3], links.z[3])
        pl.when(links.low)(links.remote[low].start)
        pl.when(jnp.logical_not(links.low))(links.remote[high].start)
        links.seen.update((low, high))
        links.gone.update((low, high))
        relays[name] = (low, high)

    def pair_start():
        for rx in range(2):
            two_away(("pair", rx), down_h.at[rx, 2, :, high_lanes], pin.at[rx])

    def pair_on():
        for rx in range(2):
            for k, r in enumerate((1, 3)):
                got, mine = stage.at[0, :, pl.ds(0, behind)], grads.at[0, rx * 2 + k, :, high_lanes]
                load = pltpu.make_async_copy(down_h.at[rx, r, :, high_lanes], mine, ssem.at[1])
                copy = pltpu.make_async_copy(pin.at[rx, 2 + k], got, ssem.at[0])
                load.start()
                load.wait()

                @pl.when(links.middle)
                def _():
                    links.remote[relays["pair", rx][k]].wait_recv()
                    copy.start()
                    copy.wait()
                    mine[...] = (mine[...].astype(F32) + got[...].astype(F32)).astype(BF)

                pairs.append(put(mine, pin.at[rx, k], links.z[r]))

    def pair_sum():
        for rx in (1, 0):
            arrived(*pairs[2 * rx : 2 * rx + 2])
            sent(*pairs[2 * rx : 2 * rx + 2])
            copies = [
                pltpu.make_async_copy(src, stage.at[k, :, pl.ds(0, behind)], ssem.at[k])
                for k, src in enumerate((down_h.at[rx, 0, :, high_lanes], pin.at[rx, 0], pin.at[rx, 1]))
            ]
            for c in copies:
                c.start()
            for c in copies:
                c.wait()
            total = stage[0, :, 0:behind].astype(F32) + stage[1, :, 0:behind].astype(F32)
            mine = grads.at[0, rx * 2, :, high_lanes]
            mine[...] = (total + stage[2, :, 0:behind].astype(F32)).astype(BF)
            if rx:
                pairs.append(put(mine, pxin, links.x))

    def grad_far(name):
        buffer, landing = spec[name][2:4]
        for r in ORDER:
            if name == "down":
                xid[name][r] = put(down_h.at[1, r, :, low_lanes], landing.at[r], links.x)
            else:
                buffer(r)[...] = block_of(name, 4 + r).astype(BF)
                xid[name][r] = put(buffer(r), landing.at[r], links.x)

    def grad_near(name, r):
        buffer, landing, zland, width = spec[name][2:6]
        arrived(xid[name][r])
        got = stage.at[0, :, pl.ds(0, width)]
        copies = [pltpu.make_async_copy(landing.at[r], got, ssem.at[0])]
        if name == "down":
            copies.append(pltpu.make_async_copy(down_h.at[0, r, :, low_lanes], stage.at[1, :, low_lanes], ssem.at[1]))
        for c in copies:
            c.start()
        if name != "down":
            mine = block_of(name, r)
            sent(xid[name][r])
        for c in copies:
            c.wait()
        if name == "down":
            mine = stage[1, :, low_lanes].astype(F32)
        buffer(r)[...] = (mine + got[...].astype(F32)).astype(BF)
        if r == 2:
            two_away(name, buffer(2), zland)

    def grad_on(name):
        buffer, _, zland, width = spec[name][2:6]
        got = stage.at[0, :, pl.ds(0, width)]
        for k, r in enumerate((1, 3)):
            copy = pltpu.make_async_copy(zland.at[2 + k], got, ssem.at[0])

            @pl.when(links.middle)
            def _():
                links.remote[relays[name][k]].wait_recv()
                copy.start()
                copy.wait()
                buffer(r)[...] = (buffer(r)[...].astype(F32) + got[...].astype(F32)).astype(BF)

            zid[name][r] = put(buffer(r), zland.at[k], links.z[r])

    def far_sent(name):
        low, high = relays[name]
        pl.when(links.low)(links.remote[low].wait_send)
        pl.when(jnp.logical_not(links.low))(links.remote[high].wait_send)

    writing = []

    def grad_final(name):
        buffer, _, zland, width, result = spec[name][2:]
        copies = []
        for k, r in enumerate((1, 3)):
            arrived(zid[name][r])
            copies.append(pltpu.make_async_copy(zland.at[k], stage.at[k, :, pl.ds(0, width)], ssem.at[k]))
            copies[-1].start()
        if name == "down":
            arrived(pairs[4])
            copies.append(pltpu.make_async_copy(pxin, stage.at[2, :, pl.ds(0, behind)], ssem.at[2]))
            copies[-1].start()
        for c in copies + writing:
            c.wait()
        lanes = slice(0, width)
        total = buffer(0)[...].astype(F32) + stage[0, :, lanes].astype(F32)
        ostage[:, lanes] = total + stage[1, :, lanes].astype(F32)
        if name == "down":
            width = ff
            ostage[:, high_lanes] = grads[0, 0, :, high_lanes].astype(F32) + stage[2, :, 0:behind].astype(F32)
        writing[:] = [pltpu.make_async_copy(ostage.at[:, pl.ds(0, width)], result, osem.at[0])]
        writing[0].start()

    def sweep(terms, row, use):
        def load(b, slot):
            return [
                pltpu.make_async_copy(
                    w.at[b // 4, lax.rem(b, 4)], wrow.at[slot, k, :, pl.ds(0, width)], rsem.at[slot, k]
                )
                for k, (_, w, width) in enumerate(terms)
            ]

        for c in load(0, 0):
            c.start()

        @pl.loop(0, 8)
        def _(b):
            slot = lax.rem(b, 2)

            @pl.when(b + 1 < 8)
            def _():
                for c in load(b + 1, 1 - slot):
                    c.start()

            for c in load(b, slot):
                c.wait()
            lanes = pl.ds(pl.multiple_of(b * 256, 256), 256)
            for m in range(2):
                total = None
                for k, (left, _, width) in enumerate(terms):
                    t = nt(left[m, row : row + HALF, 0:width], wrow[slot, k, :, 0:width])
                    total = t if total is None else total + t
                use(m, lanes, total)

    fid, yid = {}, {}

    def rows_far(i, terms):
        sent(*fid.values())

        def use(m, lanes, total):
            far[m, :, lanes] = total.astype(BF)

        sweep(terms, HALF, use)
        fid[i] = put(far, fin.at[i], links.core)

    def rows_near(i, terms, acc, leaving):
        arrived(fid[i])
        kept(keep(fin.at[i], far_st))

        def use(m, lanes, total):
            total = total + far_st[m, :, lanes].astype(F32)
            acc[m, :, lanes] = total[:ROWS]
            leaving[m, :, lanes] = total[ROWS:].astype(BF)

        sweep(terms, 0, use)

    def rows_on(i, leaving):
        yid[i] = [put(leaving.at[m], yin.at[i, m], links.y) for m in range(2)]

    def rows_final(i, m):
        arrived(yid[i][m])
        kept(keep(yin.at[i, m], far_st.at[m, pl.ds(0, ROWS)]))

    def chunks(body, m):
        @pl.loop(0, 2)
        def _(i):
            body(m, pl.ds(pl.multiple_of(i * 64, 64), 64))

    def norm_back(v, e, row):
        inverse = lax.rsqrt(jnp.mean(v * v, axis=-1, keepdims=True) + EPS)
        u = v * inverse
        gacc[row : row + 1, :] += jnp.sum(e * u, axis=0, keepdims=True)
        w = e * gain[row : row + 1, :]
        return inverse * (w - u * jnp.mean(w * u, axis=-1, keepdims=True))

    grad_far("down")
    pair_start()
    cot_in = keep(c_full, cot)
    ffn_in = [keep(fa_h, dg), keep(fb_h, du)]
    own_in = keep(c_full.at[:, pl.ds(0, ROWS)], obuf)
    late = [keep(nm_h, nm), keep(res_h, res), keep(qkv_h, qkv), keep(att_h, att)]
    late += load_table(links, table_h, table)
    gacc[...] = jnp.zeros_like(gacc)

    def load_col(t, slot):
        lanes = pl.ds(pl.multiple_of(t * 256, 256), 256)
        return pltpu.make_async_copy(wd_f.at[:, :, :, lanes], wcol.at[slot], csem.at[slot])

    load_col(0, 0).start()
    kept(cot_in, *ffn_in)
    tiles = ff // 256
    rest = ff - tiles * 256

    def product_rows(slot, width, start):
        @pl.loop(0, 2)
        def _(m):
            lanes = pl.ds(start, width)
            d = nn(cot[m], wcol[slot, :, :, :, 0:width].reshape(DM, width))
            dg[m, :, lanes] = (d * dg[m, :, lanes].astype(F32)).astype(BF)
            du[m, :, lanes] = (d * du[m, :, lanes].astype(F32)).astype(BF)

    last = pltpu.make_async_copy(
        wd_f.at[:, :, :, pl.ds(tiles * 256, rest)], wcol.at[tiles % 2, :, :, :, pl.ds(0, rest)], csem.at[tiles % 2]
    )

    @pl.loop(0, tiles)
    def _(t):
        slot = lax.rem(t, 2)

        @pl.when(t + 1 < tiles)
        def _():
            load_col(t + 1, 1 - slot).start()

        load_col(t, slot).wait()
        product_rows(slot, 256, pl.multiple_of(t * 256, 256))

    last.start()
    last.wait()
    product_rows(tiles % 2, rest, tiles * 256)

    prod_in = keep(prod_h, prod)
    kept(*late)
    ffn_terms = [(dg, wg_f, ff), (du, wu_f, ff)]
    rows_far(1, ffn_terms)
    grad_far("gate")
    rows_near(1, ffn_terms, acc_m, ysend)
    rows_on(1, ysend)
    grad_near("down", 2)
    grad_near("down", 1)
    grad_far("up")
    pair_on()
    grad_near("down", 3)
    grad_near("down", 0)
    grad_on("down")
    kept(prod_in)
    out_terms = [(prod, wd_f, ff)]
    rows_far(0, out_terms)
    make_mask(links, seg, keys, mask_t, True)
    kept(own_in)

    def output_rows(m, rows):
        total = res[m, rows, :] + acc_o[m, rows, :] + far_st[m, rows, :].astype(F32)
        obuf[m, rows, :] = total.astype(BF)

    def middle(m, rows):
        e = acc_m[m, rows, :] + far_st[m, rows, :].astype(F32)
        d = norm_back(res[m, rows, :], e, 1) + obuf[m, rows, :].astype(F32)
        acc_m[m, rows, :] = d
        dr[m, rows, :] = d.astype(BF)

    ds = []
    for m in range(2):
        rows_final(1, m)
        chunks(middle, m)
        own = dr.at[m, pl.ds(0, ROWS)]
        ds.append(
            [put(own, dr.at[m, pl.ds(ROWS, ROWS)], links.y), put(own, dr.at[m, pl.ds(2 * ROWS, ROWS)], links.core)]
        )
    wo_in = [keep(wo_f.at[:, :, :, pl.ds(k * 256, 256)], wcol.at[k]) for k in range(2)]
    rows_near(0, out_terms, acc_o, ysend_o)
    rows_on(0, ysend_o)
    na_in = keep(na_h, cot)
    grad_near("gate", 2)

    def dr_arrives(m):
        arrived(ds[m][0])
        ds[m].append(put(dr.at[m, pl.ds(ROWS, ROWS)], dr.at[m, pl.ds(3 * ROWS, ROWS)], links.core))
        arrived(*ds[m])

    def attended_back(m):
        for k in range(2):
            datt[m, :, k * 256 : (k + 1) * 256] = nn(dr[m], wcol[k].reshape(DM, 256)).astype(BF)

    def attend_back(m):
        kv = qkv[m, :, 512:640].astype(F32)
        lane = lax.broadcasted_iota(jnp.int32, (LEN4, 128), 1)
        half = lax.broadcasted_iota(jnp.int32, (256, 128), 1) < 64
        ka = jnp.where(lane < 64, kv, 0.0)
        vb = jnp.where(lane < 64, 0.0, kv)
        kb, va = pltpu.roll(ka, 64, 1), pltpu.roll(vb, 64, 1)
        heads = [
            ((k * 0.125).astype(BF), (k * 0.125).T.astype(BF), v.astype(BF), keep_lanes)
            for k, v, keep_lanes in ((ka, va, half), (kb, vb, jnp.logical_not(half)))
        ]
        dkacc[...] = jnp.zeros_like(dkacc)
        dvacc[...] = jnp.zeros_like(dvacc)

        @pl.loop(0, 8)
        def _(i):
            lanes = pl.ds(pl.multiple_of(i // 2 * 128, 128), 128)
            rows = pl.ds(pl.multiple_of(lax.rem(i, 2) * 256, 256), 256)
            q, do = qkv[m, rows, lanes], datt[m, rows, lanes]
            bias = mask_t[m, :, rows].astype(F32)
            dq_t = jnp.zeros((128, 256), F32)
            for k, k_t, v, keep_lanes in heads:
                s = nt(k, q) + bias
                e = jnp.exp(s - jnp.max(s, axis=0, keepdims=True))
                p = e * (1.0 / jnp.sum(e, axis=0, keepdims=True))
                d = nt(v, do)
                ds_ = (p * (d - jnp.sum(p * d, axis=0, keepdims=True))).astype(BF)
                dq_t = dq_t + nn(k_t, ds_)
                zero = jnp.zeros_like(q)
                dkacc[...] += nn(ds_, jnp.where(keep_lanes, q, zero))
                dvacc[...] += nn(p.astype(BF), jnp.where(keep_lanes, do, zero))
            dqkv[m, rows, lanes] = rope_tile(dq_t.T, table[0, rows, :], -table[1, rows, :]).astype(BF)

        dk = dkacc[...] + pltpu.roll(dkacc[...], 64, 1)
        dv = dvacc[...] + pltpu.roll(dvacc[...], 64, 1)
        dk = rope_tile(dk * 0.125, table[0], -table[1])
        dqkv[m, :, 512:640] = jnp.where(lane < 64, dk, dv).astype(BF)

    kept(*wo_in)
    dr_arrives(0)
    attended_back(0)
    attend_back(0)
    pair_sum()
    dr_arrives(1)
    attended_back(1)
    grad_near("gate", 1)
    attend_back(1)
    na_terms = [(dqkv, wqkv_f, 640)]
    kept(na_in)
    grad_far("qkv")
    rows_far(2, na_terms)
    grad_far("out")
    grad_near("gate", 3)
    grad_near("gate", 0)
    grad_on("gate")
    for m in range(2):
        rows_final(0, m)
        chunks(output_rows, m)
    for b in range(8):
        keep(obuf.at[:, :, pl.ds(b * 256, 256)], out_o.at[:, :, links.lanes(b)])
    sent(*yid[1])
    rows_near(2, na_terms, acc_o, ysend)
    rows_on(2, ysend)
    grad_near("up", 2)
    grad_near("up", 1)
    grad_near("up", 3)
    own_x = far_st.at[:, pl.ds(ROWS, ROWS)]
    kept(*[keep(x_ref.at[:, :, links.lanes(b)], own_x.at[:, :, pl.ds(b * 256, 256)]) for b in range(8)])

    def last_rows(m, rows):
        e = acc_o[m, rows, :] + far_st[m, rows, :].astype(F32)
        v = own_x[m, rows, :].astype(F32)
        acc_m[m, rows, :] += norm_back(v, e, 0)

    for m in range(2):
        rows_final(2, m)
        chunks(last_rows, m)
    for b in range(8):
        keep(acc_m.at[:, :, pl.ds(b * 256, 256)], din_o.at[:, :, links.lanes(b)])
    gx = put(gacc.at[:, pl.ds(1024, 1024)], gxin, links.x)
    grad_near("up", 0)
    grad_on("up")
    grad_final("down")
    grad_final("gate")
    for name in ("out", "qkv"):
        for r in ORDER:
            grad_near(name, r)
        if name == "out":
            grad_on(name)
    arrived(gx)
    gnear[...] = gacc[:, 0:1024] + gxin[...]
    gz = [put(gnear.at[:, pl.ds(r * 256, 256)], gzin.at[r - 1], links.z[r]) for r in (1, 2, 3)]
    grad_on("qkv")
    grad_final("up")
    arrived(*gz)
    gown[...] = gnear[:, 0:256] + gzin[0] + gzin[1] + gzin[2]
    gs = [put(gown, gsin.at[k], p) for k, p in enumerate((links.core, links.y, links.both))]
    grad_final("out")
    arrived(*gs)
    gain_o[...] = gown[...] + gsin[0] + gsin[1] + gsin[2]
    grad_final("qkv")
    for c in writing:
        c.wait()
    for name in relays:
        far_sent(name)
    links.finish()


def backward(seg, gain, table, x, arrays):
    micro, rows, d = x.shape
    sd = jax.ShapeDtypeStruct
    ff = arrays[-4].shape[2]
    v = pltpu.VMEM
    behind = ff - 640
    out_shape = [
        sd(x.shape, BF), sd(x.shape, F32), sd((8, 256), F32), sd((256, 640), F32), sd((256, 512), F32),
        sd((256, ff), F32), sd((256, ff), F32), sd((256, ff), F32), sd((3, 4, 256, ff), BF), sd((4, 256, 512), BF),
        sd((4, 256, 640), BF), sd((3, 4, 256, ff), BF), sd((4, 256, 512), BF), sd((4, 256, 640), BF),
        sd((3, 2, 256, d), BF), sd((3, 2, 128, d), BF), sd((2, 4, 256, behind), BF), sd((256, behind), BF),
    ]
    toks = (2, 512, d)
    scratch = [
        v(toks, BF), v(toks, BF), v(toks, BF), v((2, 512, ff), BF), v((2, 512, ff), BF), v((3, 4, 256, ff), BF),
        v((4, 256, 1152), BF), v((3, 256, ff), BF), v((256, ff), F32), v((2, 2, 4, 256, 256), BF), v((2, 2, 256, ff), BF),
        v((2, 256, d), BF), v((2, 256, d), BF), v((2, 128, d), BF), v((2, 128, d), BF), v((2, 128, d), F32), v((2, 128, d), F32),
        v((2, 128, d), F32), v((2, 512, 640), BF), v((2, 512, 512), BF), v((2, 512, 512), BF), v((2, 512, 640), BF),
        v((2, 128, d), BF), v((512, 128), F32), v((512, 128), F32), v((8, d), F32), v((8, 1024), F32),
        v((8, 1024), F32), v((3, 8, 256), F32), v((8, 256), F32), v((3, 8, 256), F32),
        v((4, 512, 128), F32), v((2, 512, 512), BF), v((8, 512), F32),
        pltpu.SemaphoreType.DMA((80,)), pltpu.SemaphoreType.DMA((80,)), pltpu.SemaphoreType.DMA((64,)),
        pltpu.SemaphoreType.DMA((2,)), pltpu.SemaphoreType.DMA((2, 2)), pltpu.SemaphoreType.DMA((3,)),
        pltpu.SemaphoreType.DMA((1,)),
    ]
    return pl.pallas_call(
        backward_kernel,
        out_shape=out_shape,
        in_specs=[VMEM] * 2 + [HBM] * (2 + len(arrays)),
        out_specs=[HBM] * 2 + [VMEM] + [HBM] * 15,
        scratch_shapes=scratch,
        compiler_params=pltpu.CompilerParams(collective_id=1, has_side_effects=True, vmem_limit_bytes=LIMIT_B),
    )(seg, gain, table, x, *arrays)


def rope_table():
    frequency = THETA ** (-(np.arange(HD // 2) * (2.0 / HD)))
    angles = np.arange(LEN4)[:, None] * frequency[None, :]
    cosine, sine = np.cos(angles), np.sin(angles)
    c4 = np.tile(cosine, (1, 4))
    s4 = np.concatenate([-sine, sine, -sine, sine], axis=1)
    one, zero = np.ones((LEN4, HD)), np.zeros((LEN4, HD))
    ck, sk = np.concatenate([c4[:, :HD], one], axis=1), np.concatenate([s4[:, :HD], zero], axis=1)
    return np.stack([c4, s4, ck, sk]).astype(np.float32)


def per_device_grid(
    inputs, segments, cotangent, attn_gain, w_query, w_key, w_value, w_out, mlp_gain, w_gate, w_up, w_down,
):
    nq, nk = w_query.shape[1], w_key.shape[1]
    w_qkv = jnp.concatenate([w_query, w_key, w_value], axis=1)
    me = lax.axis_index("seq")
    size = attn_gain.shape[0]
    row = lax.broadcasted_iota(jnp.int32, (8, 4 * size), 0)
    lane = lax.broadcasted_iota(jnp.int32, (8, 4 * size), 1)
    g = jnp.where(row == 0, jnp.tile(attn_gain, 4)[None].astype(F32), jnp.tile(mlp_gain, 4)[None].astype(F32))
    g = jnp.where(jnp.logical_and(row < 2, lane // size == me), g, 0.0)
    table = jnp.asarray(rope_table())
    made = forward(inputs, cotangent, g, segments, table, [w_qkv, w_out, w_gate, w_up, w_down])
    c_full, wqkv, wo, wg, wu, wd, na, qkv, att, res, nm, gain, prod, fa, fb, down = made
    arrays = [c_full, wqkv, wo, wg, wu, wd, na, qkv, att, res, nm, prod, fa, fb, down]
    back = backward(segments, gain, table, inputs, arrays)
    output, d_input, gains, gq, go, gg, gu, gd = back[:8]
    gains = lax.dynamic_slice_in_dim(gains, me * size, size, 1)
    return (
        output, d_input, gains[0], gq[:, :nq], gq[:, nq : nq + nk], gq[:, nq + nk :], go, gains[1], gg, gu, gd,
    )


class AnyMesh:
    def gather(self, x, c, shards):
        fulls = [lax.all_gather(w, "dp", axis=0, tiled=True) for w in shards]
        return gather_rows(x), gather_rows(c), fulls

    def gather_gains(self, g):
        return lax.all_gather(g, ("dp", "seq"), axis=1, tiled=True)

    def scatter_gain(self, g):
        return lax.psum_scatter(g, ("dp", "seq"), scatter_dimension=0, tiled=True)

    def scatter(self, left, right):
        return lax.psum_scatter(
            outer_sum(left, right).astype(BF), "dp", scatter_dimension=0, tiled=True
        ).astype(F32)

    def to_relative(self, a):
        return a

    def from_relative(self, a):
        return a


def shift_core(a):
    return lax.ppermute(a, "seq", [(i, i ^ 1) for i in range(4)])


def shift_y(a):
    return lax.ppermute(a, "seq", [(i, i ^ 2) for i in range(4)])


def gather_rows(a):
    across = shift_y(a)
    return jnp.concatenate([a, across, shift_core(a), shift_core(across)], axis=-2)


def scatter_rows(make):
    got = shift_core(make(1).astype(BF))
    near = make(0) + got.astype(F32)
    rows = near.shape[1] // 2
    got = shift_y(near[:, rows:].astype(BF))
    return near[:, :rows] + got.astype(F32)


def per_device(
    inputs, segments, cotangent, attn_gain, w_query, w_key, w_value, w_out, mlp_gain, w_gate, w_up, w_down,
):
    micro, rows, d = inputs.shape
    seq = lax.axis_size("seq")
    length = rows * seq
    full = micro * length
    half = length // 2
    grid = AnyMesh()

    nq, nk = w_query.shape[1], w_key.shape[1]
    heads, kv_heads = nq // HD, nk // HD
    groups = heads // kv_heads
    w_qkv = jnp.concatenate([w_query, w_key, w_value], axis=1)

    inputs = grid.to_relative(inputs)
    cotangent = grid.to_relative(cotangent)
    gains = grid.gather_gains(jnp.stack([attn_gain, mlp_gain]).astype(F32))
    gain_a, gain_m = gains[0], gains[1]

    shards = [w_qkv, w_out, w_gate, w_up, w_down]
    x_full, up_full, (wqkv, wo, wg, wu, wd) = grid.gather(inputs, cotangent, shards)

    me = lax.axis_index("seq")
    order = [me, me ^ 2, me ^ 1, me ^ 3]
    pos = jnp.concatenate([j * rows + jnp.arange(rows, dtype=jnp.int32) for j in order])
    segs = jnp.concatenate([lax.dynamic_slice_in_dim(segments, j * rows, rows, 1) for j in order], axis=1)
    cosine, sine = rope_tables(pos)
    cos_f, sin_f = jnp.tile(cosine, (micro, 1)), jnp.tile(sine, (micro, 1))
    allowed = (pos[None, :] <= pos[:, None])[None] & (segs[:, :, None] == segs[:, None, :])
    allowed = allowed[:, None, None]

    def pieces(make):
        return lambda i: make(slice(i * half, (i + 1) * half)).reshape(micro, half, d)

    def rows_of(a, s):
        return a.reshape(micro, length, -1)[:, s].reshape(micro * half, -1)

    hidden_full = x_full.reshape(full, d).astype(F32)
    normed, inverse_f = normalize(hidden_full, gain_a)
    na = normed.astype(BF)
    hidden = inputs.astype(F32)
    upstream = cotangent.astype(F32)
    up_full = up_full.reshape(full, d)

    def rope(x, n, s):
        return rotate(x.reshape(full, n, HD), cos_f, s).astype(BF).reshape(full, n * HD)

    qkv = project(na, wqkv)
    q = rope(qkv[:, :nq], heads, sin_f)
    k = rope(qkv[:, nq : nq + nk], kv_heads, sin_f)
    v = qkv[:, nq + nk :].astype(BF)
    qg = q.reshape(micro, length, kv_heads, groups, HD)
    kg = k.reshape(micro, length, kv_heads, HD)
    vg = v.reshape(micro, length, kv_heads, HD)
    scores = jnp.einsum("mqkgd,mpkd->mkgqp", qg, kg, preferred_element_type=F32) * HD ** (-0.5)
    scores = jnp.where(allowed, scores, NEGATIVE)
    maximum = jnp.max(scores, axis=-1, keepdims=True)
    weights = jnp.where(allowed, jnp.exp(scores - maximum), 0.0)
    denominator = jnp.sum(weights, axis=-1, keepdims=True)
    prob = weights / denominator
    prob_b = prob.astype(BF)
    attended = jnp.einsum("mkgqp,mpkd->mqkgd", prob_b, vg, preferred_element_type=F32)
    attended = attended.astype(BF).reshape(full, heads * HD)
    residual = hidden + scatter_rows(pieces(lambda s: project_back(rows_of(attended, s), wo)))
    normed, inverse_m = normalize(residual, gain_m)
    nm = gather_rows(normed.astype(BF)).reshape(full, d)
    gate_pre = project(nm, wg)
    up_proj = project(nm, wu)
    sigmoid_g = jax.nn.sigmoid(gate_pre)
    active = gate_pre * sigmoid_g
    product = (active * up_proj).astype(BF)
    g_down = grid.scatter(up_full, product)
    d_product = project(up_full, wd)
    d_gate = (d_product * up_proj * sigmoid_g * (1.0 + gate_pre * (1.0 - sigmoid_g))).astype(BF)
    d_up = (d_product * active).astype(BF)
    d_nm = scatter_rows(
        pieces(lambda s: project_back(rows_of(d_gate, s), wg) + project_back(rows_of(d_up, s), wu))
    )
    g_gate = grid.scatter(nm, d_gate)
    g_up = grid.scatter(nm, d_up)
    output = (residual + scatter_rows(pieces(lambda s: project_back(rows_of(product, s), wd)))).astype(BF)
    flat = lambda a: a.reshape(micro * rows, -1)
    d_norm_m, g_gain_m = normalize_back(flat(residual), flat(inverse_m), gain_m, flat(d_nm))
    d_residual = upstream + d_norm_m.reshape(micro, rows, d)
    dr = gather_rows(d_residual.astype(BF)).reshape(full, d)
    d_att = project(dr, wo).astype(BF)
    dg = d_att.reshape(micro, length, kv_heads, groups, HD)
    d_values = jnp.einsum("mkgqp,mqkgd->mpkd", prob_b, dg, preferred_element_type=F32)
    d_prob = jnp.einsum("mqkgd,mpkd->mkgqp", dg, vg, preferred_element_type=F32)
    row_sum = jnp.sum(prob * d_prob, axis=-1, keepdims=True)
    d_scores = (prob * (d_prob - row_sum) * HD ** (-0.5)).astype(BF)
    d_query = jnp.einsum("mkgqp,mpkd->mqkgd", d_scores, kg, preferred_element_type=F32)
    d_keys = jnp.einsum("mkgqp,mqkgd->mpkd", d_scores, qg, preferred_element_type=F32)
    dq = rope(d_query, heads, -sin_f)
    dk = rope(d_keys, kv_heads, -sin_f)
    dv = d_values.astype(BF).reshape(full, kv_heads * HD)
    dqkv = jnp.concatenate([dq, dk, dv], axis=1)
    g_out = grid.scatter(dr, attended)
    d_na = scatter_rows(pieces(lambda s: project_back(rows_of(dqkv, s), wqkv)))
    g_qkv = grid.scatter(na, dqkv)
    inverse_a = inverse_f.reshape(micro, length, 1)[:, :rows]
    d_norm_a, g_gain_a = normalize_back(flat(hidden), flat(inverse_a), gain_a, flat(d_na))
    d_input = d_residual + d_norm_a.reshape(micro, rows, d)
    return (
        grid.from_relative(output),
        grid.from_relative(d_input),
        grid.scatter_gain(g_gain_a),
        g_qkv[:, :nq],
        g_qkv[:, nq : nq + nk],
        g_qkv[:, nq + nk :],
        g_out,
        grid.scatter_gain(g_gain_m),
        g_gate,
        g_up,
        g_down,
    )


def solution(mesh):
    tok, wt, gn = P(None, ("dp", "seq"), None), P("dp", "seq"), P(("dp", "seq"))
    grid = mesh.shape["dp"] == 8 and mesh.shape["seq"] == 4
    return jax.shard_map(
        per_device_grid if grid else per_device,
        mesh=mesh,
        in_specs=(tok, P(None, "dp"), tok, gn, wt, wt, wt, wt, gn, wt, wt, wt),
        out_specs=(tok, tok, gn, wt, wt, wt, wt, gn, wt, wt, wt),
        check_vma=False,
    )
```

```python
import jax
import jax.numpy as jnp
import numpy as np
from jax import lax
from jax.experimental import pallas as pl
from jax.experimental.pallas import tpu as pltpu
from jax.sharding import PartitionSpec as P

HD = 64
EPS = 1e-05
THETA = 10000.0
NEGATIVE = -1e30
BF = jnp.bfloat16
F32 = jnp.float32


def rope_tables(positions):
    half_dim = HD // 2
    frequency = THETA ** (-(jnp.arange(half_dim).astype(F32) * (2.0 / HD)))
    angles = positions.astype(F32)[:, None] * frequency[None, :]
    return (jnp.cos(angles), jnp.sin(angles))


def rotate(values, cosine, sine_table):
    half_dim = values.shape[-1] // 2
    c = cosine[:, None, :]
    s = sine_table[:, None, :]
    a = values[..., :half_dim]
    b = values[..., half_dim:]
    return jnp.concatenate([a * c - b * s, b * c + a * s], axis=-1)


def unrotate(gradient, cosine, sine_table):
    return rotate(gradient, cosine, -sine_table)


def normalize(hidden, gain_vec):
    inverse = lax.rsqrt(jnp.mean(hidden * hidden, axis=-1, keepdims=True) + EPS)
    return (hidden * inverse * gain_vec, inverse)


def normalize_back(hidden, inverse, gain_vec, gradient):
    unit_rows = hidden * inverse
    gain_grad = jnp.sum(gradient * unit_rows, axis=0)
    weighted = gradient * gain_vec
    return (
        inverse * (weighted - unit_rows * jnp.mean(weighted * unit_rows, axis=-1, keepdims=True)),
        gain_grad,
    )


def project(a, b):
    return jnp.dot(a, b, preferred_element_type=F32)


def project_back(a, b):
    return lax.dot_general(a, b, (((1,), (1,)), ((), ())), preferred_element_type=F32)


def outer_sum(a, b):
    return lax.dot_general(a, b, (((0,), (0,)), ((), ())), preferred_element_type=F32)


MESH_ID = pl.DeviceIdType.MESH
HBM = pl.BlockSpec(memory_space=pl.ANY)
VMEM = pl.BlockSpec(memory_space=pltpu.VMEM)
ROWS = 128
LEN4 = 512
HALF = 256
DM = 2048
LIMIT = 60 * 1024 * 1024
LIMIT_B = 62 * 1024 * 1024


def nt(a, b):
    return lax.dot_general(a, b, (((1,), (1,)), ((), ())), preferred_element_type=F32)


def tn(a, b):
    return lax.dot_general(a, b, (((0,), (0,)), ((), ())), preferred_element_type=F32)


def nn(a, b):
    return jnp.dot(a, b, preferred_element_type=F32)


class Links:
    def __init__(self, send, recv, local):
        self.send, self.recv, self.local = send, recv, local
        self.remote, self.own = [], []
        self.seen, self.gone, self.middle_only = set(), set(), set()
        dp, sq = lax.axis_index("dp"), lax.axis_index("seq")
        self.dp, self.sq = dp, sq
        height = lax.div(dp, 2)
        self.middle = jnp.logical_and(height >= 1, height <= 2)
        self.low = height <= 1
        self.z = [(lax.rem(dp + 2 * r, 8), sq) for r in range(4)]
        self.x = (dp + 1 - 2 * lax.rem(dp, 2), sq)
        core = sq + 1 - 2 * lax.rem(sq, 2)
        self.core = (dp, core)
        self.y = (dp, lax.rem(sq + 2, 4))
        self.both = (dp, lax.rem(core + 2, 4))
        peers = self.z[1:] + [self.x, self.core, self.y, self.both]
        barrier = pltpu.get_barrier_semaphore()
        for peer in peers:
            pl.semaphore_signal(barrier, inc=1, device_id=peer, device_id_type=MESH_ID)
        pl.semaphore_wait(barrier, len(peers))

    def lanes(self, b):
        z, x = lax.div(self.dp, 2), lax.rem(self.dp, 2)
        at = lax.rem(z + b % 4, 4) * 2 + (x if b < 4 else 1 - x)
        return pl.ds(pl.multiple_of(at * 256, 256), 256)

    def order(self, k):
        return (self.sq, self.y[1], self.core[1], self.both[1])[k]

    def describe(self, src, dst, peer, landing=None):
        i = len(self.remote)
        copy = pltpu.make_async_remote_copy(
            src_ref=src,
            dst_ref=dst,
            send_sem=self.send.at[i],
            recv_sem=self.recv.at[i if landing is None else landing],
            device_id=peer,
            device_id_type=MESH_ID,
        )
        self.remote.append(copy)
        return i

    def put(self, src, dst, peer):
        i = self.describe(src, dst, peer)
        self.remote[i].start()
        return i

    def start_in_middle(self, i):
        self.middle_only.add(i)
        pl.when(self.middle)(self.remote[i].start)

    def arrived(self, *ids):
        for i in ids:
            if i not in self.seen:
                self.seen.add(i)
                self.remote[i].wait_recv()

    def sent(self, *ids):
        for i in ids:
            if i not in self.gone:
                self.gone.add(i)
                if i in self.middle_only:
                    pl.when(self.middle)(self.remote[i].wait_send)
                else:
                    self.remote[i].wait_send()

    def keep(self, src, dst):
        copy = pltpu.make_async_copy(src, dst, self.local.at[len(self.own)])
        copy.start()
        self.own.append([copy, False])
        return len(self.own) - 1

    def kept(self, *ids):
        for i in ids:
            if not self.own[i][1]:
                self.own[i][1] = True
                self.own[i][0].wait()

    def finish(self):
        self.sent(*range(len(self.remote)))
        self.arrived(*range(len(self.remote)))
        self.kept(*range(len(self.own)))


def load_table(links, table_h, table):
    return [
        links.keep(
            table_h.at[:, pl.ds(pl.multiple_of(links.order(k) * ROWS, ROWS), ROWS)],
            table.at[:, pl.ds(k * ROWS, ROWS)],
        )
        for k in range(4)
    ]


def make_mask(links, seg, keys, mask, by_key):
    for k in range(4):
        at = pl.ds(k * ROWS, ROWS)
        place = links.order(k) * ROWS
        keys[0:2, at] = seg[:, pl.ds(pl.multiple_of(place, ROWS), ROWS)].astype(F32)
        keys[2:3, at] = (lax.broadcasted_iota(jnp.int32, (1, ROWS), 1) + place).astype(F32)
    columns = keys[...].T
    for m in range(2):
        for k in range(4):
            at = slice(k * ROWS, (k + 1) * ROWS)
            same = columns[at, m : m + 1] == keys[m : m + 1, :]
            a, b = columns[at, 2:3], keys[2:3, :]
            ahead = (a <= b) if by_key else (b <= a)
            mask[m, at, :] = jnp.where(jnp.logical_and(same, ahead), 0.0, NEGATIVE).astype(BF)


def rope_tile(t, cosine, sine):
    lane = lax.broadcasted_iota(jnp.int32, t.shape, 1)
    turned = jnp.where(lax.rem(lane, 64) < 32, pltpu.roll(t, 96, 1), pltpu.roll(t, 32, 1))
    return t * cosine + turned * sine


def forward_kernel(
    x_ref, c_ref, g_ref, seg, table_h, wqkv_s, wo_s, wg_s, wu_s, wd_s,
    c_full, wqkv_f, wo_f, wg_f, wu_f, wd_f, na_o, qkv_o, att_o, res_o, nm_o, gain_o, prod_o, fa_o, fb_o, down_o,
    xf, nm, wqkv_v, wo_v, qkv, att, far, far_in, near, ysend, yin, own_x, gseq, gfull, gown, prod, fa, fb, wt, lbuf, gbuf, table, mask, keys,
    send, recv, local, wsem, lsem, gsem,
):
    links = Links(send, recv, local)
    put, arrived = links.put, links.arrived
    first, rest = pl.ds(0, 768), pl.ds(768, wg_s.shape[1] - 768)
    sixth, seventh = pl.ds(0, 640), pl.ds(640, wd_s.shape[1] - 640)
    shards = [wqkv_s, wo_s] + [w.at[:, s] for s in (first, rest) for w in (wg_s, wu_s)]
    fulls = [wqkv_f, wo_f] + [w.at[:, :, :, s] for s in (first, rest) for w in (wg_f, wu_f)]
    shards += [wd_s.at[:, sixth], wd_s.at[:, seventh]]
    fulls += [wd_f.at[:, :, :, sixth], wd_f.at[:, :, :, seventh]]

    def part(full, k):
        return full.at[:, pl.ds(k * ROWS, ROWS)]

    def seq_start(src, full):
        return [put(src, part(full, 1), links.y), put(src, part(full, 2), links.core)]

    def seq_forward(full, ids):
        arrived(ids[0])
        ids.append(put(part(full, 1), part(full, 3), links.core))

    placed = []

    def z_start(i):
        placed.append(links.keep(shards[i], fulls[i].at[0, 0]))
        return {r: put(shards[i], fulls[i].at[0, r], links.z[4 - r]) for r in (1, 3)}

    def x_own(i):
        return [put(shards[i], fulls[i].at[1, 0], links.x)]

    def relays(full, rx, copies):
        copies[2] = links.describe(full.at[rx, 1], full.at[rx, 2], links.z[3])
        other = links.describe(full.at[rx, 3], full.at[rx, 2], links.z[1], copies[2])
        links.seen.add(other)
        return {1: copies[2], 3: other}

    def x_near(i, copies, ids):
        full = fulls[i]
        relay = relays(full, 0, copies)
        for r in (1, 3):
            arrived(copies[r])
            links.start_in_middle(relay[r])
            ids.append(put(full.at[0, r], full.at[1, r], links.x))

    def pair_start(i, ids):
        full = fulls[i]
        placed.append(links.keep(shards[i], full.at[0, 0]))
        arrived(*ids)
        return [
            {r: put(src, full.at[rx, r], links.z[4 - r]) for r in (1, 3)}
            for rx, src in enumerate((shards[i], full.at[1, 0]))
        ]

    def pair_on(i, pair):
        for rx, copies in enumerate(pair):
            relay = relays(fulls[i], rx, copies)
            for r in (1, 3):
                arrived(copies[r])
                links.start_in_middle(relay[r])

    def x_far(i, copies, ids):
        arrived(copies[2])
        ids.append(put(fulls[i].at[0, 2], fulls[i].at[1, 2], links.x))

    placing = [links.keep(x_ref.at[:, :, links.lanes(b)], xf.at[:, pl.ds(0, ROWS), pl.ds(b * 256, 256)]) for b in range(8)]
    c_own = [links.keep(c_ref.at[:, :, links.lanes(b)], c_full.at[:, pl.ds(0, ROWS), pl.ds(b * 256, 256)]) for b in range(8)]
    table_in = load_table(links, table_h, table)
    gs = [put(g_ref, gseq.at[k], p) for k, p in ((1, links.core), (2, links.y), (3, links.both))]
    zs, xd = {}, {}

    def start(i):
        zs[i] = z_start(i)

    def across(i):
        xd[i] = x_own(i)

    def near_blocks(i):
        x_near(i, zs[i], xd[i])

    def far_block(i):
        x_far(i, zs[i], xd[i])

    start(0)
    across(0)
    links.kept(*placing)
    xs = seq_start(part(xf, 0), xf)
    own1 = links.keep(part(xf, 0), own_x)
    arrived(*gs)
    gown[...] = g_ref[...] + gseq[1] + gseq[2] + gseq[3]
    gfull[0, 0] = gown[...]
    gz = [put(gown, gfull.at[0, r], links.z[4 - r]) for r in (1, 2, 3)]
    gx = [put(gown, gfull.at[1, 0], links.x)]
    start(1)
    near_blocks(0)
    make_mask(links, seg, keys, mask, False)
    links.kept(*table_in)
    for r in (1, 2, 3):
        arrived(gz[r - 1])
        gx.append(put(gfull.at[0, r], gfull.at[1, r], links.x))
    far_block(0)
    across(1)
    start(2)
    seq_forward(xf, xs)
    arrived(*gx)
    for b in range(8):
        gain_o[:, b * 256 : (b + 1) * 256] = gfull[b // 4, b % 4]
    arrived(*xs)
    links.sent(*xs)
    links.kept(own1)

    @pl.loop(0, 16)
    def _(i):
        m, r = i // 8, pl.multiple_of(lax.rem(i, 8) * 64, 64)
        v = xf[m, pl.ds(r, 64), :].astype(F32)
        inverse = lax.rsqrt(jnp.mean(v * v, axis=-1, keepdims=True) + EPS)
        xf[m, pl.ds(r, 64), :] = (v * inverse * gain_o[0:1, :]).astype(BF)

    na_copy = links.keep(xf, na_o)
    near_blocks(1)
    arrived(*xd[0])
    links.kept(placed[0])
    load0 = links.keep(wqkv_f, wqkv_v)
    links.kept(load0)

    @pl.loop(0, 4)
    def _(i):
        m, r = i // 2, pl.multiple_of(lax.rem(i, 2) * 256, 256)
        rows = pl.ds(r, 256)
        a = xf[m, rows, :]
        cq, sq = table[0, rows, :], table[1, rows, :]
        for n in range(2):
            t = nn(a, wqkv_v[:, :, :, n * 256 : (n + 1) * 256].reshape(DM, 256))
            for j in range(2):
                lanes = slice(n * 256 + j * 128, n * 256 + (j + 1) * 128)
                qkv[m, rows, lanes] = rope_tile(t[:, j * 128 : (j + 1) * 128], cq, sq).astype(BF)
        t = nn(a, wqkv_v[:, :, :, 512:640].reshape(DM, 128))
        qkv[m, rows, 512:640] = rope_tile(t, table[2, rows, :], table[3, rows, :]).astype(BF)

    links.keep(qkv, qkv_o)
    far_block(1)
    across(2)
    start(3)
    across(3)

    def attend(m):
        kv = qkv[m, :, 512:640].astype(F32)
        lane = lax.broadcasted_iota(jnp.int32, (LEN4, 128), 1)
        ka = jnp.where(lane < 64, kv, 0.0)
        vb = jnp.where(lane < 64, 0.0, kv)
        ka = ka * 0.125
        ks = [ka.astype(BF), pltpu.roll(ka, 64, 1).astype(BF)]
        vs = [pltpu.roll(vb, 64, 1).astype(BF), vb.astype(BF)]

        @pl.loop(0, 8)
        def _(i):
            lanes = pl.ds(pl.multiple_of(i // 2 * 128, 128), 128)
            rows = pl.ds(pl.multiple_of(lax.rem(i, 2) * 256, 256), 256)
            q = qkv[m, rows, lanes]
            bias = mask[m, rows, :].astype(F32)
            out = jnp.zeros((256, 128), F32)
            for k, v in zip(ks, vs):
                s = nt(q, k) + bias
                e = jnp.exp(s - jnp.max(s, axis=-1, keepdims=True))
                p = (e * (1.0 / jnp.sum(e, axis=-1, keepdims=True))).astype(BF)
                out = out + nn(p, v)
            att[m, rows, lanes] = out.astype(BF)

    attend(0)
    near_blocks(2)
    start(4)
    attend(1)
    far_block(2)
    links.keep(att, att_o)
    arrived(*xd[1])
    links.kept(placed[1])
    load1 = links.keep(wo_f, wo_v)
    links.kept(load1)

    def out_rows(m, row, dst, dtype):
        @pl.loop(0, 8)
        def _(n):
            w = wo_v[n // 4, lax.rem(n, 4)]
            lanes = pl.ds(pl.multiple_of(n * 256, 256), 256)
            dst[m, :, lanes] = nt(att[m, row : row + HALF, :], w).astype(dtype)

    for m in range(2):
        out_rows(m, HALF, far, BF)
    fc = put(far, far_in, links.core)
    near_blocks(3)
    for m in range(2):
        out_rows(m, 0, near, F32)
    arrived(fc)

    @pl.loop(0, 4)
    def _(i):
        m, r = i // 2, pl.multiple_of(lax.rem(i, 2) * 64, 64)
        rows = pl.ds(r + ROWS, 64)
        ysend[m, pl.ds(r, 64), :] = (near[m, rows, :] + far_in[m, rows, :].astype(F32)).astype(BF)

    yc = put(ysend, yin, links.y)
    far_block(3)
    across(4)
    start(5)
    across(5)
    across(7)
    arrived(yc)

    @pl.loop(0, 4)
    def _(i):
        m, r = i // 2, pl.multiple_of(lax.rem(i, 2) * 64, 64)
        rows = pl.ds(r, 64)
        v = near[m, rows, :] + far_in[m, rows, :].astype(F32) + yin[m, rows, :].astype(F32) + own_x[m, rows, :].astype(F32)
        res_o[m, rows, :] = v
        inverse = lax.rsqrt(jnp.mean(v * v, axis=-1, keepdims=True) + EPS)
        nm[m, rows, :] = (v * inverse * gain_o[1:2, :]).astype(BF)

    ns = seq_start(part(nm, 0), nm)
    near_blocks(4)
    far_block(4)
    start(6)
    seq_forward(nm, ns)
    links.kept(*c_own)
    cs = seq_start(part(c_full, 0), c_full)
    arrived(*ns)
    links.keep(nm, nm_o)
    arrived(*xd[2], *xd[3])
    links.kept(placed[2], placed[3])

    def load(t, slot):
        lanes = pl.ds(pl.multiple_of(t * 128, 128), 128)
        return [
            pltpu.make_async_copy(w.at[:, :, :, lanes], wt.at[slot, :, :, :, pl.ds(k * 128, 128)], wsem.at[slot, k])
            for k, w in enumerate((wg_f, wu_f))
        ]

    def up_tile(t, slot):
        lanes = pl.ds(pl.multiple_of(t * 128, 128), 128)

        @pl.loop(0, 2)
        def _(m):
            r = nn(nm[m], wt[slot].reshape(DM, 256))
            g, u = r[:, :128], r[:, 128:]
            s = jax.nn.sigmoid(g)
            active = g * s
            prod[m, :, lanes] = (active * u).astype(BF)
            fa[m, :, lanes] = (u * s * (1.0 + g * (1.0 - s))).astype(BF)
            fb[m, :, lanes] = active.astype(BF)

    for c in load(0, 0):
        c.start()
    tiles = wg_s.shape[1] // 128

    def tile_step(t):
        slot = lax.rem(t, 2)

        @pl.when(t + 1 < tiles)
        def _():
            for c in load(t + 1, 1 - slot):
                c.start()

        for c in load(t, slot):
            c.wait()
        up_tile(t, slot)

    pl.loop(0, 3)(tile_step)
    near_blocks(5)
    far_block(5)
    across(6)
    pair = pair_start(7, xd[7])
    pl.loop(3, 5)(tile_step)
    near_blocks(6)
    seq_forward(c_full, cs)
    arrived(*xd[4], *xd[5])
    links.kept(placed[4], placed[5])
    far_block(6)
    pl.loop(5, tiles)(tile_step)
    pair_on(7, pair)
    links.keep(prod, prod_o)
    links.keep(fa, fa_o)
    links.keep(fb, fb_o)
    arrived(*cs)

    def load_left(b, slot):
        lanes = pl.ds(pl.multiple_of(b * 256, 256), 256)
        return pltpu.make_async_copy(c_full.at[:, :, lanes], lbuf.at[slot], lsem.at[slot])

    def store_grad(b, slot):
        return pltpu.make_async_copy(gbuf.at[slot], down_o.at[b // 4, lax.rem(b, 4)], gsem.at[slot])

    load_left(0, 0).start()

    @pl.loop(0, 8)
    def _(b):
        slot = lax.rem(b, 2)

        @pl.when(b + 1 < 8)
        def _():
            load_left(b + 1, 1 - slot).start()

        load_left(b, slot).wait()

        @pl.when(b >= 2)
        def _():
            store_grad(b - 2, slot).wait()

        gbuf[slot] = (tn(lbuf[slot, 0], prod[0]) + tn(lbuf[slot, 1], prod[1])).astype(BF)
        store_grad(b, slot).start()

    store_grad(6, 0).wait()
    store_grad(7, 1).wait()
    links.finish()


def forward(x, c, g, seg, table, shards):
    micro, rows, d = x.shape
    sd = jax.ShapeDtypeStruct
    toks = (micro, 4 * rows, d)
    nq, nf = shards[1].shape[1], shards[2].shape[1]
    fulls = [sd((2, 4) + w.shape, BF) for w in shards]
    ffn = sd((micro, 4 * rows, nf), BF)
    out_shape = [sd(toks, BF)] + fulls + [
        sd(toks, BF), sd((micro, 4 * rows, 640), BF), sd((micro, 4 * rows, nq), BF),
        sd((micro, rows, d), F32), sd(toks, BF), sd((8, d), F32), ffn, ffn, ffn, sd((2, 4, 256, nf), BF),
    ]
    v = pltpu.VMEM
    scratch = [
        v(toks, BF), v(toks, BF), v((2, 4, 256, 640), BF), v((2, 4, 256, 512), BF), v((2, 512, 640), BF),
        v((2, 512, 512), BF), v((2, 256, d), BF), v((2, 256, d), BF), v((2, 256, d), F32), v((2, 128, d), BF),
        v((2, 128, d), BF), v((2, 128, d), BF), v((4, 8, 256), F32), v((2, 4, 8, 256), F32), v((8, 256), F32),
        v((2, 512, nf), BF), v((2, 512, nf), BF), v((2, 512, nf), BF), v((2, 2, 4, 256, 256), BF), v((2, 2, 512, 256), BF), v((2, 256, nf), BF),
        v((4, 512, 128), F32), v((2, 512, 512), BF), v((8, 512), F32),
        pltpu.SemaphoreType.DMA((96,)), pltpu.SemaphoreType.DMA((96,)), pltpu.SemaphoreType.DMA((56,)),
        pltpu.SemaphoreType.DMA((2, 2)), pltpu.SemaphoreType.DMA((2,)), pltpu.SemaphoreType.DMA((2,)),
    ]
    return pl.pallas_call(
        forward_kernel,
        out_shape=out_shape,
        in_specs=[HBM, HBM, VMEM, VMEM, HBM] + [HBM] * 5,
        out_specs=[HBM] * 9 + [VMEM, HBM, VMEM] + [HBM] * 4,
        scratch_shapes=scratch,
        compiler_params=pltpu.CompilerParams(collective_id=0, has_side_effects=True, vmem_limit_bytes=LIMIT),
    )(x, c, g, seg, table, *shards)


ORDER = (2, 1, 3, 0)


def backward_kernel(
    seg, gain, table_h, x_ref, c_full, wqkv_f, wo_f, wg_f, wu_f, wd_f, na_h, qkv_h, att_h, res_h, nm_h, prod_h, fa_h,
    fb_h, down_h,
    out_o, din_o, gain_o, gq_o, gkv_o, go_o, gg_o, gu_o, gd_o, xin_f, xin_o, xin_q, zin_f, zin_o, zin_q, fin, yin, pin, pxin,
    cot, nm, dr, dg, du, grads, grads_a, stage, ostage, wcol, wrow, far, far_st, ysend, ysend_o, acc_m, acc_o, res, qkv, att, datt, dqkv,
    obuf, dkacc, dvacc, gacc, gxin, gnear, gzin, gown, gsin, table, mask_t, keys,
    send, recv, local, csem, rsem, ssem, osem,
):
    links = Links(send, recv, local)
    put, arrived, sent, keep, kept = links.put, links.arrived, links.sent, links.keep, links.kept
    ff = fa_h.shape[2]
    prod = cot.at[:, :, pl.ds(0, ff)]

    def wide(k):
        return lambda r: grads.at[k, r]

    def cut(start, width):
        return lambda r: grads_a.at[r, :, pl.ds(start, width)]

    ahead = 640
    behind = ff - ahead
    low_lanes, high_lanes = pl.ds(0, ahead), pl.ds(ahead, behind)

    def down_block(r):
        return grads.at[0, r, :, low_lanes]

    spec = {
        "down": (None, None, down_block, xin_f.at[0, :, :, low_lanes], zin_f.at[0, :, :, low_lanes], ahead, gd_o),
        "gate": (nm, dg, wide(1), xin_f.at[1], zin_f.at[1], ff, gg_o),
        "up": (nm, du, wide(2), xin_f.at[2], zin_f.at[2], ff, gu_o),
        "out": (dr, att, cut(0, 512), xin_o, zin_o, 512, go_o),
        "qkv": (cot, dqkv, cut(512, 640), xin_q, zin_q, 640, gq_o),
    }
    relays, pairs = {}, []
    xid = {name: {} for name in spec}
    zid = {name: {} for name in spec}

    def block_of(name, b):
        left, right = spec[name][:2]
        lanes = pl.ds(b * 256, 256)
        return tn(left[0, :, lanes], right[0]) + tn(left[1, :, lanes], right[1])

    def two_away(name, src, zland):
        low = links.describe(src, zland.at[2], links.z[1])
        high = links.describe(src, zland.at[3], links.z[3])
        pl.when(links.low)(links.remote[low].start)
        pl.when(jnp.logical_not(links.low))(links.remote[high].start)
        links.seen.update((low, high))
        links.gone.update((low, high))
        relays[name] = (low, high)

    def pair_start():
        for rx in range(2):
            two_away(("pair", rx), down_h.at[rx, 2, :, high_lanes], pin.at[rx])

    def pair_on():
        for rx in range(2):
            for k, r in enumerate((1, 3)):
                got, mine = stage.at[0, :, pl.ds(0, behind)], grads.at[0, rx * 2 + k, :, high_lanes]
                load = pltpu.make_async_copy(down_h.at[rx, r, :, high_lanes], mine, ssem.at[1])
                copy = pltpu.make_async_copy(pin.at[rx, 2 + k], got, ssem.at[0])
                load.start()
                load.wait()

                @pl.when(links.middle)
                def _():
                    links.remote[relays["pair", rx][k]].wait_recv()
                    copy.start()
                    copy.wait()
                    mine[...] = (mine[...].astype(F32) + got[...].astype(F32)).astype(BF)

                pairs.append(put(mine, pin.at[rx, k], links.z[r]))

    def pair_sum():
        for rx in (1, 0):
            arrived(*pairs[2 * rx : 2 * rx + 2])
            sent(*pairs[2 * rx : 2 * rx + 2])
            copies = [
                pltpu.make_async_copy(src, stage.at[k, :, pl.ds(0, behind)], ssem.at[k])
                for k, src in enumerate((down_h.at[rx, 0, :, high_lanes], pin.at[rx, 0], pin.at[rx, 1]))
            ]
            for c in copies:
                c.start()
            for c in copies:
                c.wait()
            total = stage[0, :, 0:behind].astype(F32) + stage[1, :, 0:behind].astype(F32)
            mine = grads.at[0, rx * 2, :, high_lanes]
            mine[...] = (total + stage[2, :, 0:behind].astype(F32)).astype(BF)
            if rx:
                pairs.append(put(mine, pxin, links.x))

    def grad_far(name):
        buffer, landing = spec[name][2:4]
        for r in ORDER:
            if name == "down":
                xid[name][r] = put(down_h.at[1, r, :, low_lanes], landing.at[r], links.x)
            else:
                buffer(r)[...] = block_of(name, 4 + r).astype(BF)
                xid[name][r] = put(buffer(r), landing.at[r], links.x)

    def grad_near(name, r):
        buffer, landing, zland, width = spec[name][2:6]
        arrived(xid[name][r])
        got = stage.at[0, :, pl.ds(0, width)]
        copies = [pltpu.make_async_copy(landing.at[r], got, ssem.at[0])]
        if name == "down":
            copies.append(pltpu.make_async_copy(down_h.at[0, r, :, low_lanes], stage.at[1, :, low_lanes], ssem.at[1]))
        for c in copies:
            c.start()
        if name != "down":
            mine = block_of(name, r)
            sent(xid[name][r])
        for c in copies:
            c.wait()
        if name == "down":
            mine = stage[1, :, low_lanes].astype(F32)
        buffer(r)[...] = (mine + got[...].astype(F32)).astype(BF)
        if r == 2:
            two_away(name, buffer(2), zland)

    def grad_on(name):
        buffer, _, zland, width = spec[name][2:6]
        got = stage.at[0, :, pl.ds(0, width)]
        for k, r in enumerate((1, 3)):
            copy = pltpu.make_async_copy(zland.at[2 + k], got, ssem.at[0])

            @pl.when(links.middle)
            def _():
                links.remote[relays[name][k]].wait_recv()
                copy.start()
                copy.wait()
                buffer(r)[...] = (buffer(r)[...].astype(F32) + got[...].astype(F32)).astype(BF)

            zid[name][r] = put(buffer(r), zland.at[k], links.z[r])

    def far_sent(name):
        low, high = relays[name]
        pl.when(links.low)(links.remote[low].wait_send)
        pl.when(jnp.logical_not(links.low))(links.remote[high].wait_send)

    writing = []

    def grad_final(name):
        buffer, _, zland, width, result = spec[name][2:]
        copies = []
        for k, r in enumerate((1, 3)):
            arrived(zid[name][r])
            copies.append(pltpu.make_async_copy(zland.at[k], stage.at[k, :, pl.ds(0, width)], ssem.at[k]))
            copies[-1].start()
        if name == "down":
            arrived(pairs[4])
            copies.append(pltpu.make_async_copy(pxin, stage.at[2, :, pl.ds(0, behind)], ssem.at[2]))
            copies[-1].start()
        for c in copies + writing:
            c.wait()
        lanes = slice(0, width)
        total = buffer(0)[...].astype(F32) + stage[0, :, lanes].astype(F32)
        ostage[:, lanes] = total + stage[1, :, lanes].astype(F32)
        if name == "down":
            width = ff
            ostage[:, high_lanes] = grads[0, 0, :, high_lanes].astype(F32) + stage[2, :, 0:behind].astype(F32)
        if name == "qkv":
            width = gq_o.shape[1]
            writing[:] = [pltpu.make_async_copy(ostage.at[:, pl.ds(width, gkv_o.shape[1])], gkv_o, osem.at[1])]
        else:
            writing[:] = []
        writing.append(pltpu.make_async_copy(ostage.at[:, pl.ds(0, width)], result, osem.at[0]))
        for c in writing:
            c.start()

    def sweep(terms, row, use):
        def load(b, slot):
            return [
                pltpu.make_async_copy(
                    w.at[b // 4, lax.rem(b, 4)], wrow.at[slot, k, :, pl.ds(0, width)], rsem.at[slot, k]
                )
                for k, (_, w, width) in enumerate(terms)
            ]

        for c in load(0, 0):
            c.start()

        @pl.loop(0, 8)
        def _(b):
            slot = lax.rem(b, 2)

            @pl.when(b + 1 < 8)
            def _():
                for c in load(b + 1, 1 - slot):
                    c.start()

            for c in load(b, slot):
                c.wait()
            lanes = pl.ds(pl.multiple_of(b * 256, 256), 256)
            for m in range(2):
                total = None
                for k, (left, _, width) in enumerate(terms):
                    t = nt(left[m, row : row + HALF, 0:width], wrow[slot, k, :, 0:width])
                    total = t if total is None else total + t
                use(m, lanes, total)

    fid, yid = {}, {}

    def rows_far(i, terms):
        sent(*fid.values())

        def use(m, lanes, total):
            far[m, :, lanes] = total.astype(BF)

        sweep(terms, HALF, use)
        fid[i] = put(far, fin.at[i], links.core)

    def rows_near(i, terms, acc, leaving):
        arrived(fid[i])
        kept(keep(fin.at[i], far_st))

        def use(m, lanes, total):
            total = total + far_st[m, :, lanes].astype(F32)
            acc[m, :, lanes] = total[:ROWS]
            leaving[m, :, lanes] = total[ROWS:].astype(BF)

        sweep(terms, 0, use)

    def rows_on(i, leaving):
        yid[i] = [put(leaving.at[m], yin.at[i, m], links.y) for m in range(2)]

    def rows_final(i, m):
        arrived(yid[i][m])
        kept(keep(yin.at[i, m], far_st.at[m, pl.ds(0, ROWS)]))

    def chunks(body, m):
        @pl.loop(0, 2)
        def _(i):
            body(m, pl.ds(pl.multiple_of(i * 64, 64), 64))

    def norm_back(v, e, row):
        inverse = lax.rsqrt(jnp.mean(v * v, axis=-1, keepdims=True) + EPS)
        u = v * inverse
        gacc[row : row + 1, :] += jnp.sum(e * u, axis=0, keepdims=True)
        w = e * gain[row : row + 1, :]
        return inverse * (w - u * jnp.mean(w * u, axis=-1, keepdims=True))

    grad_far("down")
    pair_start()
    cot_in = keep(c_full, cot)
    ffn_in = [keep(fa_h, dg), keep(fb_h, du)]
    own_in = keep(c_full.at[:, pl.ds(0, ROWS)], obuf)
    late = [keep(nm_h, nm), keep(res_h, res), keep(qkv_h, qkv), keep(att_h, att)]
    late += load_table(links, table_h, table)
    gacc[...] = jnp.zeros_like(gacc)

    def load_col(t, slot):
        lanes = pl.ds(pl.multiple_of(t * 256, 256), 256)
        return pltpu.make_async_copy(wd_f.at[:, :, :, lanes], wcol.at[slot], csem.at[slot])

    load_col(0, 0).start()
    kept(cot_in, *ffn_in)
    tiles = ff // 256
    rest = ff - tiles * 256

    def product_rows(slot, width, start):
        @pl.loop(0, 2)
        def _(m):
            lanes = pl.ds(start, width)
            d = nn(cot[m], wcol[slot, :, :, :, 0:width].reshape(DM, width))
            dg[m, :, lanes] = (d * dg[m, :, lanes].astype(F32)).astype(BF)
            du[m, :, lanes] = (d * du[m, :, lanes].astype(F32)).astype(BF)

    last = pltpu.make_async_copy(
        wd_f.at[:, :, :, pl.ds(tiles * 256, rest)], wcol.at[tiles % 2, :, :, :, pl.ds(0, rest)], csem.at[tiles % 2]
    )

    @pl.loop(0, tiles)
    def _(t):
        slot = lax.rem(t, 2)

        @pl.when(t + 1 < tiles)
        def _():
            load_col(t + 1, 1 - slot).start()

        load_col(t, slot).wait()
        product_rows(slot, 256, pl.multiple_of(t * 256, 256))

    last.start()
    last.wait()
    product_rows(tiles % 2, rest, tiles * 256)

    prod_in = keep(prod_h, prod)
    kept(*late)
    ffn_terms = [(dg, wg_f, ff), (du, wu_f, ff)]
    rows_far(1, ffn_terms)
    grad_far("gate")
    rows_near(1, ffn_terms, acc_m, ysend)
    rows_on(1, ysend)
    grad_near("down", 2)
    grad_near("down", 1)
    grad_far("up")
    pair_on()
    grad_near("down", 3)
    grad_near("down", 0)
    grad_on("down")
    kept(prod_in)
    out_terms = [(prod, wd_f, ff)]
    rows_far(0, out_terms)
    make_mask(links, seg, keys, mask_t, True)
    kept(own_in)

    def output_rows(m, rows):
        total = res[m, rows, :] + acc_o[m, rows, :] + far_st[m, rows, :].astype(F32)
        obuf[m, rows, :] = total.astype(BF)

    def middle(m, rows):
        e = acc_m[m, rows, :] + far_st[m, rows, :].astype(F32)
        d = norm_back(res[m, rows, :], e, 1) + obuf[m, rows, :].astype(F32)
        acc_m[m, rows, :] = d
        dr[m, rows, :] = d.astype(BF)

    ds = []
    for m in range(2):
        rows_final(1, m)
        chunks(middle, m)
        own = dr.at[m, pl.ds(0, ROWS)]
        ds.append(
            [put(own, dr.at[m, pl.ds(ROWS, ROWS)], links.y), put(own, dr.at[m, pl.ds(2 * ROWS, ROWS)], links.core)]
        )
    wo_in = [keep(wo_f.at[:, :, :, pl.ds(k * 256, 256)], wcol.at[k]) for k in range(2)]
    rows_near(0, out_terms, acc_o, ysend_o)
    rows_on(0, ysend_o)
    na_in = keep(na_h, cot)
    grad_near("gate", 2)

    def dr_arrives(m):
        arrived(ds[m][0])
        ds[m].append(put(dr.at[m, pl.ds(ROWS, ROWS)], dr.at[m, pl.ds(3 * ROWS, ROWS)], links.core))
        arrived(*ds[m])

    def attended_back(m):
        for k in range(2):
            datt[m, :, k * 256 : (k + 1) * 256] = nn(dr[m], wcol[k].reshape(DM, 256)).astype(BF)

    def attend_back(m):
        kv = qkv[m, :, 512:640].astype(F32)
        lane = lax.broadcasted_iota(jnp.int32, (LEN4, 128), 1)
        half = lax.broadcasted_iota(jnp.int32, (256, 128), 1) < 64
        ka = jnp.where(lane < 64, kv, 0.0)
        vb = jnp.where(lane < 64, 0.0, kv)
        kb, va = pltpu.roll(ka, 64, 1), pltpu.roll(vb, 64, 1)
        heads = [
            ((k * 0.125).astype(BF), (k * 0.125).T.astype(BF), v.astype(BF), keep_lanes)
            for k, v, keep_lanes in ((ka, va, half), (kb, vb, jnp.logical_not(half)))
        ]
        dkacc[...] = jnp.zeros_like(dkacc)
        dvacc[...] = jnp.zeros_like(dvacc)

        @pl.loop(0, 8)
        def _(i):
            lanes = pl.ds(pl.multiple_of(i // 2 * 128, 128), 128)
            rows = pl.ds(pl.multiple_of(lax.rem(i, 2) * 256, 256), 256)
            q, do = qkv[m, rows, lanes], datt[m, rows, lanes]
            bias = mask_t[m, :, rows].astype(F32)
            dq_t = jnp.zeros((128, 256), F32)
            for k, k_t, v, keep_lanes in heads:
                s = nt(k, q) + bias
                e = jnp.exp(s - jnp.max(s, axis=0, keepdims=True))
                p = e * (1.0 / jnp.sum(e, axis=0, keepdims=True))
                d = nt(v, do)
                ds_ = (p * (d - jnp.sum(p * d, axis=0, keepdims=True))).astype(BF)
                dq_t = dq_t + nn(k_t, ds_)
                zero = jnp.zeros_like(q)
                dkacc[...] += nn(ds_, jnp.where(keep_lanes, q, zero))
                dvacc[...] += nn(p.astype(BF), jnp.where(keep_lanes, do, zero))
            dqkv[m, rows, lanes] = rope_tile(dq_t.T, table[0, rows, :], -table[1, rows, :]).astype(BF)

        dk = dkacc[...] + pltpu.roll(dkacc[...], 64, 1)
        dv = dvacc[...] + pltpu.roll(dvacc[...], 64, 1)
        dk = rope_tile(dk * 0.125, table[0], -table[1])
        dqkv[m, :, 512:640] = jnp.where(lane < 64, dk, dv).astype(BF)

    kept(*wo_in)
    dr_arrives(0)
    attended_back(0)
    attend_back(0)
    pair_sum()
    dr_arrives(1)
    attended_back(1)
    grad_near("gate", 1)
    attend_back(1)
    na_terms = [(dqkv, wqkv_f, 640)]
    kept(na_in)
    grad_far("qkv")
    rows_far(2, na_terms)
    grad_far("out")
    grad_near("gate", 3)
    grad_near("gate", 0)
    grad_on("gate")
    for m in range(2):
        rows_final(0, m)
        chunks(output_rows, m)
    for b in range(8):
        keep(obuf.at[:, :, pl.ds(b * 256, 256)], out_o.at[:, :, links.lanes(b)])
    sent(*yid[1])
    rows_near(2, na_terms, acc_o, ysend)
    rows_on(2, ysend)
    grad_near("up", 2)
    grad_near("up", 1)
    grad_near("up", 3)
    own_x = far_st.at[:, pl.ds(ROWS, ROWS)]
    kept(*[keep(x_ref.at[:, :, links.lanes(b)], own_x.at[:, :, pl.ds(b * 256, 256)]) for b in range(8)])

    def last_rows(m, rows):
        e = acc_o[m, rows, :] + far_st[m, rows, :].astype(F32)
        v = own_x[m, rows, :].astype(F32)
        acc_m[m, rows, :] += norm_back(v, e, 0)

    for m in range(2):
        rows_final(2, m)
        chunks(last_rows, m)
    for b in range(8):
        keep(acc_m.at[:, :, pl.ds(b * 256, 256)], din_o.at[:, :, links.lanes(b)])
    gx = put(gacc.at[:, pl.ds(1024, 1024)], gxin, links.x)
    grad_near("up", 0)
    grad_on("up")
    grad_final("down")
    grad_final("gate")
    for name in ("out", "qkv"):
        for r in ORDER:
            grad_near(name, r)
        if name == "out":
            grad_on(name)
    arrived(gx)
    gnear[...] = gacc[:, 0:1024] + gxin[...]
    gz = [put(gnear.at[:, pl.ds(r * 256, 256)], gzin.at[r - 1], links.z[r]) for r in (1, 2, 3)]
    grad_on("qkv")
    grad_final("up")
    arrived(*gz)
    gown[...] = gnear[:, 0:256] + gzin[0] + gzin[1] + gzin[2]
    gs = [put(gown, gsin.at[k], p) for k, p in enumerate((links.core, links.y, links.both))]
    grad_final("out")
    arrived(*gs)
    gain_o[...] = gown[...] + gsin[0] + gsin[1] + gsin[2]
    grad_final("qkv")
    for c in writing:
        c.wait()
    for name in relays:
        far_sent(name)
    links.finish()


def backward(seg, gain, table, x, arrays):
    micro, rows, d = x.shape
    sd = jax.ShapeDtypeStruct
    ff = arrays[-4].shape[2]
    v = pltpu.VMEM
    behind = ff - 640
    out_shape = [
        sd(x.shape, BF), sd(x.shape, F32), sd((8, 256), F32), sd((256, 512), F32), sd((256, 128), F32), sd((256, 512), F32),
        sd((256, ff), F32), sd((256, ff), F32), sd((256, ff), F32), sd((3, 4, 256, ff), BF), sd((4, 256, 512), BF),
        sd((4, 256, 640), BF), sd((3, 4, 256, ff), BF), sd((4, 256, 512), BF), sd((4, 256, 640), BF),
        sd((3, 2, 256, d), BF), sd((3, 2, 128, d), BF), sd((2, 4, 256, behind), BF), sd((256, behind), BF),
    ]
    toks = (2, 512, d)
    scratch = [
        v(toks, BF), v(toks, BF), v(toks, BF), v((2, 512, ff), BF), v((2, 512, ff), BF), v((3, 4, 256, ff), BF),
        v((4, 256, 1152), BF), v((3, 256, ff), BF), v((256, ff), F32), v((2, 2, 4, 256, 256), BF), v((2, 2, 256, ff), BF),
        v((2, 256, d), BF), v((2, 256, d), BF), v((2, 128, d), BF), v((2, 128, d), BF), v((2, 128, d), F32), v((2, 128, d), F32),
        v((2, 128, d), F32), v((2, 512, 640), BF), v((2, 512, 512), BF), v((2, 512, 512), BF), v((2, 512, 640), BF),
        v((2, 128, d), BF), v((512, 128), F32), v((512, 128), F32), v((8, d), F32), v((8, 1024), F32),
        v((8, 1024), F32), v((3, 8, 256), F32), v((8, 256), F32), v((3, 8, 256), F32),
        v((4, 512, 128), F32), v((2, 512, 512), BF), v((8, 512), F32),
        pltpu.SemaphoreType.DMA((80,)), pltpu.SemaphoreType.DMA((80,)), pltpu.SemaphoreType.DMA((64,)),
        pltpu.SemaphoreType.DMA((2,)), pltpu.SemaphoreType.DMA((2, 2)), pltpu.SemaphoreType.DMA((3,)),
        pltpu.SemaphoreType.DMA((2,)),
    ]
    return pl.pallas_call(
        backward_kernel,
        out_shape=out_shape,
        in_specs=[VMEM] * 2 + [HBM] * (2 + len(arrays)),
        out_specs=[HBM] * 2 + [VMEM] + [HBM] * 16,
        scratch_shapes=scratch,
        compiler_params=pltpu.CompilerParams(collective_id=1, has_side_effects=True, vmem_limit_bytes=LIMIT_B),
    )(seg, gain, table, x, *arrays)


def rope_table():
    frequency = THETA ** (-(np.arange(HD // 2) * (2.0 / HD)))
    angles = np.arange(LEN4)[:, None] * frequency[None, :]
    cosine, sine = np.cos(angles), np.sin(angles)
    c4 = np.tile(cosine, (1, 4))
    s4 = np.concatenate([-sine, sine, -sine, sine], axis=1)
    one, zero = np.ones((LEN4, HD)), np.zeros((LEN4, HD))
    ck, sk = np.concatenate([c4[:, :HD], one], axis=1), np.concatenate([s4[:, :HD], zero], axis=1)
    return np.stack([c4, s4, ck, sk]).astype(np.float32)


def per_device_grid(
    inputs, segments, cotangent, attn_gain, w_query, w_key, w_value, w_out, mlp_gain, w_gate, w_up, w_down,
):
    nq, nk = w_query.shape[1], w_key.shape[1]
    w_qkv = jnp.concatenate([w_query, w_key, w_value], axis=1)
    me = lax.axis_index("seq")
    size = attn_gain.shape[0]
    row = lax.broadcasted_iota(jnp.int32, (8, 4 * size), 0)
    lane = lax.broadcasted_iota(jnp.int32, (8, 4 * size), 1)
    g = jnp.where(row == 0, jnp.tile(attn_gain, 4)[None].astype(F32), jnp.tile(mlp_gain, 4)[None].astype(F32))
    g = jnp.where(jnp.logical_and(row < 2, lane // size == me), g, 0.0)
    table = jnp.asarray(rope_table())
    made = forward(inputs, cotangent, g, segments, table, [w_qkv, w_out, w_gate, w_up, w_down])
    c_full, wqkv, wo, wg, wu, wd, na, qkv, att, res, nm, gain, prod, fa, fb, down = made
    arrays = [c_full, wqkv, wo, wg, wu, wd, na, qkv, att, res, nm, prod, fa, fb, down]
    back = backward(segments, gain, table, inputs, arrays)
    output, d_input, gains, gq, gkv, go, gg, gu, gd = back[:9]
    gains = lax.dynamic_slice_in_dim(gains, me * size, size, 1)
    return (
        output, d_input, gains[0], gq, gkv[:, :nk], gkv[:, nk:], go, gains[1], gg, gu, gd,
    )


class AnyMesh:
    def gather(self, x, c, shards):
        fulls = [lax.all_gather(w, "dp", axis=0, tiled=True) for w in shards]
        return gather_rows(x), gather_rows(c), fulls

    def gather_gains(self, g):
        return lax.all_gather(g, ("dp", "seq"), axis=1, tiled=True)

    def scatter_gain(self, g):
        return lax.psum_scatter(g, ("dp", "seq"), scatter_dimension=0, tiled=True)

    def scatter(self, left, right):
        return lax.psum_scatter(
            outer_sum(left, right).astype(BF), "dp", scatter_dimension=0, tiled=True
        ).astype(F32)

    def to_relative(self, a):
        return a

    def from_relative(self, a):
        return a


def shift_core(a):
    return lax.ppermute(a, "seq", [(i, i ^ 1) for i in range(4)])


def shift_y(a):
    return lax.ppermute(a, "seq", [(i, i ^ 2) for i in range(4)])


def gather_rows(a):
    across = shift_y(a)
    return jnp.concatenate([a, across, shift_core(a), shift_core(across)], axis=-2)


def scatter_rows(make):
    got = shift_core(make(1).astype(BF))
    near = make(0) + got.astype(F32)
    rows = near.shape[1] // 2
    got = shift_y(near[:, rows:].astype(BF))
    return near[:, :rows] + got.astype(F32)


def per_device(
    inputs, segments, cotangent, attn_gain, w_query, w_key, w_value, w_out, mlp_gain, w_gate, w_up, w_down,
):
    micro, rows, d = inputs.shape
    seq = lax.axis_size("seq")
    length = rows * seq
    full = micro * length
    half = length // 2
    grid = AnyMesh()

    nq, nk = w_query.shape[1], w_key.shape[1]
    heads, kv_heads = nq // HD, nk // HD
    groups = heads // kv_heads
    w_qkv = jnp.concatenate([w_query, w_key, w_value], axis=1)

    inputs = grid.to_relative(inputs)
    cotangent = grid.to_relative(cotangent)
    gains = grid.gather_gains(jnp.stack([attn_gain, mlp_gain]).astype(F32))
    gain_a, gain_m = gains[0], gains[1]

    shards = [w_qkv, w_out, w_gate, w_up, w_down]
    x_full, up_full, (wqkv, wo, wg, wu, wd) = grid.gather(inputs, cotangent, shards)

    me = lax.axis_index("seq")
    order = [me, me ^ 2, me ^ 1, me ^ 3]
    pos = jnp.concatenate([j * rows + jnp.arange(rows, dtype=jnp.int32) for j in order])
    segs = jnp.concatenate([lax.dynamic_slice_in_dim(segments, j * rows, rows, 1) for j in order], axis=1)
    cosine, sine = rope_tables(pos)
    cos_f, sin_f = jnp.tile(cosine, (micro, 1)), jnp.tile(sine, (micro, 1))
    allowed = (pos[None, :] <= pos[:, None])[None] & (segs[:, :, None] == segs[:, None, :])
    allowed = allowed[:, None, None]

    def pieces(make):
        return lambda i: make(slice(i * half, (i + 1) * half)).reshape(micro, half, d)

    def rows_of(a, s):
        return a.reshape(micro, length, -1)[:, s].reshape(micro * half, -1)

    hidden_full = x_full.reshape(full, d).astype(F32)
    normed, inverse_f = normalize(hidden_full, gain_a)
    na = normed.astype(BF)
    hidden = inputs.astype(F32)
    upstream = cotangent.astype(F32)
    up_full = up_full.reshape(full, d)

    def rope(x, n, s):
        return rotate(x.reshape(full, n, HD), cos_f, s).astype(BF).reshape(full, n * HD)

    qkv = project(na, wqkv)
    q = rope(qkv[:, :nq], heads, sin_f)
    k = rope(qkv[:, nq : nq + nk], kv_heads, sin_f)
    v = qkv[:, nq + nk :].astype(BF)
    qg = q.reshape(micro, length, kv_heads, groups, HD)
    kg = k.reshape(micro, length, kv_heads, HD)
    vg = v.reshape(micro, length, kv_heads, HD)
    scores = jnp.einsum("mqkgd,mpkd->mkgqp", qg, kg, preferred_element_type=F32) * HD ** (-0.5)
    scores = jnp.where(allowed, scores, NEGATIVE)
    maximum = jnp.max(scores, axis=-1, keepdims=True)
    weights = jnp.where(allowed, jnp.exp(scores - maximum), 0.0)
    denominator = jnp.sum(weights, axis=-1, keepdims=True)
    prob = weights / denominator
    prob_b = prob.astype(BF)
    attended = jnp.einsum("mkgqp,mpkd->mqkgd", prob_b, vg, preferred_element_type=F32)
    attended = attended.astype(BF).reshape(full, heads * HD)
    residual = hidden + scatter_rows(pieces(lambda s: project_back(rows_of(attended, s), wo)))
    normed, inverse_m = normalize(residual, gain_m)
    nm = gather_rows(normed.astype(BF)).reshape(full, d)
    gate_pre = project(nm, wg)
    up_proj = project(nm, wu)
    sigmoid_g = jax.nn.sigmoid(gate_pre)
    active = gate_pre * sigmoid_g
    product = (active * up_proj).astype(BF)
    g_down = grid.scatter(up_full, product)
    d_product = project(up_full, wd)
    d_gate = (d_product * up_proj * sigmoid_g * (1.0 + gate_pre * (1.0 - sigmoid_g))).astype(BF)
    d_up = (d_product * active).astype(BF)
    d_nm = scatter_rows(
        pieces(lambda s: project_back(rows_of(d_gate, s), wg) + project_back(rows_of(d_up, s), wu))
    )
    g_gate = grid.scatter(nm, d_gate)
    g_up = grid.scatter(nm, d_up)
    output = (residual + scatter_rows(pieces(lambda s: project_back(rows_of(product, s), wd)))).astype(BF)
    flat = lambda a: a.reshape(micro * rows, -1)
    d_norm_m, g_gain_m = normalize_back(flat(residual), flat(inverse_m), gain_m, flat(d_nm))
    d_residual = upstream + d_norm_m.reshape(micro, rows, d)
    dr = gather_rows(d_residual.astype(BF)).reshape(full, d)
    d_att = project(dr, wo).astype(BF)
    dg = d_att.reshape(micro, length, kv_heads, groups, HD)
    d_values = jnp.einsum("mkgqp,mqkgd->mpkd", prob_b, dg, preferred_element_type=F32)
    d_prob = jnp.einsum("mqkgd,mpkd->mkgqp", dg, vg, preferred_element_type=F32)
    row_sum = jnp.sum(prob * d_prob, axis=-1, keepdims=True)
    d_scores = (prob * (d_prob - row_sum) * HD ** (-0.5)).astype(BF)
    d_query = jnp.einsum("mkgqp,mpkd->mqkgd", d_scores, kg, preferred_element_type=F32)
    d_keys = jnp.einsum("mkgqp,mqkgd->mpkd", d_scores, qg, preferred_element_type=F32)
    dq = rope(d_query, heads, -sin_f)
    dk = rope(d_keys, kv_heads, -sin_f)
    dv = d_values.astype(BF).reshape(full, kv_heads * HD)
    dqkv = jnp.concatenate([dq, dk, dv], axis=1)
    g_out = grid.scatter(dr, attended)
    d_na = scatter_rows(pieces(lambda s: project_back(rows_of(dqkv, s), wqkv)))
    g_qkv = grid.scatter(na, dqkv)
    inverse_a = inverse_f.reshape(micro, length, 1)[:, :rows]
    d_norm_a, g_gain_a = normalize_back(flat(hidden), flat(inverse_a), gain_a, flat(d_na))
    d_input = d_residual + d_norm_a.reshape(micro, rows, d)
    return (
        grid.from_relative(output),
        grid.from_relative(d_input),
        grid.scatter_gain(g_gain_a),
        g_qkv[:, :nq],
        g_qkv[:, nq : nq + nk],
        g_qkv[:, nq + nk :],
        g_out,
        grid.scatter_gain(g_gain_m),
        g_gate,
        g_up,
        g_down,
    )


def solution(mesh):
    tok, wt, gn = P(None, ("dp", "seq"), None), P("dp", "seq"), P(("dp", "seq"))
    grid = mesh.shape["dp"] == 8 and mesh.shape["seq"] == 4
    return jax.shard_map(
        per_device_grid if grid else per_device,
        mesh=mesh,
        in_specs=(tok, P(None, "dp"), tok, gn, wt, wt, wt, wt, gn, wt, wt, wt),
        out_specs=(tok, tok, gn, wt, wt, wt, wt, gn, wt, wt, wt),
        check_vma=False,
    )
```
